32 devices in a mesh: chan: 4 (over x, core), tm: 8 (over z, y).
Axes of the slice: x: 2, y: 2, z: 4, core: 2. Of those that a mesh axis runs over, the one named last changes fastest.
Arguments:
- record: float32 [2048, 65536], P('chan', 'tm'), may hold values from -6 to 6
- whitening: float32 [65], replicated, may hold values from -0.75 to 0.75
- offsets: int32 [128], P('tm'), may hold values from 0 to 256, as said below
- window_valid: int32 [128], P('tm'), may hold values 0 or 1
Outputs:
- cross_spectra: bfloat16 [64, 2, 2048, 2048], P('tm', None, 'chan')
The draws below stay inside these ranges and needn't reach their ends.
Inputs may be any that keep to these rules, and one draw needn't show every extreme that they name: `offsets`: some window has offset exactly 256.
All inputs are finite; a program needn't handle non-finite values. No bound on the sum of `window_valid` on one device may be relied on, other than what follows from the above.
Results may differ from the reference program's by a relative error of at most 0.006.
Values may be sent and summed in bfloat16 or wider, within the bound.
No kernel may reach another device: no remote copies, remote signals or barrier semaphores. Data moves between devices by JAX's collectives and lax.ppermute only.
A program may use at most 192 MiB of HBM per device.

```python
import math
import jax
import jax.numpy as jnp
from jax import lax

C = 2048
L = 2048
HOP = 512
JITTER = 256
TAPS = 65
BINS = 64
K0 = 64
WINDOWS = 128
SAMPLES = 65536


def draw_offsets(key, part):
    key_one, key_two = jax.random.split(jax.random.fold_in(key, 17))
    drawn = jax.random.randint(key_one, (WINDOWS,), 0, JITTER + 1, dtype=jnp.int32)
    chosen = jax.random.randint(key_two, (), 0, WINDOWS, dtype=jnp.int32)
    return drawn.at[chosen].set(JITTER)


def with_ends(result, key, low, high):
    dims = result.shape
    place = [jax.random.randint(jax.random.fold_in(key, axis), (), 0, dims[axis]) for axis in range(len(dims))]
    result = result.at[tuple(place)].set(low)
    longest = dims.index(max(dims))
    place[longest] = (place[longest] + 1) % dims[longest]
    return result.at[tuple(place)].set(high)


def block_levels(own_key, extent, pieces, low, largest):
    level, own = 1.0, jax.random.fold_in(own_key, 6)
    for dim, blocks in pieces:
        draws = jnp.exp(jax.random.uniform(jax.random.fold_in(own, dim), (blocks,), jnp.float32, low / len(pieces), largest / len(pieces)))
        level = level * jnp.repeat(draws, extent[dim] // blocks).reshape([-1 if axis == dim else 1 for axis in range(len(extent))])
    return level


def noise(rng, shape, deviation, limit, cuts=(), kind=jnp.bfloat16):
    result = deviation * jax.random.normal(rng, shape, jnp.float32)
    if cuts:
        result = result * block_levels(rng, shape, cuts, -0.22, 0.18)
    return jnp.clip(result, -limit, limit).astype(kind)


def setup_inputs(seed: int = 0) -> dict:
    seeds = jax.random.split(jax.random.key(seed), 5)
    record = noise(seeds[0], (C, SAMPLES), 1.0, 6.0, ((0, 4), (1, 8)), jnp.float32)
    whitening = noise(seeds[1], (TAPS,), TAPS ** -0.5, 0.75, (), jnp.float32)
    offsets = draw_offsets(jax.random.fold_in(seeds[4], 71), 0)
    window_valid = with_ends((jax.random.randint(seeds[3], (WINDOWS,), 0, 4) < 3).astype(jnp.int32), jax.random.fold_in(seeds[3], 1), 0, 1)
    return dict(record=record, whitening=whitening, offsets=offsets, window_valid=window_valid)


def dft_table_build():
    sample = jnp.arange(L, dtype=jnp.float32)
    bin_ids = (K0 + jnp.arange(BINS)).astype(jnp.float32)
    angles = 2.0 * jnp.pi * jnp.mod(sample[:, None] * bin_ids[None, :], L) / L
    weighting = 1.0 / math.sqrt(L)
    return jnp.concatenate([jnp.cos(angles) * weighting, -jnp.sin(angles) * weighting], axis=1)

def joined_matrix(whitening):
    dft_table = dft_table_build()
    padded = jnp.pad(dft_table, ((TAPS - 1, TAPS - 1), (0, 0)))

    def add_tap(m, summed):
        return summed + whitening[m] * lax.dynamic_slice_in_dim(padded, m, L + TAPS - 1, 0)
    return lax.fori_loop(0, TAPS, add_tap, jnp.zeros((L + TAPS - 1, 2 * BINS), jnp.float32))

def reference(record, whitening, offsets, window_valid):
    matrix = joined_matrix(whitening)
    extended = jnp.pad(record, ((0, 0), (TAPS - 1, L - HOP + JITTER)))

    def one_window(w):
        begin_at = (w * HOP + offsets[w]).astype(jnp.int32)
        segments = lax.dynamic_slice_in_dim(extended, begin_at, L + TAPS - 1, 1)
        spectra = jnp.dot(segments, matrix, precision=lax.Precision.HIGHEST, preferred_element_type=jnp.float32)
        return (spectra * window_valid[w].astype(jnp.float32)).astype(jnp.bfloat16)
    spectra = lax.map(one_window, jnp.arange(WINDOWS, dtype=jnp.int32))
    by_bin = jnp.transpose(spectra, (2, 1, 0))

    def one_bin(f):
        real_rows = by_bin[f].astype(jnp.float32)
        imag_rows = by_bin[f + BINS].astype(jnp.float32)
        own_rows = jnp.concatenate([real_rows, imag_rows], axis=1)
        turned = jnp.concatenate([-imag_rows, real_rows], axis=1)
        real_part = jnp.dot(own_rows, own_rows.T, precision=lax.Precision.HIGHEST, preferred_element_type=jnp.float32)
        imag_part = jnp.dot(own_rows, turned.T, precision=lax.Precision.HIGHEST, preferred_element_type=jnp.float32)
        return (jnp.stack([real_part, imag_part], axis=0) / WINDOWS).astype(jnp.bfloat16)
    return lax.map(one_bin, jnp.arange(BINS, dtype=jnp.int32))
```

```python
import functools
import math

import jax
import jax.numpy as jnp
import numpy as np
from jax import lax
from jax.experimental import pallas as pl
from jax.experimental.pallas import tpu as pltpu
from jax.sharding import PartitionSpec as P

L = 2048
HOP = 512
JITTER = 256
TAPS = 65
BINS = 64
K0 = 64
RIM = 128
GROUP = L // HOP
EDGE = RIM + JITTER
LANES = 2 * BINS
PAIR = 2
MIB = 1 << 20
F32 = jnp.float32
BF16 = jnp.bfloat16


def from_behind(shard, axis, by):
    devices = lax.axis_size(axis)
    pairs = [(i, i + by) for i in range(devices) if 0 <= i + by < devices]
    return lax.ppermute(shard, axis, pairs)


def phase_table():
    sample = np.arange(L) - (TAPS - 1)
    angles = 2.0 * np.pi * np.mod(sample[:, None] * (K0 + np.arange(BINS))[None, :], L) / L
    return (np.concatenate([np.cos(angles), -np.sin(angles)], axis=1) / math.sqrt(L)).astype(np.float32)


def matmul(a, b):
    return jnp.dot(a, b, preferred_element_type=F32)


def turn(values, place):
    lane = lax.broadcasted_iota(jnp.int32, (8, LANES), 1)
    bins = K0 + (lane & (BINS - 1))
    angles = ((bins * (place + L)) & (L - 1)).astype(F32) * (2.0 * math.pi / L)
    sine = jnp.sin(angles)
    sine = jnp.where(lane < BINS, -sine, sine)
    return values * jnp.cos(angles)[:1] + pltpu.roll(values, BINS, 1) * sine[:1]


def edge_table(rise, fall, offset):
    start = JITTER - offset
    return jnp.concatenate([rise[pl.ds(start, RIM), :], fall[pl.ds(start, JITTER), :]], axis=0).astype(BF16)


def across(values):
    channels = values.shape[0]
    if channels % 128:
        values = jnp.pad(values, ((0, 128 - channels), (0, 0)))
    return values.T


def border_kernel(meta, taps, table, record, parts, blocks, rise, fall, padded, collected):
    channels = record.shape[0]
    padded[0 : TAPS - 1, :] = jnp.zeros((TAPS - 1, LANES), F32)
    padded[TAPS - 1 :, :] = table[TAPS - 1 : TAPS - 1 + padded.shape[0] - (TAPS - 1), :]
    ramp = jnp.zeros((TAPS - 1, LANES), F32)
    gain = jnp.zeros((1, LANES), F32)
    for m in range(TAPS):
        tap = taps[m : m + 1, :]
        ramp = ramp + tap * padded[m : m + TAPS - 1, :]
        gain = gain + tap * padded[TAPS - 1 + m : TAPS + m, :]
    gain = jnp.broadcast_to(gain * math.sqrt(L), (8, LANES))
    lane = lax.broadcasted_iota(jnp.int32, (8, LANES), 1)
    swapped = pltpu.roll(gain, BINS, 1)
    gain_re = jnp.where(lane < BINS, gain, swapped)[:1]
    gain_im = jnp.where(lane < BINS, -swapped, gain)[:1]
    columns = table[...]
    pure = columns * gain_re + pltpu.roll(columns, BINS, 1) * gain_im
    blocks[...] = pure.astype(BF16)
    rise[...] = jnp.zeros_like(rise)
    rise[rise.shape[0] - (TAPS - 1) :, :] = -ramp
    ahead = JITTER - (TAPS - 1)
    fall[0:ahead, :] = pure[L - ahead :]
    fall[ahead:JITTER, :] = pure[: TAPS - 1] - ramp
    fall[JITTER:, :] = jnp.zeros((fall.shape[0] - JITTER, LANES), F32)

    before = jnp.zeros((channels, LANES), F32)
    for q in range(GROUP):
        offset = meta[q]
        edges = edge_table(rise, fall, offset)
        if q == 0:
            part = matmul(record[:, 0:JITTER].astype(BF16), edges[RIM:])
        else:
            part = matmul(record[:, HOP * q - RIM : HOP * q + JITTER].astype(BF16), edges)
        place = HOP * q + offset - (TAPS - 1)
        part = (part + turn(before, place)) * meta[GROUP + q].astype(F32)
        upright = across(part)
        for c in range(collected.shape[0]):
            piece = upright[:, 128 * c : 128 * c + 128]
            collected[c, pl.ds(q, BINS, stride=2 * GROUP), :] = piece[:BINS]
            collected[c, pl.ds(GROUP + q, BINS, stride=2 * GROUP), :] = piece[BINS:]
        if q < GROUP - 1:
            before = before + matmul(
                record[:, HOP * q : HOP * q + HOP].astype(BF16), blocks[HOP * q : HOP * q + HOP, :]
            )
    width = min(128, channels)
    for c in range(collected.shape[0]):
        block = collected[c].reshape(BINS, 2 * GROUP, 128).astype(BF16)
        parts[:, :, width * c : width * c + width] = block[:, :, :width]


def border_parts(record, whitening, meta):
    channels = record.shape[0]
    taps = jnp.broadcast_to(jnp.pad(whitening, (0, 7))[:, None], (TAPS + 7, LANES))
    vmem = pl.BlockSpec(memory_space=pltpu.VMEM)
    lead = L - HOP + JITTER
    return pl.pallas_call(
        border_kernel,
        grid=(1,),
        out_shape=(
            jax.ShapeDtypeStruct((BINS, 2 * GROUP, channels), BF16),
            jax.ShapeDtypeStruct((L, LANES), BF16),
            jax.ShapeDtypeStruct((EDGE, LANES), F32),
            jax.ShapeDtypeStruct((2 * JITTER, LANES), F32),
        ),
        in_specs=[
            pl.BlockSpec(memory_space=pltpu.SMEM),
            vmem,
            vmem,
            pl.BlockSpec((channels, lead), lambda i: (0, 0)),
        ],
        out_specs=(vmem, vmem, vmem, vmem),
        scratch_shapes=[
            pltpu.VMEM((2 * TAPS + 6, LANES), F32),
            pltpu.VMEM((max(channels // 128, 1), 2 * GROUP * BINS, 128), F32),
        ],
        compiler_params=pltpu.CompilerParams(vmem_limit_bytes=48 * MIB),
        cost_estimate=pl.CostEstimate(
            flops=2 * channels * LANES * 3072, bytes_accessed=4 * channels * lead, transcendentals=0
        ),
        name="border_parts",
    )(meta, taps, phase_table(), record)


def spectra_kernel(offsets, valid, record, rim, blocks, rise, fall, out, samples, later, collected, sems):
    channels, slab = record.shape
    steps = slab // L
    windows = out.shape[2]

    def fetch(s):
        return pltpu.make_async_copy(
            record.at[:, pl.ds(L * s, L)], samples.at[:, pl.ds(RIM + L * s, L)], sems.at[s]
        )

    for s in range(steps):
        fetch(s).start()
    samples[:, 0:RIM] = rim[...].astype(F32)
    samples[:, RIM + slab :] = jnp.zeros((channels, samples.shape[1] - RIM - slab), F32)

    def block_sums(s):
        found = []
        for i in range(GROUP):
            begin = pl.multiple_of(RIM + L * s + HOP * i, 128)
            found.append(
                matmul(samples[:, pl.ds(begin, HOP)].astype(BF16), blocks[HOP * i : HOP * i + HOP, :])
            )
        return found

    def keep(found):
        total = found[GROUP - 1]
        later[GROUP - 1] = total
        for q in range(GROUP - 2, -1, -1):
            total = total + found[q]
            later[q] = total

    def one_window(w, q, before):
        offset = offsets[w]
        begin = pl.multiple_of(HOP * w, 128)
        ends = samples[:, pl.ds(begin + L, EDGE)] - samples[:, pl.ds(begin, EDGE)]
        part = matmul(ends.astype(BF16), edge_table(rise, fall, offset))
        total = later[q] if before is None else later[q] + before
        part = (part + turn(total, HOP * q + offset - (TAPS - 1))) * valid[w].astype(F32)
        upright = across(part)
        for c in range(collected.shape[0]):
            collected[c, pl.ds(w, LANES, stride=windows), :] = upright[:, 128 * c : 128 * c + 128]

    fetch(0).wait()
    keep(block_sums(0))

    @pl.loop(0, steps - 1)
    def _(s):
        fetch(s + 1).wait()
        found = block_sums(s + 1)
        before = None
        for q in range(GROUP):
            one_window(GROUP * s + q, q, before)
            before = found[q] if before is None else before + found[q]
        keep(found)

    for q in range(GROUP):
        one_window(GROUP * (steps - 1) + q, q, None)

    width = min(128, channels)
    for c in range(collected.shape[0]):
        block = collected[c].reshape(LANES, windows, 128).astype(BF16)
        out[:, 0, :, width * c : width * c + width] = block[:BINS, :, :width]
        out[:, 1, :, width * c : width * c + width] = block[BINS:, :, :width]


def own_spectra(record, rim, offsets, valid, blocks, rise, fall):
    channels, slab = record.shape
    windows = offsets.shape[0]
    smem = pl.BlockSpec(memory_space=pltpu.SMEM)
    vmem = pl.BlockSpec(memory_space=pltpu.VMEM)
    return pl.pallas_call(
        spectra_kernel,
        out_shape=jax.ShapeDtypeStruct((BINS, 2, windows, channels), BF16),
        in_specs=[smem, smem, pl.BlockSpec(memory_space=pl.ANY), vmem, vmem, vmem, vmem],
        out_specs=vmem,
        scratch_shapes=[
            pltpu.VMEM((channels, RIM + slab + L - HOP + JITTER), F32),
            pltpu.VMEM((GROUP, channels, LANES), F32),
            pltpu.VMEM((max(channels // 128, 1), LANES * windows, 128), F32),
            pltpu.SemaphoreType.DMA((slab // L,)),
        ],
        compiler_params=pltpu.CompilerParams(vmem_limit_bytes=56 * MIB),
        cost_estimate=pl.CostEstimate(
            flops=2 * channels * LANES * 896 * windows, bytes_accessed=4 * channels * slab, transcendentals=0
        ),
        name="own_spectra",
    )(offsets, valid, record, rim, blocks, rise, fall)


def join_kernel(own, parts, *chunks):
    windows = own.shape[2]
    half = windows - 2 * GROUP
    part = parts[...].astype(F32)
    row = lax.broadcasted_iota(jnp.int32, part.shape, 1)
    late = row >= GROUP
    moved = jnp.concatenate([part[:, GROUP:], part[:, :GROUP]], axis=1)
    for ri, extra in enumerate((moved, part)):
        spectra = own[:, ri].astype(F32)
        upper = spectra[:, half:] + jnp.where(late, extra, 0.0)
        joined = jnp.concatenate([spectra[:, :half], upper], axis=1).astype(BF16)
        for p, chunk in enumerate(chunks):
            chunk[0, :, ri] = joined[PAIR * p : PAIR * p + PAIR]


def joined_chunks(own, parts, devices):
    _, _, windows, channels = own.shape
    bins = BINS // devices
    n = bins // PAIR
    shape = (devices, PAIR, 2, windows, channels)
    return pl.pallas_call(
        join_kernel,
        grid=(devices,),
        out_shape=(jax.ShapeDtypeStruct(shape, BF16),) * n,
        in_specs=[
            pl.BlockSpec((bins, 2, windows, channels), lambda g: (g, 0, 0, 0)),
            pl.BlockSpec((bins, 2 * GROUP, channels), lambda g: (g, 0, 0)),
        ],
        out_specs=(pl.BlockSpec((1,) + shape[1:], lambda g: (g, 0, 0, 0, 0)),) * n,
        compiler_params=pltpu.CompilerParams(vmem_limit_bytes=32 * MIB),
        name="joined_chunks",
    )(own, parts)


def cross_kernel(scale, own, arrival, *rest):
    out = rest[-1]
    sources, _, _, windows, channels = own.shape
    depth = sources * 2 * windows
    straight = own[:, 0].reshape(depth, channels)
    turned = jnp.concatenate([own[:, 0, 1:], -own[:, 0, :1]], axis=1).reshape(depth, channels)
    left = jnp.concatenate([straight, turned], axis=1)
    for n in range(arrival.shape[0]):
        right = arrival[n, :, 0].reshape(depth, channels)
        both = lax.dot_general(left, right, (((0,), (0,)), ((), ())), preferred_element_type=F32) * scale
        out[0, 0, :, channels * n : channels * n + channels] = both[:channels].astype(BF16)
        out[0, 1, :, channels * n : channels * n + channels] = both[channels:].astype(BF16)


def cross_products(own, arrival, result, chunk, bins):
    sources, _, _, windows, channels = own.shape
    blocks = arrival.shape[0]
    shape = (bins, 2, channels, blocks * channels)
    operands = [own, arrival]
    in_specs = [
        pl.BlockSpec((sources, 1, 2, windows, channels), lambda f: (0, f, 0, 0, 0)),
        pl.BlockSpec((blocks, sources, 1, 2, windows, channels), lambda f: (0, 0, f, 0, 0, 0)),
    ]
    aliases = {}
    if result is not None:
        operands.append(result)
        in_specs.append(pl.BlockSpec(memory_space=pl.ANY))
        aliases = {2: 0}
    flops = 2 * PAIR * 2 * channels * blocks * channels * sources * 2 * windows
    return pl.pallas_call(
        functools.partial(cross_kernel, 1.0 / (sources * windows)),
        grid=(PAIR,),
        out_shape=jax.ShapeDtypeStruct(shape, BF16),
        in_specs=in_specs,
        out_specs=pl.BlockSpec((1,) + shape[1:], lambda f: (PAIR * chunk + f, 0, 0, 0)),
        input_output_aliases=aliases,
        compiler_params=pltpu.CompilerParams(vmem_limit_bytes=56 * MIB),
        cost_estimate=pl.CostEstimate(
            flops=flops, bytes_accessed=2 * PAIR * 2 * channels * blocks * channels, transcendentals=0
        ),
        name=f"cross_products_{chunk}",
    )(*operands)


def per_device(record, whitening, offsets, window_valid):
    devices = lax.axis_size("tm")
    slab = record.shape[1]
    bins = BINS // devices
    meta = jnp.concatenate([offsets[-GROUP:], window_valid[-GROUP:]])
    meta = from_behind(meta, "tm", 1)
    rim = from_behind(record[:, slab - RIM :].astype(BF16), "tm", 1)
    parts, blocks, rise, fall = border_parts(record, whitening, meta)
    parts = from_behind(parts, "tm", -1)
    own = own_spectra(record, rim, offsets, window_valid, blocks, rise, fall)
    chunks = joined_chunks(own, parts, devices)
    result = None
    for p, chunk in enumerate(chunks):
        mine = lax.all_to_all(chunk, "tm", split_axis=0, concat_axis=0, tiled=True)
        arrival = lax.all_gather(mine, "chan", axis=0, tiled=False)
        result = cross_products(mine, arrival, result, p, bins)
    return result


def solution(mesh):
    in_specs = (P("chan", "tm"), P(), P("tm"), P("tm"))
    out_specs = P("tm", None, "chan", None)
    return jax.shard_map(
        per_device, mesh=mesh, in_specs=in_specs, out_specs=out_specs, check_vma=False
    )
```

```python
import functools
import math

import jax
import jax.numpy as jnp
import numpy as np
from jax import lax
from jax.experimental import pallas as pl
from jax.experimental.pallas import tpu as pltpu
from jax.sharding import PartitionSpec as P

L = 2048
HOP = 512
JITTER = 256
TAPS = 65
BINS = 64
K0 = 64
RIM = 128
GROUP = L // HOP
EDGE = RIM + JITTER
LANES = 2 * BINS
MIB = 1 << 20
F32 = jnp.float32
BF16 = jnp.bfloat16


def from_behind(shard, axis, by):
    devices = lax.axis_size(axis)
    pairs = [(i, i + by) for i in range(devices) if 0 <= i + by < devices]
    return lax.ppermute(shard, axis, pairs)


def phase_table():
    sample = np.arange(L) - (TAPS - 1)
    angles = 2.0 * np.pi * np.mod(sample[:, None] * (K0 + np.arange(BINS))[None, :], L) / L
    return (np.concatenate([np.cos(angles), -np.sin(angles)], axis=1) / math.sqrt(L)).astype(np.float32)


def matmul(a, b):
    return jnp.dot(a, b, preferred_element_type=F32)


def turn(values, place):
    lane = lax.broadcasted_iota(jnp.int32, (8, LANES), 1)
    bins = K0 + (lane & (BINS - 1))
    angles = ((bins * (place + L)) & (L - 1)).astype(F32) * (2.0 * math.pi / L)
    sine = jnp.sin(angles)
    sine = jnp.where(lane < BINS, -sine, sine)
    return values * jnp.cos(angles)[:1] + pltpu.roll(values, BINS, 1) * sine[:1]


def edge_table(rise, fall, offset):
    start = JITTER - offset
    return jnp.concatenate([rise[pl.ds(start, RIM), :], fall[pl.ds(start, JITTER), :]], axis=0).astype(BF16)


def across(values):
    channels = values.shape[0]
    if channels % 128:
        values = jnp.pad(values, ((0, 128 - channels), (0, 0)))
    return values.T


def outbox_kernel(offsets, valid, record, out):
    top = record[0:8, :]
    row = lax.broadcasted_iota(jnp.int32, top.shape, 0)
    lane = lax.broadcasted_iota(jnp.int32, top.shape, 1)
    first = offsets.shape[0] - GROUP
    for q in range(GROUP):
        top = jnp.where((row == 0) & (lane == q), offsets[first + q].astype(F32), top)
        top = jnp.where((row == 0) & (lane == GROUP + q), valid[first + q].astype(F32), top)
    out[...] = jnp.concatenate([top, record[8:, :]], axis=0).astype(BF16)


def outbox(record, offsets, valid):
    channels, slab = record.shape
    smem = pl.BlockSpec(memory_space=pltpu.SMEM)
    return pl.pallas_call(
        outbox_kernel,
        grid=(1,),
        out_shape=jax.ShapeDtypeStruct((channels, RIM), BF16),
        in_specs=[smem, smem, pl.BlockSpec((channels, RIM), lambda i: (0, slab // RIM - 1))],
        out_specs=pl.BlockSpec(memory_space=pltpu.VMEM),
        name="outbox",
    )(offsets, valid, record)


def tables_kernel(taps, table, blocks, rise, fall, padded):
    padded[0 : TAPS - 1, :] = jnp.zeros((TAPS - 1, LANES), F32)
    padded[TAPS - 1 :, :] = table[TAPS - 1 : TAPS - 1 + padded.shape[0] - (TAPS - 1), :]
    ramp = jnp.zeros((TAPS - 1, LANES), F32)
    gain = jnp.zeros((1, LANES), F32)
    for m in range(TAPS):
        tap = taps[m]
        ramp = ramp + tap * padded[m : m + TAPS - 1, :]
        gain = gain + tap * padded[TAPS - 1 + m : TAPS + m, :]
    gain = jnp.broadcast_to(gain * math.sqrt(L), (8, LANES))
    lane = lax.broadcasted_iota(jnp.int32, (8, LANES), 1)
    swapped = pltpu.roll(gain, BINS, 1)
    gain_re = jnp.where(lane < BINS, gain, swapped)[:1]
    gain_im = jnp.where(lane < BINS, -swapped, gain)[:1]
    columns = table[...]
    pure = columns * gain_re + pltpu.roll(columns, BINS, 1) * gain_im
    blocks[...] = pure.astype(BF16)
    rise[...] = jnp.zeros_like(rise)
    rise[rise.shape[0] - (TAPS - 1) :, :] = -ramp
    ahead = JITTER - (TAPS - 1)
    fall[0:ahead, :] = pure[L - ahead :]
    fall[ahead:JITTER, :] = pure[: TAPS - 1] - ramp
    fall[JITTER:, :] = jnp.zeros((fall.shape[0] - JITTER, LANES), F32)


def tables(whitening):
    vmem = pl.BlockSpec(memory_space=pltpu.VMEM)
    return pl.pallas_call(
        tables_kernel,
        out_shape=(
            jax.ShapeDtypeStruct((L, LANES), BF16),
            jax.ShapeDtypeStruct((EDGE, LANES), F32),
            jax.ShapeDtypeStruct((2 * JITTER, LANES), F32),
        ),
        in_specs=[pl.BlockSpec(memory_space=pltpu.SMEM), vmem],
        out_specs=(vmem, vmem, vmem),
        scratch_shapes=[pltpu.VMEM((2 * TAPS + 6, LANES), F32)],
        compiler_params=pltpu.CompilerParams(vmem_limit_bytes=16 * MIB),
        name="tables",
    )(whitening, phase_table())


def border_kernel(inbox, record, blocks, rise, fall, parts, collected):
    channels = record.shape[0]
    head = inbox[0:16, :].astype(F32)[:1]
    lane = lax.broadcasted_iota(jnp.int32, (1, LANES), 1)

    def told(at):
        return jnp.sum(jnp.where(lane == at, head, 0.0)).astype(jnp.int32)

    before = jnp.zeros((channels, LANES), F32)
    for q in range(GROUP):
        offset = told(q)
        edges = edge_table(rise, fall, offset)
        if q == 0:
            part = matmul(record[:, 0:JITTER].astype(BF16), edges[RIM:])
        else:
            part = matmul(record[:, HOP * q - RIM : HOP * q + JITTER].astype(BF16), edges)
        place = HOP * q + offset - (TAPS - 1)
        part = (part + turn(before, place)) * told(GROUP + q).astype(F32)
        upright = across(part)
        for c in range(collected.shape[0]):
            piece = upright[:, 128 * c : 128 * c + 128]
            collected[c, pl.ds(q, BINS, stride=2 * GROUP), :] = piece[:BINS]
            collected[c, pl.ds(GROUP + q, BINS, stride=2 * GROUP), :] = piece[BINS:]
        if q < GROUP - 1:
            before = before + matmul(
                record[:, HOP * q : HOP * q + HOP].astype(BF16), blocks[HOP * q : HOP * q + HOP, :]
            )
    width = min(128, channels)
    for c in range(collected.shape[0]):
        block = collected[c].reshape(BINS, 2 * GROUP, 128).astype(BF16)
        parts[:, :, width * c : width * c + width] = block[:, :, :width]


def border_parts(record, inbox, blocks, rise, fall):
    channels = record.shape[0]
    vmem = pl.BlockSpec(memory_space=pltpu.VMEM)
    lead = L - HOP + JITTER
    return pl.pallas_call(
        border_kernel,
        grid=(1,),
        out_shape=jax.ShapeDtypeStruct((BINS, 2 * GROUP, channels), BF16),
        in_specs=[vmem, pl.BlockSpec((channels, lead), lambda i: (0, 0)), vmem, vmem, vmem],
        out_specs=vmem,
        scratch_shapes=[pltpu.VMEM((max(channels // 128, 1), 2 * GROUP * BINS, 128), F32)],
        compiler_params=pltpu.CompilerParams(vmem_limit_bytes=24 * MIB),
        cost_estimate=pl.CostEstimate(
            flops=2 * channels * LANES * 3072, bytes_accessed=4 * channels * lead, transcendentals=0
        ),
        name="border_parts",
    )(inbox, record, blocks, rise, fall)


def spectra_kernel(offsets, valid, record, rim, blocks, rise, fall, out, samples, later, collected, sems):
    channels, slab = record.shape
    steps = slab // L
    windows = out.shape[2]

    def fetch(s):
        return pltpu.make_async_copy(
            record.at[:, pl.ds(L * s, L)], samples.at[:, pl.ds(RIM + L * s, L)], sems.at[s]
        )

    for s in range(steps):
        fetch(s).start()
    samples[:, 0:RIM] = rim[...].astype(F32)
    samples[:, RIM + slab :] = jnp.zeros((channels, samples.shape[1] - RIM - slab), F32)

    def block_sums(s):
        found = []
        for i in range(GROUP):
            begin = pl.multiple_of(RIM + L * s + HOP * i, 128)
            found.append(
                matmul(samples[:, pl.ds(begin, HOP)].astype(BF16), blocks[HOP * i : HOP * i + HOP, :])
            )
        return found

    def keep(found):
        total = found[GROUP - 1]
        later[GROUP - 1] = total
        for q in range(GROUP - 2, -1, -1):
            total = total + found[q]
            later[q] = total

    def one_window(w, q, before):
        offset = offsets[w]
        begin = pl.multiple_of(HOP * w, 128)
        ends = samples[:, pl.ds(begin + L, EDGE)] - samples[:, pl.ds(begin, EDGE)]
        part = matmul(ends.astype(BF16), edge_table(rise, fall, offset))
        total = later[q] if before is None else later[q] + before
        part = (part + turn(total, HOP * q + offset - (TAPS - 1))) * valid[w].astype(F32)
        upright = across(part)
        for c in range(collected.shape[0]):
            collected[c, pl.ds(w, LANES, stride=windows), :] = upright[:, 128 * c : 128 * c + 128]

    fetch(0).wait()
    keep(block_sums(0))

    @pl.loop(0, steps - 1)
    def _(s):
        fetch(s + 1).wait()
        found = block_sums(s + 1)
        before = None
        for q in range(GROUP):
            one_window(GROUP * s + q, q, before)
            before = found[q] if before is None else before + found[q]
        keep(found)

    for q in range(GROUP):
        one_window(GROUP * (steps - 1) + q, q, None)

    width = min(128, channels)
    for c in range(collected.shape[0]):
        block = collected[c].reshape(LANES, windows, 128).astype(BF16)
        out[:, 0, :, width * c : width * c + width] = block[:BINS, :, :width]
        out[:, 1, :, width * c : width * c + width] = block[BINS:, :, :width]


def own_spectra(record, rim, offsets, valid, blocks, rise, fall):
    channels, slab = record.shape
    windows = offsets.shape[0]
    smem = pl.BlockSpec(memory_space=pltpu.SMEM)
    vmem = pl.BlockSpec(memory_space=pltpu.VMEM)
    return pl.pallas_call(
        spectra_kernel,
        out_shape=jax.ShapeDtypeStruct((BINS, 2, windows, channels), BF16),
        in_specs=[smem, smem, pl.BlockSpec(memory_space=pl.ANY), vmem, vmem, vmem, vmem],
        out_specs=vmem,
        scratch_shapes=[
            pltpu.VMEM((channels, RIM + slab + L - HOP + JITTER), F32),
            pltpu.VMEM((GROUP, channels, LANES), F32),
            pltpu.VMEM((max(channels // 128, 1), LANES * windows, 128), F32),
            pltpu.SemaphoreType.DMA((slab // L,)),
        ],
        compiler_params=pltpu.CompilerParams(vmem_limit_bytes=40 * MIB),
        cost_estimate=pl.CostEstimate(
            flops=2 * channels * LANES * 896 * windows, bytes_accessed=4 * channels * slab, transcendentals=0
        ),
        name="own_spectra",
    )(offsets, valid, record, rim, blocks, rise, fall)


def join_kernel(own, parts, *chunks):
    windows = own.shape[2]
    half = windows - 2 * GROUP
    part = parts[...].astype(F32)
    row = lax.broadcasted_iota(jnp.int32, part.shape, 1)
    late = row >= GROUP
    moved = jnp.concatenate([part[:, GROUP:], part[:, :GROUP]], axis=1)
    for ri, extra in enumerate((moved, part)):
        spectra = own[:, ri].astype(F32)
        upper = spectra[:, half:] + jnp.where(late, extra, 0.0)
        joined = jnp.concatenate([spectra[:, :half], upper], axis=1).astype(BF16)
        begin = 0
        for chunk in chunks:
            count = chunk.shape[1]
            chunk[0, :, ri] = joined[begin : begin + count]
            begin += count


def chunk_sizes(bins):
    count = min(3, bins)
    return [(bins + count - 1 - c) // count for c in range(count)]


def joined_chunks(own, parts, devices):
    _, _, windows, channels = own.shape
    bins = BINS // devices
    shapes = [(devices, count, 2, windows, channels) for count in chunk_sizes(bins)]
    return pl.pallas_call(
        join_kernel,
        grid=(devices,),
        out_shape=tuple(jax.ShapeDtypeStruct(shape, BF16) for shape in shapes),
        in_specs=[
            pl.BlockSpec((bins, 2, windows, channels), lambda g: (g, 0, 0, 0)),
            pl.BlockSpec((bins, 2 * GROUP, channels), lambda g: (g, 0, 0)),
        ],
        out_specs=tuple(pl.BlockSpec((1,) + shape[1:], lambda g: (g, 0, 0, 0, 0)) for shape in shapes),
        compiler_params=pltpu.CompilerParams(vmem_limit_bytes=16 * MIB),
        name="joined_chunks",
    )(own, parts)


def cross_kernel(scale, stacked, me, own, *rest):
    out = rest[-1]
    sources, _, _, windows, channels = own.shape
    depth = sources * 2 * windows
    straight = own[:, 0].reshape(depth, channels)
    turned = jnp.concatenate([own[:, 0, 1:], -own[:, 0, :1]], axis=1).reshape(depth, channels)
    left = jnp.concatenate([straight, turned], axis=1)
    blocks = rest[0].shape[0] if stacked else len(rest) - 1
    for n in range(blocks):
        if stacked:
            right, at = rest[0][n, :, 0], channels * n
        else:
            right = (own if n == 0 else rest[n - 1])[:, 0]
            at = pl.multiple_of(channels * (me[0] ^ n), 128)
        right = right.reshape(depth, channels)
        both = lax.dot_general(left, right, (((0,), (0,)), ((), ())), preferred_element_type=F32) * scale
        out[0, 0, :, pl.ds(at, channels)] = both[:channels].astype(BF16)
        out[0, 1, :, pl.ds(at, channels)] = both[channels:].astype(BF16)


def cross_products(own, others, result, begin, bins):
    sources, count, _, windows, channels = own.shape
    stacked = not isinstance(others, list)
    blocks = others.shape[0] if stacked else len(others) + 1
    shape = (bins, 2, channels, blocks * channels)
    spec = pl.BlockSpec((sources, 1, 2, windows, channels), lambda f: (0, f, 0, 0, 0))
    smem = pl.BlockSpec(memory_space=pltpu.SMEM)
    operands = [lax.axis_index("chan").astype(jnp.int32).reshape(1), own]
    in_specs = [smem, spec]
    if stacked:
        operands.append(others)
        in_specs.append(pl.BlockSpec((blocks, sources, 1, 2, windows, channels), lambda f: (0, 0, f, 0, 0, 0)))
    else:
        operands += others
        in_specs += [spec] * len(others)
    if result is None:
        result = jnp.zeros((8, 128), BF16)
        aliases = {}
    else:
        aliases = {len(operands): 0}
    operands.append(result)
    in_specs.append(pl.BlockSpec(memory_space=pl.ANY))
    flops = 2 * count * 2 * channels * blocks * channels * sources * 2 * windows
    return pl.pallas_call(
        functools.partial(cross_kernel, 1.0 / (sources * windows), stacked),
        grid=(count,),
        out_shape=jax.ShapeDtypeStruct(shape, BF16),
        in_specs=in_specs,
        out_specs=pl.BlockSpec((1,) + shape[1:], lambda f: (begin + f, 0, 0, 0)),
        input_output_aliases=aliases,
        compiler_params=pltpu.CompilerParams(vmem_limit_bytes=36 * MIB),
        cost_estimate=pl.CostEstimate(
            flops=flops, bytes_accessed=2 * count * 2 * channels * blocks * channels, transcendentals=0
        ),
        name="cross_products",
    )(*operands)


def swapped(shard, axis, bit):
    devices = lax.axis_size(axis)
    return lax.ppermute(shard, axis, [(i, i ^ bit) for i in range(devices)])


def gathered(mine):
    devices = lax.axis_size("chan")
    if devices & (devices - 1) or mine.shape[-1] % 128:
        return lax.all_gather(mine, "chan", axis=0, tiled=False)
    held = {0: mine}
    bit = devices // 2
    while bit:
        held.update({n | bit: swapped(block, "chan", bit) for n, block in list(held.items())})
        bit //= 2
    return [held[n] for n in range(1, devices)]


def per_device(record, whitening, offsets, window_valid):
    devices = lax.axis_size("tm")
    bins = BINS // devices
    inbox = from_behind(outbox(record, offsets, window_valid), "tm", 1)
    blocks, rise, fall = tables(whitening)
    parts = from_behind(border_parts(record, inbox, blocks, rise, fall), "tm", -1)
    own = own_spectra(record, inbox, offsets, window_valid, blocks, rise, fall)
    result, begin = None, 0
    for chunk in joined_chunks(own, parts, devices):
        mine = lax.all_to_all(chunk, "tm", split_axis=0, concat_axis=0, tiled=True)
        result = cross_products(mine, gathered(mine), result, begin, bins)
        begin += chunk.shape[1]
    return result


def solution(mesh):
    in_specs = (P("chan", "tm"), P(), P("tm"), P("tm"))
    out_specs = P("tm", None, "chan", None)
    return jax.shard_map(
        per_device, mesh=mesh, in_specs=in_specs, out_specs=out_specs, check_vma=False
    )
```

```python
import functools
import math

import jax
import jax.numpy as jnp
import numpy as np
from jax import lax
from jax.experimental import pallas as pl
from jax.experimental.pallas import tpu as pltpu
from jax.sharding import PartitionSpec as P

L = 2048
HOP = 512
JITTER = 256
TAPS = 65
BINS = 64
K0 = 64
RIM = 128
GROUP = L // HOP
EDGE = RIM + JITTER
LANES = 2 * BINS
MIB = 1 << 20
F32 = jnp.float32
BF16 = jnp.bfloat16


def from_behind(shard, axis, by):
    devices = lax.axis_size(axis)
    pairs = [(i, i + by) for i in range(devices) if 0 <= i + by < devices]
    return lax.ppermute(shard, axis, pairs)


def phase_table():
    sample = np.arange(L) - (TAPS - 1)
    angles = 2.0 * np.pi * np.mod(sample[:, None] * (K0 + np.arange(BINS))[None, :], L) / L
    return (np.concatenate([np.cos(angles), -np.sin(angles)], axis=1) / math.sqrt(L)).astype(np.float32)


def matmul(a, b):
    return jnp.dot(a, b, preferred_element_type=F32)


def turn(values, place):
    lane = lax.broadcasted_iota(jnp.int32, (8, LANES), 1)
    bins = K0 + (lane & (BINS - 1))
    angles = ((bins * (place + L)) & (L - 1)).astype(F32) * (2.0 * math.pi / L)
    sine = jnp.sin(angles)
    sine = jnp.where(lane < BINS, -sine, sine)
    return values * jnp.cos(angles)[:1] + pltpu.roll(values, BINS, 1) * sine[:1]


def edge_table(rise, fall, offset):
    start = JITTER - offset
    return jnp.concatenate([rise[pl.ds(start, RIM), :], fall[pl.ds(start, JITTER), :]], axis=0).astype(BF16)


def across(values):
    channels = values.shape[0]
    if channels % 128:
        values = jnp.pad(values, ((0, 128 - channels), (0, 0)))
    return values.T


def outbox_kernel(offsets, valid, record, out):
    top = record[0:8, :]
    row = lax.broadcasted_iota(jnp.int32, top.shape, 0)
    lane = lax.broadcasted_iota(jnp.int32, top.shape, 1)
    first = offsets.shape[0] - GROUP
    for q in range(GROUP):
        top = jnp.where((row == 0) & (lane == q), offsets[first + q].astype(F32), top)
        top = jnp.where((row == 0) & (lane == GROUP + q), valid[first + q].astype(F32), top)
    out[...] = jnp.concatenate([top, record[8:, :]], axis=0).astype(BF16)


def outbox(record, offsets, valid):
    channels, slab = record.shape
    smem = pl.BlockSpec(memory_space=pltpu.SMEM)
    return pl.pallas_call(
        outbox_kernel,
        grid=(1,),
        out_shape=jax.ShapeDtypeStruct((channels, RIM), BF16),
        in_specs=[smem, smem, pl.BlockSpec((channels, RIM), lambda i: (0, slab // RIM - 1))],
        out_specs=pl.BlockSpec(memory_space=pltpu.VMEM),
        compiler_params=pltpu.CompilerParams(vmem_limit_bytes=50 * MIB),
        name="outbox",
    )(offsets, valid, record)


def tables_kernel(taps, table, blocks, rise, fall, padded):
    padded[0 : TAPS - 1, :] = jnp.zeros((TAPS - 1, LANES), F32)
    padded[TAPS - 1 :, :] = table[TAPS - 1 : TAPS - 1 + padded.shape[0] - (TAPS - 1), :]
    ramp = jnp.zeros((TAPS - 1, LANES), F32)
    gain = jnp.zeros((1, LANES), F32)
    for m in range(TAPS):
        tap = taps[m]
        ramp = ramp + tap * padded[m : m + TAPS - 1, :]
        gain = gain + tap * padded[TAPS - 1 + m : TAPS + m, :]
    gain = jnp.broadcast_to(gain * math.sqrt(L), (8, LANES))
    lane = lax.broadcasted_iota(jnp.int32, (8, LANES), 1)
    swapped = pltpu.roll(gain, BINS, 1)
    gain_re = jnp.where(lane < BINS, gain, swapped)[:1]
    gain_im = jnp.where(lane < BINS, -swapped, gain)[:1]
    columns = table[...]
    pure = columns * gain_re + pltpu.roll(columns, BINS, 1) * gain_im
    blocks[...] = pure.astype(BF16)
    rise[...] = jnp.zeros_like(rise)
    rise[rise.shape[0] - (TAPS - 1) :, :] = -ramp
    ahead = JITTER - (TAPS - 1)
    fall[0:ahead, :] = pure[L - ahead :]
    fall[ahead:JITTER, :] = pure[: TAPS - 1] - ramp
    fall[JITTER:, :] = jnp.zeros((fall.shape[0] - JITTER, LANES), F32)


def tables(whitening):
    vmem = pl.BlockSpec(memory_space=pltpu.VMEM)
    return pl.pallas_call(
        tables_kernel,
        out_shape=(
            jax.ShapeDtypeStruct((L, LANES), BF16),
            jax.ShapeDtypeStruct((EDGE, LANES), F32),
            jax.ShapeDtypeStruct((2 * JITTER, LANES), F32),
        ),
        in_specs=[pl.BlockSpec(memory_space=pltpu.SMEM), vmem],
        out_specs=(vmem, vmem, vmem),
        scratch_shapes=[pltpu.VMEM((2 * TAPS + 6, LANES), F32)],
        compiler_params=pltpu.CompilerParams(vmem_limit_bytes=16 * MIB),
        name="tables",
    )(whitening, phase_table())


def border_kernel(inbox, record, blocks, rise, fall, parts, collected):
    channels = record.shape[0]
    head = inbox[0:16, :].astype(F32)[:1]
    lane = lax.broadcasted_iota(jnp.int32, (1, LANES), 1)

    def told(at):
        return jnp.sum(jnp.where(lane == at, head, 0.0)).astype(jnp.int32)

    before = jnp.zeros((channels, LANES), F32)
    for q in range(GROUP):
        offset = told(q)
        edges = edge_table(rise, fall, offset)
        if q == 0:
            part = matmul(record[:, 0:JITTER].astype(BF16), edges[RIM:])
        else:
            part = matmul(record[:, HOP * q - RIM : HOP * q + JITTER].astype(BF16), edges)
        place = HOP * q + offset - (TAPS - 1)
        part = (part + turn(before, place)) * told(GROUP + q).astype(F32)
        upright = across(part)
        for c in range(collected.shape[0]):
            piece = upright[:, 128 * c : 128 * c + 128]
            collected[c, pl.ds(q, BINS, stride=2 * GROUP), :] = piece[:BINS]
            collected[c, pl.ds(GROUP + q, BINS, stride=2 * GROUP), :] = piece[BINS:]
        if q < GROUP - 1:
            before = before + matmul(
                record[:, HOP * q : HOP * q + HOP].astype(BF16), blocks[HOP * q : HOP * q + HOP, :]
            )
    width = min(128, channels)
    for c in range(collected.shape[0]):
        block = collected[c].reshape(BINS, 2 * GROUP, 128).astype(BF16)
        parts[:, :, width * c : width * c + width] = block[:, :, :width]


def border_parts(record, inbox, blocks, rise, fall):
    channels = record.shape[0]
    vmem = pl.BlockSpec(memory_space=pltpu.VMEM)
    lead = L - HOP + JITTER
    return pl.pallas_call(
        border_kernel,
        grid=(1,),
        out_shape=jax.ShapeDtypeStruct((BINS, 2 * GROUP, channels), BF16),
        in_specs=[vmem, pl.BlockSpec((channels, lead), lambda i: (0, 0)), vmem, vmem, vmem],
        out_specs=vmem,
        scratch_shapes=[pltpu.VMEM((max(channels // 128, 1), 2 * GROUP * BINS, 128), F32)],
        compiler_params=pltpu.CompilerParams(vmem_limit_bytes=50 * MIB),
        cost_estimate=pl.CostEstimate(
            flops=2 * channels * LANES * 3072, bytes_accessed=4 * channels * lead, transcendentals=0
        ),
        name="border_parts",
    )(inbox, record, blocks, rise, fall)


def spectra_kernel(offsets, valid, record, rim, blocks, rise, fall, out, samples, later, collected, sems):
    channels, slab = record.shape
    steps = slab // L
    windows = out.shape[2]

    def fetch(s):
        return pltpu.make_async_copy(
            record.at[:, pl.ds(L * s, L)], samples.at[:, pl.ds(RIM + L * s, L)], sems.at[s]
        )

    for s in range(steps):
        fetch(s).start()
    samples[:, 0:RIM] = rim[...].astype(F32)
    samples[:, RIM + slab :] = jnp.zeros((channels, samples.shape[1] - RIM - slab), F32)

    def block_sums(s):
        found = []
        for i in range(GROUP):
            begin = pl.multiple_of(RIM + L * s + HOP * i, 128)
            found.append(
                matmul(samples[:, pl.ds(begin, HOP)].astype(BF16), blocks[HOP * i : HOP * i + HOP, :])
            )
        return found

    def keep(found):
        total = found[GROUP - 1]
        later[GROUP - 1] = total
        for q in range(GROUP - 2, -1, -1):
            total = total + found[q]
            later[q] = total

    def one_window(w, q, before):
        offset = offsets[w]
        begin = pl.multiple_of(HOP * w, 128)
        ends = samples[:, pl.ds(begin + L, EDGE)] - samples[:, pl.ds(begin, EDGE)]
        part = matmul(ends.astype(BF16), edge_table(rise, fall, offset))
        total = later[q] if before is None else later[q] + before
        part = (part + turn(total, HOP * q + offset - (TAPS - 1))) * valid[w].astype(F32)
        upright = across(part)
        for c in range(collected.shape[0]):
            collected[c, pl.ds(w, LANES, stride=windows), :] = upright[:, 128 * c : 128 * c + 128]

    fetch(0).wait()
    keep(block_sums(0))

    @pl.loop(0, steps - 1)
    def _(s):
        fetch(s + 1).wait()
        found = block_sums(s + 1)
        before = None
        for q in range(GROUP):
            one_window(GROUP * s + q, q, before)
            before = found[q] if before is None else before + found[q]
        keep(found)

    for q in range(GROUP):
        one_window(GROUP * (steps - 1) + q, q, None)

    width = min(128, channels)
    for c in range(collected.shape[0]):
        block = collected[c].reshape(LANES, windows, 128).astype(BF16)
        out[:, 0, :, width * c : width * c + width] = block[:BINS, :, :width]
        out[:, 1, :, width * c : width * c + width] = block[BINS:, :, :width]


def own_spectra(record, rim, offsets, valid, blocks, rise, fall):
    channels, slab = record.shape
    windows = offsets.shape[0]
    smem = pl.BlockSpec(memory_space=pltpu.SMEM)
    vmem = pl.BlockSpec(memory_space=pltpu.VMEM)
    return pl.pallas_call(
        spectra_kernel,
        out_shape=jax.ShapeDtypeStruct((BINS, 2, windows, channels), BF16),
        in_specs=[smem, smem, pl.BlockSpec(memory_space=pl.ANY), vmem, vmem, vmem, vmem],
        out_specs=vmem,
        scratch_shapes=[
            pltpu.VMEM((channels, RIM + slab + L - HOP + JITTER), F32),
            pltpu.VMEM((GROUP, channels, LANES), F32),
            pltpu.VMEM((max(channels // 128, 1), LANES * windows, 128), F32),
            pltpu.SemaphoreType.DMA((slab // L,)),
        ],
        compiler_params=pltpu.CompilerParams(vmem_limit_bytes=50 * MIB),
        cost_estimate=pl.CostEstimate(
            flops=2 * channels * LANES * 896 * windows, bytes_accessed=4 * channels * slab, transcendentals=0
        ),
        name="own_spectra",
    )(offsets, valid, record, rim, blocks, rise, fall)


def join_kernel(own, parts, *chunks):
    windows = own.shape[2]
    half = windows - 2 * GROUP
    part = parts[...].astype(F32)
    row = lax.broadcasted_iota(jnp.int32, part.shape, 1)
    late = row >= GROUP
    moved = jnp.concatenate([part[:, GROUP:], part[:, :GROUP]], axis=1)
    for ri, extra in enumerate((moved, part)):
        spectra = own[:, ri].astype(F32)
        upper = spectra[:, half:] + jnp.where(late, extra, 0.0)
        joined = jnp.concatenate([spectra[:, :half], upper], axis=1).astype(BF16)
        begin = 0
        for chunk in chunks:
            count = chunk.shape[1]
            chunk[0, :, ri] = joined[begin : begin + count]
            begin += count


def chunk_sizes(bins):
    count = min(3, bins)
    return [(bins + count - 1 - c) // count for c in range(count)]


def joined_chunks(own, parts, devices):
    _, _, windows, channels = own.shape
    bins = BINS // devices
    shapes = [(devices, count, 2, windows, channels) for count in chunk_sizes(bins)]
    return pl.pallas_call(
        join_kernel,
        grid=(devices,),
        out_shape=tuple(jax.ShapeDtypeStruct(shape, BF16) for shape in shapes),
        in_specs=[
            pl.BlockSpec((bins, 2, windows, channels), lambda g: (g, 0, 0, 0)),
            pl.BlockSpec((bins, 2 * GROUP, channels), lambda g: (g, 0, 0)),
        ],
        out_specs=tuple(pl.BlockSpec((1,) + shape[1:], lambda g: (g, 0, 0, 0, 0)) for shape in shapes),
        compiler_params=pltpu.CompilerParams(vmem_limit_bytes=16 * MIB),
        name="joined_chunks",
    )(own, parts)


def cross_kernel(scale, stacked, me, own, *rest):
    out, done = rest[-2:]
    done[...] = jnp.zeros_like(done)
    sources, _, _, windows, channels = own.shape
    depth = sources * 2 * windows
    straight = own[:, 0].reshape(depth, channels)
    turned = jnp.concatenate([own[:, 0, 1:], -own[:, 0, :1]], axis=1).reshape(depth, channels)
    left = jnp.concatenate([straight, turned], axis=1)
    blocks = rest[0].shape[0] if stacked else len(rest) - 2
    for n in range(blocks):
        if stacked:
            right, at = rest[0][n, :, 0], channels * n
        else:
            right = (own if n == 0 else rest[n - 1])[:, 0]
            at = pl.multiple_of(channels * (me[0] ^ n), 128)
        right = right.reshape(depth, channels)
        both = lax.dot_general(left, right, (((0,), (0,)), ((), ())), preferred_element_type=F32) * scale
        out[0, 0, :, pl.ds(at, channels)] = both[:channels].astype(BF16)
        out[0, 1, :, pl.ds(at, channels)] = both[channels:].astype(BF16)


def cross_products(own, others, result, begin, bins):
    sources, count, _, windows, channels = own.shape
    stacked = not isinstance(others, list)
    blocks = others.shape[0] if stacked else len(others) + 1
    shape = (bins, 2, channels, blocks * channels)
    spec = pl.BlockSpec((sources, 1, 2, windows, channels), lambda f: (0, f, 0, 0, 0))
    smem = pl.BlockSpec(memory_space=pltpu.SMEM)
    operands = [lax.axis_index("chan").astype(jnp.int32).reshape(1), own]
    in_specs = [smem, spec]
    if stacked:
        operands.append(others)
        in_specs.append(pl.BlockSpec((blocks, sources, 1, 2, windows, channels), lambda f: (0, 0, f, 0, 0, 0)))
    else:
        operands += others
        in_specs += [spec] * len(others)
    if result is None:
        result, aliases = operands[0], {}
    else:
        aliases = {len(operands): 0}
    operands.append(result)
    in_specs.append(pl.BlockSpec(memory_space=pl.ANY))
    flops = 2 * count * 2 * channels * blocks * channels * sources * 2 * windows
    return pl.pallas_call(
        functools.partial(cross_kernel, 1.0 / (sources * windows), stacked),
        grid=(count,),
        out_shape=(jax.ShapeDtypeStruct(shape, BF16), jax.ShapeDtypeStruct((8, 128), F32)),
        in_specs=in_specs,
        out_specs=(
            pl.BlockSpec((1,) + shape[1:], lambda f: (begin + f, 0, 0, 0)),
            pl.BlockSpec(memory_space=pltpu.VMEM),
        ),
        input_output_aliases=aliases,
        compiler_params=pltpu.CompilerParams(vmem_limit_bytes=36 * MIB),
        cost_estimate=pl.CostEstimate(
            flops=flops, bytes_accessed=2 * count * 2 * channels * blocks * channels, transcendentals=0
        ),
        name="cross_products",
    )(*operands)


def swapped(shard, axis, bit):
    devices = lax.axis_size(axis)
    return lax.ppermute(shard, axis, [(i, i ^ bit) for i in range(devices)])


def fan(shard, axis, bit):
    held = {0: shard}
    while bit:
        held.update({n | bit: swapped(block, axis, bit) for n, block in list(held.items())})
        bit //= 2
    return held


def after_kernel(shard, done, out):
    pass


def after(shard, done):
    if done is None:
        return shard
    anywhere = pl.BlockSpec(memory_space=pl.ANY)
    return pl.pallas_call(
        after_kernel,
        out_shape=jax.ShapeDtypeStruct(shard.shape, shard.dtype),
        in_specs=[anywhere, anywhere],
        out_specs=anywhere,
        input_output_aliases={0: 0},
        name="after",
    )(shard, done)


def per_device(record, whitening, offsets, window_valid):
    devices = lax.axis_size("tm")
    blocks = lax.axis_size("chan")
    stacked = blocks & (blocks - 1) != 0 or record.shape[0] % 128 != 0
    top = blocks // 2
    inbox = from_behind(outbox(record, offsets, window_valid), "tm", 1)
    transform, rise, fall = tables(whitening)
    parts = from_behind(border_parts(record, inbox, transform, rise, fall), "tm", -1)
    own = own_spectra(record, inbox, offsets, window_valid, transform, rise, fall)
    chunks = joined_chunks(own, parts, devices)
    bins = BINS // devices
    sizes = chunk_sizes(bins)
    held, result, done = [], None, None
    for p in range(len(sizes) + 1):
        if p < len(sizes):
            mine = lax.all_to_all(chunks[p], "tm", split_axis=0, concat_axis=0, tiled=True)
            mine = after(mine, done)
            if stacked:
                held.append((mine, lax.all_gather(mine, "chan", axis=0, tiled=False)))
            else:
                held.append((fan(mine, "chan", top // 2), swapped(mine, "chan", top)))
        if p:
            if stacked:
                mine, others = held[p - 1]
            else:
                near, far = held[p - 1]
                found = near | {n | top: block for n, block in fan(after(far, done), "chan", top // 2).items()}
                mine, others = found[0], [found[n] for n in range(1, blocks)]
            result, done = cross_products(mine, others, result, sum(sizes[: p - 1]), bins)
    return result


def solution(mesh):
    in_specs = (P("chan", "tm"), P(), P("tm"), P("tm"))
    out_specs = P("tm", None, "chan", None)
    return jax.shard_map(
        per_device, mesh=mesh, in_specs=in_specs, out_specs=out_specs, check_vma=False
    )
```

```python
import functools
import math

import jax
import jax.numpy as jnp
import numpy as np
from jax import lax
from jax.experimental import pallas as pl
from jax.experimental.pallas import tpu as pltpu
from jax.sharding import PartitionSpec as P

L = 2048
HOP = 512
JITTER = 256
TAPS = 65
BINS = 64
K0 = 64
RIM = 128
GROUP = L // HOP
EDGE = RIM + JITTER
LANES = 2 * BINS
MIB = 1 << 20
F32 = jnp.float32
BF16 = jnp.bfloat16


def from_behind(shard, axis, by):
    devices = lax.axis_size(axis)
    pairs = [(i, i + by) for i in range(devices) if 0 <= i + by < devices]
    return lax.ppermute(shard, axis, pairs)


def phase_table():
    sample = np.arange(L) - (TAPS - 1)
    angles = 2.0 * np.pi * np.mod(sample[:, None] * (K0 + np.arange(BINS))[None, :], L) / L
    return (np.concatenate([np.cos(angles), -np.sin(angles)], axis=1) / math.sqrt(L)).astype(np.float32)


def matmul(a, b):
    return jnp.dot(a, b, preferred_element_type=F32)


def turn(values, place):
    lane = lax.broadcasted_iota(jnp.int32, (8, LANES), 1)
    bins = K0 + (lane & (BINS - 1))
    angles = ((bins * (place + L)) & (L - 1)).astype(F32) * (2.0 * math.pi / L)
    sine = jnp.sin(angles)
    sine = jnp.where(lane < BINS, -sine, sine)
    return values * jnp.cos(angles)[:1] + pltpu.roll(values, BINS, 1) * sine[:1]


def edge_table(rise, fall, offset):
    start = JITTER - offset
    return jnp.concatenate([rise[pl.ds(start, RIM), :], fall[pl.ds(start, JITTER), :]], axis=0).astype(BF16)


def across(values):
    channels = values.shape[0]
    if channels % 128:
        values = jnp.pad(values, ((0, 128 - channels), (0, 0)))
    return values.T


def outbox_kernel(offsets, valid, record, out):
    top = record[0:8, :]
    row = lax.broadcasted_iota(jnp.int32, top.shape, 0)
    lane = lax.broadcasted_iota(jnp.int32, top.shape, 1)
    first = offsets.shape[0] - GROUP
    for q in range(GROUP):
        top = jnp.where((row == 0) & (lane == q), offsets[first + q].astype(F32), top)
        top = jnp.where((row == 0) & (lane == GROUP + q), valid[first + q].astype(F32), top)
    out[...] = jnp.concatenate([top, record[8:, :]], axis=0).astype(BF16)


def outbox(record, offsets, valid):
    channels, slab = record.shape
    smem = pl.BlockSpec(memory_space=pltpu.SMEM)
    return pl.pallas_call(
        outbox_kernel,
        grid=(1,),
        out_shape=jax.ShapeDtypeStruct((channels, RIM), BF16),
        in_specs=[smem, smem, pl.BlockSpec((channels, RIM), lambda i: (0, slab // RIM - 1))],
        out_specs=pl.BlockSpec(memory_space=pltpu.VMEM),
        compiler_params=pltpu.CompilerParams(vmem_limit_bytes=60 * MIB),
        name="outbox",
    )(offsets, valid, record)


def tables_kernel(taps, table, blocks, rise, fall, padded):
    padded[0 : TAPS - 1, :] = jnp.zeros((TAPS - 1, LANES), F32)
    padded[TAPS - 1 :, :] = table[TAPS - 1 : TAPS - 1 + padded.shape[0] - (TAPS - 1), :]
    ramp = jnp.zeros((TAPS - 1, LANES), F32)
    gain = jnp.zeros((1, LANES), F32)
    for m in range(TAPS):
        tap = taps[m]
        ramp = ramp + tap * padded[m : m + TAPS - 1, :]
        gain = gain + tap * padded[TAPS - 1 + m : TAPS + m, :]
    gain = jnp.broadcast_to(gain * math.sqrt(L), (8, LANES))
    lane = lax.broadcasted_iota(jnp.int32, (8, LANES), 1)
    swapped = pltpu.roll(gain, BINS, 1)
    gain_re = jnp.where(lane < BINS, gain, swapped)[:1]
    gain_im = jnp.where(lane < BINS, -swapped, gain)[:1]
    columns = table[...]
    pure = columns * gain_re + pltpu.roll(columns, BINS, 1) * gain_im
    blocks[...] = pure.astype(BF16)
    rise[...] = jnp.zeros_like(rise)
    rise[rise.shape[0] - (TAPS - 1) :, :] = -ramp
    ahead = JITTER - (TAPS - 1)
    fall[0:ahead, :] = pure[L - ahead :]
    fall[ahead:JITTER, :] = pure[: TAPS - 1] - ramp
    fall[JITTER:, :] = jnp.zeros((fall.shape[0] - JITTER, LANES), F32)


def tables(whitening):
    vmem = pl.BlockSpec(memory_space=pltpu.VMEM)
    return pl.pallas_call(
        tables_kernel,
        out_shape=(
            jax.ShapeDtypeStruct((L, LANES), BF16),
            jax.ShapeDtypeStruct((EDGE, LANES), F32),
            jax.ShapeDtypeStruct((2 * JITTER, LANES), F32),
        ),
        in_specs=[pl.BlockSpec(memory_space=pltpu.SMEM), vmem],
        out_specs=(vmem, vmem, vmem),
        scratch_shapes=[pltpu.VMEM((2 * TAPS + 6, LANES), F32)],
        compiler_params=pltpu.CompilerParams(vmem_limit_bytes=16 * MIB),
        name="tables",
    )(whitening, phase_table())


def border_kernel(inbox, record, blocks, rise, fall, parts, collected):
    channels = record.shape[0]
    head = inbox[0:16, :].astype(F32)[:1]
    lane = lax.broadcasted_iota(jnp.int32, (1, LANES), 1)

    def told(at):
        return jnp.sum(jnp.where(lane == at, head, 0.0)).astype(jnp.int32)

    before = jnp.zeros((channels, LANES), F32)
    for q in range(GROUP):
        offset = told(q)
        edges = edge_table(rise, fall, offset)
        if q == 0:
            part = matmul(record[:, 0:JITTER].astype(BF16), edges[RIM:])
        else:
            part = matmul(record[:, HOP * q - RIM : HOP * q + JITTER].astype(BF16), edges)
        place = HOP * q + offset - (TAPS - 1)
        part = (part + turn(before, place)) * told(GROUP + q).astype(F32)
        upright = across(part)
        for c in range(collected.shape[0]):
            piece = upright[:, 128 * c : 128 * c + 128]
            collected[c, pl.ds(q, BINS, stride=2 * GROUP), :] = piece[:BINS]
            collected[c, pl.ds(GROUP + q, BINS, stride=2 * GROUP), :] = piece[BINS:]
        if q < GROUP - 1:
            before = before + matmul(
                record[:, HOP * q : HOP * q + HOP].astype(BF16), blocks[HOP * q : HOP * q + HOP, :]
            )
    width = min(128, channels)
    for c in range(collected.shape[0]):
        block = collected[c].reshape(BINS, 2 * GROUP, 128).astype(BF16)
        parts[:, :, width * c : width * c + width] = block[:, :, :width]


def border_parts(record, inbox, blocks, rise, fall):
    channels = record.shape[0]
    vmem = pl.BlockSpec(memory_space=pltpu.VMEM)
    lead = L - HOP + JITTER
    return pl.pallas_call(
        border_kernel,
        grid=(1,),
        out_shape=jax.ShapeDtypeStruct((BINS, 2 * GROUP, channels), BF16),
        in_specs=[vmem, pl.BlockSpec((channels, lead), lambda i: (0, 0)), vmem, vmem, vmem],
        out_specs=vmem,
        scratch_shapes=[pltpu.VMEM((max(channels // 128, 1), 2 * GROUP * BINS, 128), F32)],
        compiler_params=pltpu.CompilerParams(vmem_limit_bytes=50 * MIB),
        cost_estimate=pl.CostEstimate(
            flops=2 * channels * LANES * 3072, bytes_accessed=4 * channels * lead, transcendentals=0
        ),
        name="border_parts",
    )(inbox, record, blocks, rise, fall)


def spectra_kernel(offsets, valid, record, rim, blocks, rise, fall, out, samples, later, collected, sems):
    channels, slab = record.shape
    steps = slab // L
    windows = out.shape[2]

    def fetch(s):
        return pltpu.make_async_copy(
            record.at[:, pl.ds(L * s, L)], samples.at[:, pl.ds(RIM + L * s, L)], sems.at[s]
        )

    for s in range(steps):
        fetch(s).start()
    samples[:, 0:RIM] = rim[...].astype(F32)
    samples[:, RIM + slab :] = jnp.zeros((channels, samples.shape[1] - RIM - slab), F32)

    def block_sums(s):
        found = []
        for i in range(GROUP):
            begin = pl.multiple_of(RIM + L * s + HOP * i, 128)
            found.append(
                matmul(samples[:, pl.ds(begin, HOP)].astype(BF16), blocks[HOP * i : HOP * i + HOP, :])
            )
        return found

    def keep(found):
        total = found[GROUP - 1]
        later[GROUP - 1] = total
        for q in range(GROUP - 2, -1, -1):
            total = total + found[q]
            later[q] = total

    def one_window(w, q, before):
        offset = offsets[w]
        begin = pl.multiple_of(HOP * w, 128)
        ends = samples[:, pl.ds(begin + L, EDGE)] - samples[:, pl.ds(begin, EDGE)]
        part = matmul(ends.astype(BF16), edge_table(rise, fall, offset))
        total = later[q] if before is None else later[q] + before
        part = (part + turn(total, HOP * q + offset - (TAPS - 1))) * valid[w].astype(F32)
        upright = across(part)
        for c in range(collected.shape[0]):
            collected[c, pl.ds(w, LANES, stride=windows), :] = upright[:, 128 * c : 128 * c + 128]

    fetch(0).wait()
    keep(block_sums(0))

    @pl.loop(0, steps - 1)
    def _(s):
        fetch(s + 1).wait()
        found = block_sums(s + 1)
        before = None
        for q in range(GROUP):
            one_window(GROUP * s + q, q, before)
            before = found[q] if before is None else before + found[q]
        keep(found)

    for q in range(GROUP):
        one_window(GROUP * (steps - 1) + q, q, None)

    width = min(128, channels)
    for c in range(collected.shape[0]):
        block = collected[c].reshape(LANES, windows, 128).astype(BF16)
        out[:, 0, :, width * c : width * c + width] = block[:BINS, :, :width]
        out[:, 1, :, width * c : width * c + width] = block[BINS:, :, :width]


def own_spectra(record, rim, offsets, valid, blocks, rise, fall):
    channels, slab = record.shape
    windows = offsets.shape[0]
    smem = pl.BlockSpec(memory_space=pltpu.SMEM)
    vmem = pl.BlockSpec(memory_space=pltpu.VMEM)
    return pl.pallas_call(
        spectra_kernel,
        out_shape=jax.ShapeDtypeStruct((BINS, 2, windows, channels), BF16),
        in_specs=[smem, smem, pl.BlockSpec(memory_space=pl.ANY), vmem, vmem, vmem, vmem],
        out_specs=vmem,
        scratch_shapes=[
            pltpu.VMEM((channels, RIM + slab + L - HOP + JITTER), F32),
            pltpu.VMEM((GROUP, channels, LANES), F32),
            pltpu.VMEM((max(channels // 128, 1), LANES * windows, 128), F32),
            pltpu.SemaphoreType.DMA((slab // L,)),
        ],
        compiler_params=pltpu.CompilerParams(vmem_limit_bytes=50 * MIB),
        cost_estimate=pl.CostEstimate(
            flops=2 * channels * LANES * 896 * windows, bytes_accessed=4 * channels * slab, transcendentals=0
        ),
        name="own_spectra",
    )(offsets, valid, record, rim, blocks, rise, fall)


def join_kernel(sizes, devices, me, own, parts, *outs):
    windows = own.shape[2]
    bins = sum(sizes)
    half = windows - 2 * GROUP
    for d in range(devices):
        group = me[0] ^ d
        part = parts[pl.ds(group * bins, bins)].astype(F32)
        row = lax.broadcasted_iota(jnp.int32, part.shape, 1)
        moved = jnp.concatenate([part[:, GROUP:], part[:, :GROUP]], axis=1)
        for ri, extra in enumerate((moved, part)):
            spectra = own[pl.ds(group * bins, bins), ri].astype(F32)
            upper = spectra[:, half:] + jnp.where(row >= GROUP, extra, 0.0)
            joined = jnp.concatenate([spectra[:, :half], upper], axis=1).astype(BF16)
            outs[d][:, ri] = joined[: sizes[0]]
            begin = sizes[0]
            for count, out in zip(sizes[1:], outs[devices:]):
                out[pl.ds(group, 1), :, ri] = joined[begin : begin + count][None]
                begin += count


def chunk_sizes(bins):
    count = min(3, bins)
    return [(bins + count - 1 - c) // count for c in range(count)]


def joined_chunks(own, parts, devices):
    _, _, windows, channels = own.shape
    sizes = chunk_sizes(BINS // devices)
    vmem = pl.BlockSpec(memory_space=pltpu.VMEM)
    shapes = [(sizes[0], 2, windows, channels)] * devices
    shapes += [(devices, count, 2, windows, channels) for count in sizes[1:]]
    outs = pl.pallas_call(
        functools.partial(join_kernel, sizes, devices),
        out_shape=tuple(jax.ShapeDtypeStruct(shape, BF16) for shape in shapes),
        in_specs=[pl.BlockSpec(memory_space=pltpu.SMEM), vmem, vmem],
        out_specs=(vmem,) * len(shapes),
        compiler_params=pltpu.CompilerParams(vmem_limit_bytes=16 * MIB),
        name="joined_chunks",
    )(lax.axis_index("tm").astype(jnp.int32).reshape(1), own, parts)
    return outs[:devices], outs[devices:]


def stack_kernel(*refs):
    for d, piece in enumerate(refs[:-1]):
        refs[-1][d] = piece[...]


def stacked_pieces(pieces):
    vmem = pl.BlockSpec(memory_space=pltpu.VMEM)
    return pl.pallas_call(
        stack_kernel,
        out_shape=jax.ShapeDtypeStruct((len(pieces),) + pieces[0].shape, BF16),
        in_specs=[vmem] * len(pieces),
        out_specs=vmem,
        compiler_params=pltpu.CompilerParams(vmem_limit_bytes=16 * MIB),
        name="stacked_pieces",
    )(*pieces)


def cross_kernel(scale, stacked, me, own, *rest):
    out, done = rest[-2:]
    done[...] = jnp.zeros_like(done)
    sources, _, _, windows, channels = own.shape
    depth = sources * 2 * windows
    straight = own[:, 0].reshape(depth, channels)
    turned = jnp.concatenate([own[:, 0, 1:], -own[:, 0, :1]], axis=1).reshape(depth, channels)
    left = jnp.concatenate([straight, turned], axis=1)
    blocks = rest[0].shape[0] if stacked else len(rest) - 2
    for n in range(blocks):
        if stacked:
            right, at = rest[0][n, :, 0], channels * n
        else:
            right = (own if n == 0 else rest[n - 1])[:, 0]
            at = pl.multiple_of(channels * (me[0] ^ n), 128)
        right = right.reshape(depth, channels)
        both = lax.dot_general(left, right, (((0,), (0,)), ((), ())), preferred_element_type=F32) * scale
        out[0, 0, :, pl.ds(at, channels)] = both[:channels].astype(BF16)
        out[0, 1, :, pl.ds(at, channels)] = both[channels:].astype(BF16)


def cross_products(own, others, result, begin, bins):
    sources, count, _, windows, channels = own.shape
    stacked = not isinstance(others, list)
    blocks = others.shape[0] if stacked else len(others) + 1
    shape = (bins, 2, channels, blocks * channels)
    spec = pl.BlockSpec((sources, 1, 2, windows, channels), lambda f: (0, f, 0, 0, 0))
    smem = pl.BlockSpec(memory_space=pltpu.SMEM)
    operands = [lax.axis_index("chan").astype(jnp.int32).reshape(1), own]
    in_specs = [smem, spec]
    if stacked:
        operands.append(others)
        in_specs.append(pl.BlockSpec((blocks, sources, 1, 2, windows, channels), lambda f: (0, 0, f, 0, 0, 0)))
    else:
        operands += others
        in_specs += [spec] * len(others)
    if result is None:
        result, aliases = operands[0], {}
    else:
        aliases = {len(operands): 0}
    operands.append(result)
    in_specs.append(pl.BlockSpec(memory_space=pl.ANY))
    flops = 2 * count * 2 * channels * blocks * channels * sources * 2 * windows
    return pl.pallas_call(
        functools.partial(cross_kernel, 1.0 / (sources * windows), stacked),
        grid=(count,),
        out_shape=(jax.ShapeDtypeStruct(shape, BF16), jax.ShapeDtypeStruct((8, 128), F32)),
        in_specs=in_specs,
        out_specs=(
            pl.BlockSpec((1,) + shape[1:], lambda f: (begin + f, 0, 0, 0)),
            pl.BlockSpec(memory_space=pltpu.VMEM),
        ),
        input_output_aliases=aliases,
        compiler_params=pltpu.CompilerParams(vmem_limit_bytes=36 * MIB),
        cost_estimate=pl.CostEstimate(
            flops=flops, bytes_accessed=2 * count * 2 * channels * blocks * channels, transcendentals=0
        ),
        name="cross_products",
    )(*operands)


def swapped(shard, axis, bit):
    devices = lax.axis_size(axis)
    return lax.ppermute(shard, axis, [(i, i ^ bit) for i in range(devices)])


def fan(shard, axis, bit):
    held = {0: shard}
    while bit:
        held.update({n | bit: swapped(block, axis, bit) for n, block in list(held.items())})
        bit //= 2
    return held


def after_kernel(shard, done, out):
    out[...] = shard[...]


def after(shard, done):
    if done is None:
        return shard
    vmem = pl.BlockSpec(memory_space=pltpu.VMEM)
    return pl.pallas_call(
        after_kernel,
        out_shape=jax.ShapeDtypeStruct(shard.shape, shard.dtype),
        in_specs=[vmem, vmem],
        out_specs=vmem,
        compiler_params=pltpu.CompilerParams(vmem_limit_bytes=8 * MIB),
        name="after",
    )(shard, done)


def per_device(record, whitening, offsets, window_valid):
    devices = lax.axis_size("tm")
    blocks = lax.axis_size("chan")
    stacked = blocks & (blocks - 1) != 0 or record.shape[0] % 128 != 0
    top = blocks // 2
    inbox = from_behind(outbox(record, offsets, window_valid), "tm", 1)
    transform, rise, fall = tables(whitening)
    parts = from_behind(border_parts(record, inbox, transform, rise, fall), "tm", -1)
    own = own_spectra(record, inbox, offsets, window_valid, transform, rise, fall)
    pieces, chunks = joined_chunks(own, parts, devices)
    bins = BINS // devices
    sizes = chunk_sizes(bins)
    pieces = [pieces[0]] + [swapped(pieces[d], "tm", d) for d in range(1, devices)]
    held, result, done = [], None, None
    for p in range(len(sizes) + 1):
        if p < len(sizes):
            if p == 0:
                mine = stacked_pieces(pieces)
            else:
                mine = lax.all_to_all(chunks[p - 1], "tm", split_axis=0, concat_axis=0, tiled=True)
            mine = after(mine, done)
            if stacked:
                held.append((mine, lax.all_gather(mine, "chan", axis=0, tiled=False)))
            else:
                held.append((fan(mine, "chan", top // 2), swapped(mine, "chan", top)))
        if p:
            if stacked:
                mine, others = held[p - 1]
            else:
                near, far = held[p - 1]
                if p == len(sizes):
                    far = after(far, done)
                found = near | {n | top: block for n, block in fan(far, "chan", top // 2).items()}
                mine, others = found[0], [found[n] for n in range(1, blocks)]
            result, done = cross_products(mine, others, result, sum(sizes[: p - 1]), bins)
    return result


def solution(mesh):
    in_specs = (P("chan", "tm"), P(), P("tm"), P("tm"))
    out_specs = P("tm", None, "chan", None)
    return jax.shard_map(
        per_device, mesh=mesh, in_specs=in_specs, out_specs=out_specs, check_vma=False
    )
```

```python
import functools
import math

import jax
import jax.numpy as jnp
import numpy as np
from jax import lax
from jax.experimental import pallas as pl
from jax.experimental.pallas import tpu as pltpu
from jax.sharding import PartitionSpec as P

L = 2048
HOP = 512
JITTER = 256
TAPS = 65
BINS = 64
K0 = 64
RIM = 128
GROUP = L // HOP
EDGE = RIM + JITTER
LANES = 2 * BINS
MIB = 1 << 20
F32 = jnp.float32
BF16 = jnp.bfloat16


def from_behind(shard, axis, by):
    devices = lax.axis_size(axis)
    pairs = [(i, i + by) for i in range(devices) if 0 <= i + by < devices]
    return lax.ppermute(shard, axis, pairs)


def phase_table():
    sample = np.arange(L) - (TAPS - 1)
    angles = 2.0 * np.pi * np.mod(sample[:, None] * (K0 + np.arange(BINS))[None, :], L) / L
    return (np.concatenate([np.cos(angles), -np.sin(angles)], axis=1) / math.sqrt(L)).astype(np.float32)


def matmul(a, b):
    return jnp.dot(a, b, preferred_element_type=F32)


def turn(values, place):
    lane = lax.broadcasted_iota(jnp.int32, (8, LANES), 1)
    bins = K0 + (lane & (BINS - 1))
    angles = ((bins * (place + L)) & (L - 1)).astype(F32) * (2.0 * math.pi / L)
    sine = jnp.sin(angles)
    sine = jnp.where(lane < BINS, -sine, sine)
    return values * jnp.cos(angles)[:1] + pltpu.roll(values, BINS, 1) * sine[:1]


def edge_table(rise, fall, offset):
    start = JITTER - offset
    return jnp.concatenate([rise[pl.ds(start, RIM), :], fall[pl.ds(start, JITTER), :]], axis=0).astype(BF16)


def across(values):
    channels = values.shape[0]
    if channels % 128:
        values = jnp.pad(values, ((0, 128 - channels), (0, 0)))
    return values.T


def outbox_kernel(offsets, valid, record, out):
    top = record[0:8, :]
    row = lax.broadcasted_iota(jnp.int32, top.shape, 0)
    lane = lax.broadcasted_iota(jnp.int32, top.shape, 1)
    first = offsets.shape[0] - GROUP
    for q in range(GROUP):
        top = jnp.where((row == 0) & (lane == q), offsets[first + q].astype(F32), top)
        top = jnp.where((row == 0) & (lane == GROUP + q), valid[first + q].astype(F32), top)
    out[...] = jnp.concatenate([top, record[8:, :]], axis=0).astype(BF16)


def outbox(record, offsets, valid):
    channels, slab = record.shape
    smem = pl.BlockSpec(memory_space=pltpu.SMEM)
    return pl.pallas_call(
        outbox_kernel,
        grid=(1,),
        out_shape=jax.ShapeDtypeStruct((channels, RIM), BF16),
        in_specs=[smem, smem, pl.BlockSpec((channels, RIM), lambda i: (0, slab // RIM - 1))],
        out_specs=pl.BlockSpec(memory_space=pltpu.VMEM),
        compiler_params=pltpu.CompilerParams(vmem_limit_bytes=60 * MIB),
        name="outbox",
    )(offsets, valid, record)


def tables_kernel(taps, table, blocks, rise, fall, padded):
    padded[0 : TAPS - 1, :] = jnp.zeros((TAPS - 1, LANES), F32)
    padded[TAPS - 1 :, :] = table[TAPS - 1 : TAPS - 1 + padded.shape[0] - (TAPS - 1), :]
    ramp = jnp.zeros((TAPS - 1, LANES), F32)
    gain = jnp.zeros((1, LANES), F32)
    for m in range(TAPS):
        tap = taps[m]
        ramp = ramp + tap * padded[m : m + TAPS - 1, :]
        gain = gain + tap * padded[TAPS - 1 + m : TAPS + m, :]
    gain = jnp.broadcast_to(gain * math.sqrt(L), (8, LANES))
    lane = lax.broadcasted_iota(jnp.int32, (8, LANES), 1)
    swapped = pltpu.roll(gain, BINS, 1)
    gain_re = jnp.where(lane < BINS, gain, swapped)[:1]
    gain_im = jnp.where(lane < BINS, -swapped, gain)[:1]
    columns = table[...]
    pure = columns * gain_re + pltpu.roll(columns, BINS, 1) * gain_im
    blocks[...] = pure.astype(BF16)
    rise[...] = jnp.zeros_like(rise)
    rise[rise.shape[0] - (TAPS - 1) :, :] = -ramp
    ahead = JITTER - (TAPS - 1)
    fall[0:ahead, :] = pure[L - ahead :]
    fall[ahead:JITTER, :] = pure[: TAPS - 1] - ramp
    fall[JITTER:, :] = jnp.zeros((fall.shape[0] - JITTER, LANES), F32)


def tables(whitening):
    vmem = pl.BlockSpec(memory_space=pltpu.VMEM)
    return pl.pallas_call(
        tables_kernel,
        out_shape=(
            jax.ShapeDtypeStruct((L, LANES), BF16),
            jax.ShapeDtypeStruct((EDGE, LANES), F32),
            jax.ShapeDtypeStruct((2 * JITTER, LANES), F32),
        ),
        in_specs=[pl.BlockSpec(memory_space=pltpu.SMEM), vmem],
        out_specs=(vmem, vmem, vmem),
        scratch_shapes=[pltpu.VMEM((2 * TAPS + 6, LANES), F32)],
        compiler_params=pltpu.CompilerParams(vmem_limit_bytes=16 * MIB),
        name="tables",
    )(whitening, phase_table())


def border_kernel(inbox, record, blocks, rise, fall, done, parts, collected):
    channels = record.shape[0]
    head = inbox[0:16, :].astype(F32)[:1]
    lane = lax.broadcasted_iota(jnp.int32, (1, LANES), 1)

    def told(at):
        return jnp.sum(jnp.where(lane == at, head, 0.0)).astype(jnp.int32)

    before = jnp.zeros((channels, LANES), F32)
    for q in range(GROUP):
        offset = told(q)
        edges = edge_table(rise, fall, offset)
        if q == 0:
            part = matmul(record[:, 0:JITTER].astype(BF16), edges[RIM:])
        else:
            part = matmul(record[:, HOP * q - RIM : HOP * q + JITTER].astype(BF16), edges)
        place = HOP * q + offset - (TAPS - 1)
        part = (part + turn(before, place)) * told(GROUP + q).astype(F32)
        upright = across(part)
        for c in range(collected.shape[0]):
            piece = upright[:, 128 * c : 128 * c + 128]
            collected[c, pl.ds(q, BINS, stride=2 * GROUP), :] = piece[:BINS]
            collected[c, pl.ds(GROUP + q, BINS, stride=2 * GROUP), :] = piece[BINS:]
        if q < GROUP - 1:
            before = before + matmul(
                record[:, HOP * q : HOP * q + HOP].astype(BF16), blocks[HOP * q : HOP * q + HOP, :]
            )
    width = min(128, channels)
    for c in range(collected.shape[0]):
        block = collected[c].reshape(BINS, 2 * GROUP, 128).astype(BF16)
        parts[:, :, width * c : width * c + width] = block[:, :, :width]


def border_parts(record, inbox, blocks, rise, fall, done):
    channels = record.shape[0]
    vmem = pl.BlockSpec(memory_space=pltpu.VMEM)
    lead = L - HOP + JITTER
    return pl.pallas_call(
        border_kernel,
        grid=(1,),
        out_shape=jax.ShapeDtypeStruct((BINS, 2 * GROUP, channels), BF16),
        in_specs=[vmem, pl.BlockSpec((channels, lead), lambda i: (0, 0)), vmem, vmem, vmem, vmem],
        out_specs=vmem,
        scratch_shapes=[pltpu.VMEM((max(channels // 128, 1), 2 * GROUP * BINS, 128), F32)],
        compiler_params=pltpu.CompilerParams(vmem_limit_bytes=50 * MIB),
        cost_estimate=pl.CostEstimate(
            flops=2 * channels * LANES * 3072, bytes_accessed=4 * channels * lead, transcendentals=0
        ),
        name="border_parts",
    )(inbox, record, blocks, rise, fall, done)


def spectra_kernel(first, span, offsets, valid, record, rim, blocks, rise, fall, out, done, samples, later, collected, sems):
    channels, slab = record.shape
    windows = GROUP * span
    tail = L - HOP + JITTER
    end = RIM + L * span
    base = L * first
    if first == 0:
        fetches = [(base + L * s, RIM + L * s, L) for s in range(span)]
        samples[:, 0:RIM] = rim[...].astype(F32)
    else:
        fetches = [(base - RIM, 0, RIM + L)] + [(base + L * s, RIM + L * s, L) for s in range(1, span)]
    more = base + L * span < slab
    if more:
        fetches.append((base + L * span, end, tail))
    else:
        samples[:, end:] = jnp.zeros((channels, tail), F32)
    copies = [
        pltpu.make_async_copy(record.at[:, pl.ds(src, size)], samples.at[:, pl.ds(dst, size)], sems.at[i])
        for i, (src, dst, size) in enumerate(fetches)
    ]
    for copy in copies:
        copy.start()
    done[...] = jnp.zeros_like(done)

    def block_sums(s):
        return [
            matmul(
                samples[:, RIM + L * s + HOP * i : RIM + L * s + HOP * i + HOP].astype(BF16),
                blocks[HOP * i : HOP * i + HOP, :],
            )
            for i in range(GROUP if s < span else GROUP - 1)
        ]

    def keep(found):
        total = found[GROUP - 1]
        later[GROUP - 1] = total
        for q in range(GROUP - 2, -1, -1):
            total = total + found[q]
            later[q] = total

    copies[0].wait()
    keep(block_sums(0))
    for s in range(span):
        if s + 1 < len(copies):
            copies[s + 1].wait()
        found = block_sums(s + 1) if s + 1 < span or more else []
        before = None
        for q in range(GROUP):
            w = GROUP * s + q
            offset = offsets[GROUP * first + w]
            begin = HOP * w
            ends = samples[:, begin + L : begin + L + EDGE] - samples[:, begin : begin + EDGE]
            part = matmul(ends.astype(BF16), edge_table(rise, fall, offset))
            total = later[q] if before is None else later[q] + before
            part = (part + turn(total, HOP * q + offset - (TAPS - 1))) * valid[GROUP * first + w].astype(F32)
            upright = across(part)
            for c in range(collected.shape[0]):
                piece = upright[:, 128 * c : 128 * c + 128]
                collected[c, pl.ds(w, BINS, stride=2 * windows), :] = piece[:BINS]
                collected[c, pl.ds(windows + w, BINS, stride=2 * windows), :] = piece[BINS:]
            if found and q < GROUP - 1:
                before = found[q] if before is None else before + found[q]
        if s + 1 < span:
            keep(found)

    width = min(128, channels)
    for c in range(collected.shape[0]):
        block = collected[c].reshape(BINS, 2 * windows, 128).astype(BF16)
        out[:, :, width * c : width * c + width] = block[:, :, :width]


def own_spectra(record, rim, offsets, valid, transform, rise, fall, half):
    channels, slab = record.shape
    span = slab // L // 2
    windows = GROUP * span
    smem = pl.BlockSpec(memory_space=pltpu.SMEM)
    vmem = pl.BlockSpec(memory_space=pltpu.VMEM)
    return pl.pallas_call(
        functools.partial(spectra_kernel, span * half, span),
        out_shape=(
            jax.ShapeDtypeStruct((BINS, 2 * windows, channels), BF16),
            jax.ShapeDtypeStruct((8, 128), F32),
        ),
        in_specs=[smem, smem, pl.BlockSpec(memory_space=pl.ANY), vmem, vmem, vmem, vmem],
        out_specs=(vmem, vmem),
        scratch_shapes=[
            pltpu.VMEM((channels, RIM + L * span + L - HOP + JITTER), F32),
            pltpu.VMEM((GROUP, channels, LANES), F32),
            pltpu.VMEM((max(channels // 128, 1), LANES * windows, 128), F32),
            pltpu.SemaphoreType.DMA((span + 1,)),
        ],
        compiler_params=pltpu.CompilerParams(vmem_limit_bytes=50 * MIB),
        cost_estimate=pl.CostEstimate(
            flops=2 * channels * LANES * 896 * windows, bytes_accessed=2 * channels * slab, transcendentals=0
        ),
        name=f"own_spectra_{half}",
    )(offsets, valid, record, rim, transform, rise, fall)


def join_kernel(sizes, own, parts, *chunks):
    bins = sum(sizes)
    rows = own.shape[1] // 2
    for group in range(chunks[0].shape[0]):
        part = parts[group * bins : group * bins + bins].astype(F32)
        row = lax.broadcasted_iota(jnp.int32, part.shape, 1)
        moved = jnp.concatenate([part[:, GROUP:], part[:, :GROUP]], axis=1)
        spectra = own[group * bins : group * bins + bins].astype(F32)
        late = [jnp.where(row >= GROUP, extra, 0.0) for extra in (moved, part)]
        cut = rows - 2 * GROUP
        joined = jnp.concatenate(
            [piece for ri in range(2) for piece in (spectra[:, rows * ri : rows * ri + cut], spectra[:, rows * ri + cut : rows * ri + rows] + late[ri]) if piece.shape[1]],
            axis=1,
        ).astype(BF16)
        begin = 0
        for count, chunk in zip(sizes, chunks):
            chunk[group] = joined[begin : begin + count]
            begin += count


def chunk_sizes(bins):
    return [(bins + 1) // 2, bins // 2]


def joined_chunks(own, parts, devices):
    _, rows, channels = own.shape
    sizes = chunk_sizes(BINS // devices)
    vmem = pl.BlockSpec(memory_space=pltpu.VMEM)
    shapes = [(devices, count, rows, channels) for count in sizes]
    return pl.pallas_call(
        functools.partial(join_kernel, sizes),
        out_shape=tuple(jax.ShapeDtypeStruct(shape, BF16) for shape in shapes),
        in_specs=[vmem, vmem],
        out_specs=(vmem,) * len(shapes),
        compiler_params=pltpu.CompilerParams(vmem_limit_bytes=16 * MIB),
        name="joined_chunks",
    )(own, parts)


def cross_kernel(scale, stacked, me, *rest):
    out, done, left = rest[-3:]
    done[...] = jnp.zeros_like(done)
    early, late = rest[0], rest[1]
    sources, _, rows, channels = early.shape
    depth = sources * rows
    half = rows // 2
    for i, own in enumerate((early, late)):
        straight = own[:, 0].astype(F32)
        turned = jnp.concatenate([straight[:, half:], -straight[:, :half]], axis=1)
        for j, side in enumerate((straight, turned)):
            left[channels * j : channels * j + channels, depth * i : depth * i + depth] = side.reshape(depth, channels).T.astype(BF16)
    blocks = rest[2].shape[0] if stacked else (len(rest) - 4) // 2
    tile = min(256, channels)
    for n in range(blocks):
        if stacked:
            pair = [rest[2][n], rest[3][n]]
            at = channels * n
        else:
            pair = [rest[2 * n][...], rest[2 * n + 1][...]]
            at = pl.multiple_of(channels * (me[0] ^ n), 128)
        right = jnp.concatenate([one[:, 0].reshape(depth, channels) for one in pair], axis=0)
        for j in range(0, channels, tile):
            for r in range(0, 2 * channels, tile):
                both = matmul(left[r : r + tile, :], right[:, j : j + tile]) * scale
                out[0, r // channels, r % channels : r % channels + tile, pl.ds(at + j, tile)] = both.astype(BF16)


def cross_products(early, late, result, begin, bins):
    sources, count, rows, channels = late[0].shape
    stacked = not isinstance(late[1], list)
    blocks = late[1].shape[0] if stacked else len(late[1]) + 1
    shape = (bins, 2, channels, blocks * channels)
    specs = [
        pl.BlockSpec((sources, 1, rows, channels), lambda f: (0, begin + f, 0, 0)),
        pl.BlockSpec((sources, 1, rows, channels), lambda f: (0, f, 0, 0)),
    ]
    operands = [lax.axis_index("chan").astype(jnp.int32).reshape(1), early[0], late[0]]
    in_specs = [pl.BlockSpec(memory_space=pltpu.SMEM)] + specs
    if stacked:
        operands += [early[1], late[1]]
        in_specs += [
            pl.BlockSpec((blocks, sources, 1, rows, channels), lambda f: (0, 0, begin + f, 0, 0)),
            pl.BlockSpec((blocks, sources, 1, rows, channels), lambda f: (0, 0, f, 0, 0)),
        ]
    else:
        for pair in zip(early[1], late[1]):
            operands += pair
            in_specs += specs
    if result is None:
        result, aliases = operands[0], {}
    else:
        aliases = {len(operands): 0}
    operands.append(result)
    in_specs.append(pl.BlockSpec(memory_space=pl.ANY))
    depth = 2 * sources * rows
    return pl.pallas_call(
        functools.partial(cross_kernel, 2.0 / depth, stacked),
        grid=(count,),
        out_shape=(jax.ShapeDtypeStruct(shape, BF16), jax.ShapeDtypeStruct((8, 128), F32)),
        in_specs=in_specs,
        out_specs=(
            pl.BlockSpec((1,) + shape[1:], lambda f: (begin + f, 0, 0, 0)),
            pl.BlockSpec(memory_space=pltpu.VMEM),
        ),
        scratch_shapes=[pltpu.VMEM((2 * channels, depth), BF16)],
        input_output_aliases=aliases,
        compiler_params=pltpu.CompilerParams(vmem_limit_bytes=36 * MIB),
        cost_estimate=pl.CostEstimate(
            flops=4 * count * channels * blocks * channels * depth,
            bytes_accessed=4 * count * channels * blocks * channels,
            transcendentals=0,
        ),
        name="cross_products",
    )(*operands)


def swapped(shard, axis, bit):
    devices = lax.axis_size(axis)
    return lax.ppermute(shard, axis, [(i, i ^ bit) for i in range(devices)])


def fan(shard, axis, bit):
    held = {0: shard}
    while bit:
        held.update({n | bit: swapped(block, axis, bit) for n, block in list(held.items())})
        bit //= 2
    return held


def after_kernel(shard, done, out):
    out[...] = shard[...]


def after(shard, done):
    if done is None:
        return shard
    vmem = pl.BlockSpec(memory_space=pltpu.VMEM)
    return pl.pallas_call(
        after_kernel,
        out_shape=jax.ShapeDtypeStruct(shard.shape, shard.dtype),
        in_specs=[vmem, vmem],
        out_specs=vmem,
        compiler_params=pltpu.CompilerParams(vmem_limit_bytes=8 * MIB),
        name="after",
    )(shard, done)


def per_device(record, whitening, offsets, window_valid):
    devices = lax.axis_size("tm")
    blocks = lax.axis_size("chan")
    stacked = blocks & (blocks - 1) != 0 or record.shape[0] % 128 != 0
    top = blocks // 2
    bins = BINS // devices

    def exchanged(chunk):
        return lax.all_to_all(chunk, "tm", split_axis=0, concat_axis=0, tiled=True)

    def spread(mine, ready, done):
        if stacked:
            return mine, lax.all_gather(mine, "chan", axis=0, tiled=False)
        near = fan(mine, "chan", top // 2)
        far = after(swapped(mine, "chan", top), ready if done is None else done)
        found = near | {n | top: block for n, block in fan(far, "chan", top // 2).items()}
        return mine, [found[n] for n in range(1, blocks)]

    inbox = from_behind(outbox(record, offsets, window_valid), "tm", 1)
    transform, rise, fall = tables(whitening)
    early, done = own_spectra(record, inbox, offsets, window_valid, transform, rise, fall, 0)
    parts = from_behind(border_parts(record, inbox, transform, rise, fall, done), "tm", -1)
    late, _ = own_spectra(record, inbox, offsets, window_valid, transform, rise, fall, 1)
    sizes = chunk_sizes(bins)
    early = exchanged(early.reshape((devices, bins) + early.shape[1:]))
    late = [exchanged(chunk) for chunk in joined_chunks(late, parts, devices)]
    early = spread(early, late[0], None)
    result, done, begin = None, None, 0
    for p, mine in enumerate(late):
        result, done = cross_products(early, spread(mine, None, done), result, begin, bins)
        begin += sizes[p]
    return result


def solution(mesh):
    in_specs = (P("chan", "tm"), P(), P("tm"), P("tm"))
    out_specs = P("tm", None, "chan", None)
    return jax.shard_map(
        per_device, mesh=mesh, in_specs=in_specs, out_specs=out_specs, check_vma=False
    )
```

```python
import functools
import math

import jax
import jax.numpy as jnp
import numpy as np
from jax import lax
from jax.experimental import pallas as pl
from jax.experimental.pallas import tpu as pltpu
from jax.sharding import PartitionSpec as P

L = 2048
HOP = 512
JITTER = 256
TAPS = 65
BINS = 64
K0 = 64
RIM = 128
GROUP = L // HOP
EDGE = RIM + JITTER
LANES = 2 * BINS
MIB = 1 << 20
F32 = jnp.float32
BF16 = jnp.bfloat16


def from_behind(shard, axis, by):
    devices = lax.axis_size(axis)
    pairs = [(i, i + by) for i in range(devices) if 0 <= i + by < devices]
    return lax.ppermute(shard, axis, pairs)


def phase_table():
    sample = np.arange(L) - (TAPS - 1)
    angles = 2.0 * np.pi * np.mod(sample[:, None] * (K0 + np.arange(BINS))[None, :], L) / L
    return (np.concatenate([np.cos(angles), -np.sin(angles)], axis=1) / math.sqrt(L)).astype(np.float32)


def matmul(a, b):
    return jnp.dot(a, b, preferred_element_type=F32)


def turn(values, place):
    lane = lax.broadcasted_iota(jnp.int32, (8, LANES), 1)
    bins = K0 + (lane & (BINS - 1))
    angles = ((bins * (place + L)) & (L - 1)).astype(F32) * (2.0 * math.pi / L)
    sine = jnp.sin(angles)
    sine = jnp.where(lane < BINS, -sine, sine)
    return values * jnp.cos(angles)[:1] + pltpu.roll(values, BINS, 1) * sine[:1]


def edge_table(rise, fall, offset):
    start = JITTER - offset
    return jnp.concatenate([rise[pl.ds(start, RIM), :], fall[pl.ds(start, JITTER), :]], axis=0).astype(BF16)


def across(values):
    channels = values.shape[0]
    if channels % 128:
        values = jnp.pad(values, ((0, 128 - channels), (0, 0)))
    return values.T


def outbox_kernel(offsets, valid, record, out):
    top = record[0:8, :]
    row = lax.broadcasted_iota(jnp.int32, top.shape, 0)
    lane = lax.broadcasted_iota(jnp.int32, top.shape, 1)
    first = offsets.shape[0] - GROUP
    for q in range(GROUP):
        top = jnp.where((row == 0) & (lane == q), offsets[first + q].astype(F32), top)
        top = jnp.where((row == 0) & (lane == GROUP + q), valid[first + q].astype(F32), top)
    out[...] = jnp.concatenate([top, record[8:, :]], axis=0).astype(BF16)


def outbox(record, offsets, valid):
    channels, slab = record.shape
    smem = pl.BlockSpec(memory_space=pltpu.SMEM)
    return pl.pallas_call(
        outbox_kernel,
        grid=(1,),
        out_shape=jax.ShapeDtypeStruct((channels, RIM), BF16),
        in_specs=[smem, smem, pl.BlockSpec((channels, RIM), lambda i: (0, slab // RIM - 1))],
        out_specs=pl.BlockSpec(memory_space=pltpu.VMEM),
        compiler_params=pltpu.CompilerParams(vmem_limit_bytes=60 * MIB),
        name="outbox",
    )(offsets, valid, record)


def tables_kernel(taps, table, blocks, rise, fall, padded):
    padded[0 : TAPS - 1, :] = jnp.zeros((TAPS - 1, LANES), F32)
    padded[TAPS - 1 :, :] = table[TAPS - 1 : TAPS - 1 + padded.shape[0] - (TAPS - 1), :]
    ramp = jnp.zeros((TAPS - 1, LANES), F32)
    gain = jnp.zeros((1, LANES), F32)
    for m in range(TAPS):
        tap = taps[m]
        ramp = ramp + tap * padded[m : m + TAPS - 1, :]
        gain = gain + tap * padded[TAPS - 1 + m : TAPS + m, :]
    gain = jnp.broadcast_to(gain * math.sqrt(L), (8, LANES))
    lane = lax.broadcasted_iota(jnp.int32, (8, LANES), 1)
    swapped = pltpu.roll(gain, BINS, 1)
    gain_re = jnp.where(lane < BINS, gain, swapped)[:1]
    gain_im = jnp.where(lane < BINS, -swapped, gain)[:1]
    columns = table[...]
    pure = columns * gain_re + pltpu.roll(columns, BINS, 1) * gain_im
    blocks[...] = pure.astype(BF16)
    rise[...] = jnp.zeros_like(rise)
    rise[rise.shape[0] - (TAPS - 1) :, :] = -ramp
    ahead = JITTER - (TAPS - 1)
    fall[0:ahead, :] = pure[L - ahead :]
    fall[ahead:JITTER, :] = pure[: TAPS - 1] - ramp
    fall[JITTER:, :] = jnp.zeros((fall.shape[0] - JITTER, LANES), F32)


def tables(whitening):
    vmem = pl.BlockSpec(memory_space=pltpu.VMEM)
    return pl.pallas_call(
        tables_kernel,
        out_shape=(
            jax.ShapeDtypeStruct((L, LANES), BF16),
            jax.ShapeDtypeStruct((EDGE, LANES), F32),
            jax.ShapeDtypeStruct((2 * JITTER, LANES), F32),
        ),
        in_specs=[pl.BlockSpec(memory_space=pltpu.SMEM), vmem],
        out_specs=(vmem, vmem, vmem),
        scratch_shapes=[pltpu.VMEM((2 * TAPS + 6, LANES), F32)],
        compiler_params=pltpu.CompilerParams(vmem_limit_bytes=16 * MIB),
        name="tables",
    )(whitening, phase_table())


def border_kernel(inbox, record, blocks, rise, fall, parts, done, collected):
    channels = record.shape[0]
    done[...] = jnp.zeros_like(done)
    head = inbox[0:16, :].astype(F32)[:1]
    lane = lax.broadcasted_iota(jnp.int32, (1, LANES), 1)

    def told(at):
        return jnp.sum(jnp.where(lane == at, head, 0.0)).astype(jnp.int32)

    before = jnp.zeros((channels, LANES), F32)
    for q in range(GROUP):
        offset = told(q)
        edges = edge_table(rise, fall, offset)
        if q == 0:
            part = matmul(record[:, 0:JITTER].astype(BF16), edges[RIM:])
        else:
            part = matmul(record[:, HOP * q - RIM : HOP * q + JITTER].astype(BF16), edges)
        place = HOP * q + offset - (TAPS - 1)
        part = (part + turn(before, place)) * told(GROUP + q).astype(F32)
        upright = across(part)
        for c in range(collected.shape[0]):
            piece = upright[:, 128 * c : 128 * c + 128]
            collected[c, pl.ds(q, BINS, stride=2 * GROUP), :] = piece[:BINS]
            collected[c, pl.ds(GROUP + q, BINS, stride=2 * GROUP), :] = piece[BINS:]
        if q < GROUP - 1:
            before = before + matmul(
                record[:, HOP * q : HOP * q + HOP].astype(BF16), blocks[HOP * q : HOP * q + HOP, :]
            )
    width = min(128, channels)
    for c in range(collected.shape[0]):
        block = collected[c].reshape(BINS, 2 * GROUP, 128).astype(BF16)
        parts[:, :, width * c : width * c + width] = block[:, :, :width]


def border_parts(record, inbox, blocks, rise, fall):
    channels = record.shape[0]
    vmem = pl.BlockSpec(memory_space=pltpu.VMEM)
    lead = L - HOP + JITTER
    return pl.pallas_call(
        border_kernel,
        grid=(1,),
        out_shape=(jax.ShapeDtypeStruct((BINS, 2 * GROUP, channels), BF16), jax.ShapeDtypeStruct((8, 128), F32)),
        in_specs=[vmem, pl.BlockSpec((channels, lead), lambda i: (0, 0)), vmem, vmem, vmem],
        out_specs=(vmem, vmem),
        scratch_shapes=[pltpu.VMEM((max(channels // 128, 1), 2 * GROUP * BINS, 128), F32)],
        compiler_params=pltpu.CompilerParams(vmem_limit_bytes=50 * MIB),
        cost_estimate=pl.CostEstimate(
            flops=2 * channels * LANES * 3072, bytes_accessed=4 * channels * lead, transcendentals=0
        ),
        name="border_parts",
    )(inbox, record, blocks, rise, fall)


def spectra_kernel(first, span, offsets, valid, record, rim, blocks, rise, fall, done, out, samples, later, collected, sems):
    channels, slab = record.shape
    windows = GROUP * span
    tail = L - HOP + JITTER
    end = RIM + L * span
    base = L * first
    fetches = [(base + HOP * i, RIM + HOP * i, HOP) for i in range(GROUP * span)]
    if first == 0:
        samples[:, 0:RIM] = rim[...].astype(F32)
    else:
        fetches[0] = (base - RIM, 0, RIM + HOP)
    more = base + L * span < slab
    if more:
        fetches += [(base + HOP * i, RIM + HOP * i, HOP) for i in range(GROUP * span, GROUP * (span + 1) - 1)]
        left = tail - HOP * (GROUP - 1)
        fetches.append((base + L * span + tail - left, end + tail - left, left))
    else:
        samples[:, end:] = jnp.zeros((channels, tail), F32)
    copies = [
        pltpu.make_async_copy(record.at[:, pl.ds(src, size)], samples.at[:, pl.ds(dst, size)], sems.at[i])
        for i, (src, dst, size) in enumerate(fetches)
    ]
    for copy in copies:
        copy.start()

    def arrived(i):
        if i < len(copies):
            copies[i].wait()

    def block_sums(s):
        found = []
        for i in range(GROUP if s < span else GROUP - 1):
            arrived(GROUP * s + i)
            found.append(
                matmul(
                    samples[:, RIM + L * s + HOP * i : RIM + L * s + HOP * i + HOP].astype(BF16),
                    blocks[HOP * i : HOP * i + HOP, :],
                )
            )
        return found

    def keep(found):
        total = found[GROUP - 1]
        later[GROUP - 1] = total
        for q in range(GROUP - 2, -1, -1):
            total = total + found[q]
            later[q] = total

    keep(block_sums(0))
    for s in range(span):
        found = block_sums(s + 1) if s + 1 < span or more else []
        if s + 1 == span and more:
            arrived(len(copies) - 1)
        before = None
        for q in range(GROUP):
            w = GROUP * s + q
            offset = offsets[GROUP * first + w]
            begin = HOP * w
            ends = samples[:, begin + L : begin + L + EDGE] - samples[:, begin : begin + EDGE]
            part = matmul(ends.astype(BF16), edge_table(rise, fall, offset))
            total = later[q] if before is None else later[q] + before
            part = (part + turn(total, HOP * q + offset - (TAPS - 1))) * valid[GROUP * first + w].astype(F32)
            upright = across(part)
            for c in range(collected.shape[0]):
                piece = upright[:, 128 * c : 128 * c + 128]
                collected[c, pl.ds(w, BINS, stride=2 * windows), :] = piece[:BINS]
                collected[c, pl.ds(windows + w, BINS, stride=2 * windows), :] = piece[BINS:]
            if found and q < GROUP - 1:
                before = found[q] if before is None else before + found[q]
        if s + 1 < span:
            keep(found)

    width = min(128, channels)
    for c in range(collected.shape[0]):
        block = collected[c].reshape(BINS, 2 * windows, 128).astype(BF16)
        out[:, :, width * c : width * c + width] = block[:, :, :width]


def own_spectra(record, rim, offsets, valid, transform, rise, fall, done, half):
    channels, slab = record.shape
    span = slab // L // 2
    windows = GROUP * span
    smem = pl.BlockSpec(memory_space=pltpu.SMEM)
    vmem = pl.BlockSpec(memory_space=pltpu.VMEM)
    return pl.pallas_call(
        functools.partial(spectra_kernel, span * half, span),
        out_shape=jax.ShapeDtypeStruct((BINS, 2 * windows, channels), BF16),
        in_specs=[smem, smem, pl.BlockSpec(memory_space=pl.ANY), vmem, vmem, vmem, vmem, vmem],
        out_specs=vmem,
        scratch_shapes=[
            pltpu.VMEM((channels, RIM + L * span + L - HOP + JITTER), F32),
            pltpu.VMEM((GROUP, channels, LANES), F32),
            pltpu.VMEM((max(channels // 128, 1), LANES * windows, 128), F32),
            pltpu.SemaphoreType.DMA((GROUP * (span + 1),)),
        ],
        compiler_params=pltpu.CompilerParams(vmem_limit_bytes=50 * MIB),
        cost_estimate=pl.CostEstimate(
            flops=2 * channels * LANES * 896 * windows, bytes_accessed=2 * channels * slab, transcendentals=0
        ),
        name=f"own_spectra_{half}",
    )(offsets, valid, record, rim, transform, rise, fall, done)


def join_kernel(sizes, own, parts, *chunks):
    *chunks, done = chunks
    done[...] = jnp.zeros_like(done)
    bins = sum(sizes)
    rows = own.shape[1] // 2
    for group in range(chunks[0].shape[0]):
        part = parts[group * bins : group * bins + bins].astype(F32)
        row = lax.broadcasted_iota(jnp.int32, part.shape, 1)
        moved = jnp.concatenate([part[:, GROUP:], part[:, :GROUP]], axis=1)
        spectra = own[group * bins : group * bins + bins].astype(F32)
        late = [jnp.where(row >= GROUP, extra, 0.0) for extra in (moved, part)]
        cut = rows - 2 * GROUP
        joined = jnp.concatenate(
            [piece for ri in range(2) for piece in (spectra[:, rows * ri : rows * ri + cut], spectra[:, rows * ri + cut : rows * ri + rows] + late[ri]) if piece.shape[1]],
            axis=1,
        ).astype(BF16)
        begin = 0
        for count, chunk in zip(sizes, chunks):
            chunk[group] = joined[begin : begin + count]
            begin += count


def chunk_sizes(bins):
    return [bins - 3 * bins // 8, 3 * bins // 8]


def joined_chunks(own, parts, devices):
    _, rows, channels = own.shape
    sizes = chunk_sizes(BINS // devices)
    vmem = pl.BlockSpec(memory_space=pltpu.VMEM)
    shapes = [(devices, count, rows, channels) for count in sizes]
    *chunks, done = pl.pallas_call(
        functools.partial(join_kernel, sizes),
        out_shape=tuple(jax.ShapeDtypeStruct(shape, BF16) for shape in shapes) + (jax.ShapeDtypeStruct((8, 128), F32),),
        in_specs=[vmem, vmem],
        out_specs=(vmem,) * (len(shapes) + 1),
        compiler_params=pltpu.CompilerParams(vmem_limit_bytes=16 * MIB),
        name="joined_chunks",
    )(own, parts)
    return chunks, done


def left_kernel(early, late, done, out, ready):
    ready[...] = jnp.zeros_like(ready)
    sources, _, rows, channels = early.shape
    depth = sources * rows
    half = rows // 2
    for i, own in enumerate((early, late)):
        straight = own[:, 0].astype(F32)
        turned = jnp.concatenate([straight[:, half:], -straight[:, :half]], axis=1)
        for j, side in enumerate((straight, turned)):
            out[0, channels * j : channels * j + channels, depth * i : depth * i + depth] = (
                side.reshape(depth, channels).T.astype(BF16)
            )


def left_sides(early, late, begin, done):
    sources, count, rows, channels = late.shape
    shape = (count, 2 * channels, 2 * sources * rows)
    vmem = pl.BlockSpec(memory_space=pltpu.VMEM)
    return pl.pallas_call(
        left_kernel,
        grid=(count,),
        out_shape=(jax.ShapeDtypeStruct(shape, BF16), jax.ShapeDtypeStruct((8, 128), F32)),
        in_specs=[
            pl.BlockSpec((sources, 1, rows, channels), lambda f: (0, begin + f, 0, 0)),
            pl.BlockSpec((sources, 1, rows, channels), lambda f: (0, f, 0, 0)),
            vmem,
        ],
        out_specs=(pl.BlockSpec((1,) + shape[1:], lambda f: (f, 0, 0)), vmem),
        compiler_params=pltpu.CompilerParams(vmem_limit_bytes=16 * MIB),
        name="left_sides",
    )(early, late, done)


def cross_kernel(scale, stacked, me, left, *rest):
    out, done = rest[-2:]
    done[...] = jnp.zeros_like(done)
    sources, _, rows, channels = rest[0].shape[-4:]
    depth = sources * rows
    blocks = rest[0].shape[0] if stacked else (len(rest) - 3) // 2
    tile = min(256, channels)
    for n in range(blocks):
        if stacked:
            pair = [rest[0][n], rest[1][n]]
            at = channels * n
        else:
            pair = [rest[2 * n][...], rest[2 * n + 1][...]]
            at = pl.multiple_of(channels * (me[0] ^ n), 128)
        right = jnp.concatenate([one[:, 0].reshape(depth, channels) for one in pair], axis=0)
        for j in range(0, channels, tile):
            for r in range(0, 2 * channels, tile):
                both = matmul(left[0, r : r + tile, :], right[:, j : j + tile]) * scale
                out[0, r // channels, r % channels : r % channels + tile, pl.ds(at + j, tile)] = both.astype(BF16)


def cross_products(left, early, late, result, begin, bins):
    sources, count, rows, channels = late[0].shape
    stacked = not isinstance(late[1], list)
    blocks = late[1].shape[0] if stacked else len(late[1]) + 1
    shape = (bins, 2, channels, blocks * channels)
    specs = [
        pl.BlockSpec((sources, 1, rows, channels), lambda f: (0, begin + f, 0, 0)),
        pl.BlockSpec((sources, 1, rows, channels), lambda f: (0, f, 0, 0)),
    ]
    operands = [lax.axis_index("chan").astype(jnp.int32).reshape(1), left]
    in_specs = [pl.BlockSpec(memory_space=pltpu.SMEM), pl.BlockSpec((1,) + left.shape[1:], lambda f: (f, 0, 0))]
    if stacked:
        operands += [early[1], late[1]]
        in_specs += [
            pl.BlockSpec((blocks, sources, 1, rows, channels), lambda f: (0, 0, begin + f, 0, 0)),
            pl.BlockSpec((blocks, sources, 1, rows, channels), lambda f: (0, 0, f, 0, 0)),
        ]
    else:
        for pair in zip([early[0]] + early[1], [late[0]] + late[1]):
            operands += pair
            in_specs += specs
    if result is None:
        result, aliases = operands[0], {}
    else:
        aliases = {len(operands): 0}
    operands.append(result)
    in_specs.append(pl.BlockSpec(memory_space=pl.ANY))
    depth = 2 * sources * rows
    return pl.pallas_call(
        functools.partial(cross_kernel, 2.0 / depth, stacked),
        grid=(count,),
        out_shape=(jax.ShapeDtypeStruct(shape, BF16), jax.ShapeDtypeStruct((8, 128), F32)),
        in_specs=in_specs,
        out_specs=(
            pl.BlockSpec((1,) + shape[1:], lambda f: (begin + f, 0, 0, 0)),
            pl.BlockSpec(memory_space=pltpu.VMEM),
        ),
        input_output_aliases=aliases,
        compiler_params=pltpu.CompilerParams(vmem_limit_bytes=36 * MIB),
        cost_estimate=pl.CostEstimate(
            flops=4 * count * channels * blocks * channels * depth,
            bytes_accessed=4 * count * channels * blocks * channels,
            transcendentals=0,
        ),
        name="cross_products",
    )(*operands)


def swapped(shard, axis, bit):
    devices = lax.axis_size(axis)
    return lax.ppermute(shard, axis, [(i, i ^ bit) for i in range(devices)])


def fan(shard, axis, bit):
    held = {0: shard}
    while bit:
        held.update({n | bit: swapped(block, axis, bit) for n, block in list(held.items())})
        bit //= 2
    return held


def after_kernel(shard, done, out):
    out[...] = shard[...]


def after(shard, done):
    if done is None:
        return shard
    vmem = pl.BlockSpec(memory_space=pltpu.VMEM)
    return pl.pallas_call(
        after_kernel,
        out_shape=jax.ShapeDtypeStruct(shard.shape, shard.dtype),
        in_specs=[vmem, vmem],
        out_specs=vmem,
        compiler_params=pltpu.CompilerParams(vmem_limit_bytes=8 * MIB),
        name="after",
    )(shard, done)


def per_device(record, whitening, offsets, window_valid):
    devices = lax.axis_size("tm")
    blocks = lax.axis_size("chan")
    stacked = blocks & (blocks - 1) != 0 or record.shape[0] % 128 != 0
    top = blocks // 2
    bins = BINS // devices

    def exchanged(chunk):
        return lax.all_to_all(chunk, "tm", split_axis=0, concat_axis=0, tiled=True)

    def spread(mine, ready):
        if stacked:
            return mine, lax.all_gather(mine, "chan", axis=0, tiled=False)
        near = fan(mine, "chan", top // 2)
        far = after(swapped(mine, "chan", top), ready)
        found = near | {n | top: block for n, block in fan(far, "chan", top // 2).items()}
        return mine, [found[n] for n in range(1, blocks)]

    inbox = from_behind(outbox(record, offsets, window_valid), "tm", 1)
    transform, rise, fall = tables(whitening)
    parts, done = border_parts(record, inbox, transform, rise, fall)
    parts = from_behind(parts, "tm", -1)
    early, late = (
        own_spectra(record, inbox, offsets, window_valid, transform, rise, fall, done, half) for half in range(2)
    )
    late, done = joined_chunks(late, parts, devices)
    early = after(exchanged(early.reshape((devices, bins) + early.shape[1:])), done)
    late = [exchanged(chunk) for chunk in late]
    early = spread(early, late[0])
    result, begin = None, 0
    for mine in late:
        left, done = left_sides(early[0], mine, begin, done)
        result, done = cross_products(left, early, spread(mine, done), result, begin, bins)
        begin += mine.shape[1]
    return result


def solution(mesh):
    in_specs = (P("chan", "tm"), P(), P("tm"), P("tm"))
    out_specs = P("tm", None, "chan", None)
    return jax.shard_map(
        per_device, mesh=mesh, in_specs=in_specs, out_specs=out_specs, check_vma=False
    )
```

```python
import functools
import math

import jax
import jax.numpy as jnp
import numpy as np
from jax import lax
from jax.experimental import pallas as pl
from jax.experimental.pallas import tpu as pltpu
from jax.sharding import PartitionSpec as P

L = 2048
HOP = 512
JITTER = 256
TAPS = 65
BINS = 64
K0 = 64
RIM = 128
GROUP = L // HOP
EDGE = RIM + JITTER
LANES = 2 * BINS
MIB = 1 << 20
F32 = jnp.float32
BF16 = jnp.bfloat16


def from_behind(shard, axis, by):
    devices = lax.axis_size(axis)
    pairs = [(i, i + by) for i in range(devices) if 0 <= i + by < devices]
    return lax.ppermute(shard, axis, pairs)


def phase_table():
    sample = np.arange(L) - (TAPS - 1)
    angles = 2.0 * np.pi * np.mod(sample[:, None] * (K0 + np.arange(BINS))[None, :], L) / L
    return (np.concatenate([np.cos(angles), -np.sin(angles)], axis=1) / math.sqrt(L)).astype(np.float32)


def matmul(a, b):
    return jnp.dot(a, b, preferred_element_type=F32)


def turn(values, place):
    lane = lax.broadcasted_iota(jnp.int32, (8, LANES), 1)
    bins = K0 + (lane & (BINS - 1))
    angles = ((bins * (place + L)) & (L - 1)).astype(F32) * (2.0 * math.pi / L)
    sine = jnp.sin(angles)
    sine = jnp.where(lane < BINS, -sine, sine)
    return values * jnp.cos(angles)[:1] + pltpu.roll(values, BINS, 1) * sine[:1]


def edge_table(rise, fall, offset):
    start = JITTER - offset
    return jnp.concatenate([rise[pl.ds(start, RIM), :], fall[pl.ds(start, JITTER), :]], axis=0).astype(BF16)


def across(values):
    channels = values.shape[0]
    if channels % 128:
        values = jnp.pad(values, ((0, 128 - channels), (0, 0)))
    return values.T


def outbox_kernel(offsets, valid, record, out):
    top = record[0:8, :]
    row = lax.broadcasted_iota(jnp.int32, top.shape, 0)
    lane = lax.broadcasted_iota(jnp.int32, top.shape, 1)
    first = offsets.shape[0] - GROUP
    for q in range(GROUP):
        top = jnp.where((row == 0) & (lane == q), offsets[first + q].astype(F32), top)
        top = jnp.where((row == 0) & (lane == GROUP + q), valid[first + q].astype(F32), top)
    out[...] = jnp.concatenate([top, record[8:, :]], axis=0).astype(BF16)


def outbox(record, offsets, valid):
    channels, slab = record.shape
    smem = pl.BlockSpec(memory_space=pltpu.SMEM)
    return pl.pallas_call(
        outbox_kernel,
        grid=(1,),
        out_shape=jax.ShapeDtypeStruct((channels, RIM), BF16),
        in_specs=[smem, smem, pl.BlockSpec((channels, RIM), lambda i: (0, slab // RIM - 1))],
        out_specs=pl.BlockSpec(memory_space=pltpu.VMEM),
        compiler_params=pltpu.CompilerParams(vmem_limit_bytes=60 * MIB),
        name="outbox",
    )(offsets, valid, record)


def tables_kernel(taps, table, blocks, rise, fall, padded):
    padded[0 : TAPS - 1, :] = jnp.zeros((TAPS - 1, LANES), F32)
    padded[TAPS - 1 :, :] = table[TAPS - 1 : TAPS - 1 + padded.shape[0] - (TAPS - 1), :]
    ramp = jnp.zeros((TAPS - 1, LANES), F32)
    gain = jnp.zeros((1, LANES), F32)
    for m in range(TAPS):
        tap = taps[m]
        ramp = ramp + tap * padded[m : m + TAPS - 1, :]
        gain = gain + tap * padded[TAPS - 1 + m : TAPS + m, :]
    gain = jnp.broadcast_to(gain * math.sqrt(L), (8, LANES))
    lane = lax.broadcasted_iota(jnp.int32, (8, LANES), 1)
    swapped = pltpu.roll(gain, BINS, 1)
    gain_re = jnp.where(lane < BINS, gain, swapped)[:1]
    gain_im = jnp.where(lane < BINS, -swapped, gain)[:1]
    columns = table[...]
    pure = columns * gain_re + pltpu.roll(columns, BINS, 1) * gain_im
    blocks[...] = pure.astype(BF16)
    rise[...] = jnp.zeros_like(rise)
    rise[rise.shape[0] - (TAPS - 1) :, :] = -ramp
    ahead = JITTER - (TAPS - 1)
    fall[0:ahead, :] = pure[L - ahead :]
    fall[ahead:JITTER, :] = pure[: TAPS - 1] - ramp
    fall[JITTER:, :] = jnp.zeros((fall.shape[0] - JITTER, LANES), F32)


def tables(whitening):
    vmem = pl.BlockSpec(memory_space=pltpu.VMEM)
    return pl.pallas_call(
        tables_kernel,
        out_shape=(
            jax.ShapeDtypeStruct((L, LANES), BF16),
            jax.ShapeDtypeStruct((EDGE, LANES), F32),
            jax.ShapeDtypeStruct((2 * JITTER, LANES), F32),
        ),
        in_specs=[pl.BlockSpec(memory_space=pltpu.SMEM), vmem],
        out_specs=(vmem, vmem, vmem),
        scratch_shapes=[pltpu.VMEM((2 * TAPS + 6, LANES), F32)],
        compiler_params=pltpu.CompilerParams(vmem_limit_bytes=16 * MIB),
        name="tables",
    )(whitening, phase_table())


def border_kernel(inbox, record, blocks, rise, fall, parts, done, collected):
    channels = record.shape[0]
    done[...] = jnp.zeros_like(done)
    head = inbox[0:16, :].astype(F32)[:1]
    lane = lax.broadcasted_iota(jnp.int32, (1, LANES), 1)

    def told(at):
        return jnp.sum(jnp.where(lane == at, head, 0.0)).astype(jnp.int32)

    before = jnp.zeros((channels, LANES), F32)
    for q in range(GROUP):
        offset = told(q)
        edges = edge_table(rise, fall, offset)
        if q == 0:
            part = matmul(record[:, 0:JITTER].astype(BF16), edges[RIM:])
        else:
            part = matmul(record[:, HOP * q - RIM : HOP * q + JITTER].astype(BF16), edges)
        place = HOP * q + offset - (TAPS - 1)
        part = (part + turn(before, place)) * told(GROUP + q).astype(F32)
        upright = across(part)
        for c in range(collected.shape[0]):
            piece = upright[:, 128 * c : 128 * c + 128]
            collected[c, pl.ds(q, BINS, stride=2 * GROUP), :] = piece[:BINS]
            collected[c, pl.ds(GROUP + q, BINS, stride=2 * GROUP), :] = piece[BINS:]
        if q < GROUP - 1:
            before = before + matmul(
                record[:, HOP * q : HOP * q + HOP].astype(BF16), blocks[HOP * q : HOP * q + HOP, :]
            )
    width = min(128, channels)
    for c in range(collected.shape[0]):
        block = collected[c].reshape(BINS, 2 * GROUP, 128).astype(BF16)
        parts[:, :, width * c : width * c + width] = block[:, :, :width]


def border_parts(record, inbox, blocks, rise, fall):
    channels = record.shape[0]
    vmem = pl.BlockSpec(memory_space=pltpu.VMEM)
    lead = L - HOP + JITTER
    return pl.pallas_call(
        border_kernel,
        grid=(1,),
        out_shape=(jax.ShapeDtypeStruct((BINS, 2 * GROUP, channels), BF16), jax.ShapeDtypeStruct((8, 128), F32)),
        in_specs=[vmem, pl.BlockSpec((channels, lead), lambda i: (0, 0)), vmem, vmem, vmem],
        out_specs=(vmem, vmem),
        scratch_shapes=[pltpu.VMEM((max(channels // 128, 1), 2 * GROUP * BINS, 128), F32)],
        compiler_params=pltpu.CompilerParams(vmem_limit_bytes=50 * MIB),
        cost_estimate=pl.CostEstimate(
            flops=2 * channels * LANES * 3072, bytes_accessed=4 * channels * lead, transcendentals=0
        ),
        name="border_parts",
    )(inbox, record, blocks, rise, fall)


def spectra_kernel(first, span, offsets, valid, record, rim, blocks, rise, fall, parts, *rest):
    *outs, done, samples, later, collected, sems = rest
    channels, slab = record.shape
    windows = GROUP * span
    tail = L - HOP + JITTER
    done[...] = jnp.zeros_like(done)
    end = RIM + L * span
    base = L * first
    fetches = [(base + HOP * i, RIM + HOP * i, HOP) for i in range(GROUP * span)]
    if first == 0:
        samples[:, 0:RIM] = rim[...].astype(F32)
    else:
        fetches[0] = (base - RIM, 0, RIM + HOP)
    more = base + L * span < slab
    if more:
        fetches += [(base + HOP * i, RIM + HOP * i, HOP) for i in range(GROUP * span, GROUP * (span + 1) - 1)]
        left = tail - HOP * (GROUP - 1)
        fetches.append((base + L * span + tail - left, end + tail - left, left))
    else:
        samples[:, end:] = jnp.zeros((channels, tail), F32)
    copies = [
        pltpu.make_async_copy(record.at[:, pl.ds(src, size)], samples.at[:, pl.ds(dst, size)], sems.at[i])
        for i, (src, dst, size) in enumerate(fetches)
    ]
    for copy in copies:
        copy.start()

    def arrived(i):
        if i < len(copies):
            copies[i].wait()

    def block_sums(s):
        found = []
        for i in range(GROUP if s < span else GROUP - 1):
            arrived(GROUP * s + i)
            found.append(
                matmul(
                    samples[:, RIM + L * s + HOP * i : RIM + L * s + HOP * i + HOP].astype(BF16),
                    blocks[HOP * i : HOP * i + HOP, :],
                )
            )
        return found

    def keep(found):
        total = found[GROUP - 1]
        later[GROUP - 1] = total
        for q in range(GROUP - 2, -1, -1):
            total = total + found[q]
            later[q] = total

    keep(block_sums(0))
    for s in range(span):
        found = block_sums(s + 1) if s + 1 < span or more else []
        if s + 1 == span and more:
            arrived(len(copies) - 1)
        before = None
        for q in range(GROUP):
            w = GROUP * s + q
            offset = offsets[GROUP * first + w]
            begin = HOP * w
            ends = samples[:, begin + L : begin + L + EDGE] - samples[:, begin : begin + EDGE]
            part = matmul(ends.astype(BF16), edge_table(rise, fall, offset))
            total = later[q] if before is None else later[q] + before
            part = (part + turn(total, HOP * q + offset - (TAPS - 1))) * valid[GROUP * first + w].astype(F32)
            upright = across(part)
            for c in range(collected.shape[0]):
                piece = upright[:, 128 * c : 128 * c + 128]
                collected[c, pl.ds(w, BINS, stride=2 * windows), :] = piece[:BINS]
                collected[c, pl.ds(windows + w, BINS, stride=2 * windows), :] = piece[BINS:]
            if found and q < GROUP - 1:
                before = found[q] if before is None else before + found[q]
        if s + 1 < span:
            keep(found)

    width = min(128, channels)
    for c in range(collected.shape[0]):
        lanes = slice(width * c, width * c + width)
        block = collected[c].reshape(BINS, 2 * windows, 128)[:, :, :width]
        if not more:
            block = with_parts(block, parts[:, :, lanes].astype(F32))
        block = block.astype(BF16)
        for group in range(outs[0].shape[0]):
            begin = group * BINS // outs[0].shape[0]
            for out in outs:
                out[group, :, :, lanes] = block[begin : begin + out.shape[1]]
                begin += out.shape[1]


def with_parts(block, part):
    windows = block.shape[1] // 2
    row = lax.broadcasted_iota(jnp.int32, part.shape, 1)
    moved = jnp.concatenate([part[:, GROUP:], part[:, :GROUP]], axis=1)
    pieces = []
    for ri, extra in enumerate((moved, part)):
        end = windows * ri + windows
        if windows > 2 * GROUP:
            pieces.append(block[:, windows * ri : end - 2 * GROUP])
        pieces.append(block[:, end - 2 * GROUP : end] + jnp.where(row >= GROUP, extra, 0.0))
    return jnp.concatenate(pieces, axis=1)


def chunk_sizes(bins):
    return [bins - 3 * bins // 8, 3 * bins // 8]


def own_spectra(record, rim, offsets, valid, transform, rise, fall, parts, devices, half):
    channels, slab = record.shape
    span = slab // L // 2
    windows = GROUP * span
    sizes = chunk_sizes(BINS // devices) if half else [BINS // devices]
    smem = pl.BlockSpec(memory_space=pltpu.SMEM)
    vmem = pl.BlockSpec(memory_space=pltpu.VMEM)
    *chunks, done = pl.pallas_call(
        functools.partial(spectra_kernel, span * half, span),
        out_shape=tuple(jax.ShapeDtypeStruct((devices, count, 2 * windows, channels), BF16) for count in sizes)
        + (jax.ShapeDtypeStruct((8, 128), F32),),
        in_specs=[smem, smem, pl.BlockSpec(memory_space=pl.ANY), vmem, vmem, vmem, vmem, vmem],
        out_specs=(vmem,) * (len(sizes) + 1),
        scratch_shapes=[
            pltpu.VMEM((channels, RIM + L * span + L - HOP + JITTER), F32),
            pltpu.VMEM((GROUP, channels, LANES), F32),
            pltpu.VMEM((max(channels // 128, 1), LANES * windows, 128), F32),
            pltpu.SemaphoreType.DMA((GROUP * (span + 1),)),
        ],
        compiler_params=pltpu.CompilerParams(vmem_limit_bytes=50 * MIB),
        cost_estimate=pl.CostEstimate(
            flops=2 * channels * LANES * 896 * windows, bytes_accessed=2 * channels * slab, transcendentals=0
        ),
        name=f"own_spectra_{half}",
    )(offsets, valid, record, rim, transform, rise, fall, parts)
    return chunks, done


def left_kernel(early, late, done, out, ready):
    ready[...] = jnp.zeros_like(ready)
    sources, _, rows, channels = early.shape
    depth = sources * rows
    half = rows // 2
    for i, own in enumerate((early, late)):
        straight = own[:, 0].astype(F32)
        turned = jnp.concatenate([straight[:, half:], -straight[:, :half]], axis=1)
        for j, side in enumerate((straight, turned)):
            out[0, channels * j : channels * j + channels, depth * i : depth * i + depth] = (
                side.reshape(depth, channels).T.astype(BF16)
            )


def left_sides(early, late, begin, done):
    sources, count, rows, channels = late.shape
    shape = (count, 2 * channels, 2 * sources * rows)
    vmem = pl.BlockSpec(memory_space=pltpu.VMEM)
    return pl.pallas_call(
        left_kernel,
        grid=(count,),
        out_shape=(jax.ShapeDtypeStruct(shape, BF16), jax.ShapeDtypeStruct((8, 128), F32)),
        in_specs=[
            pl.BlockSpec((sources, 1, rows, channels), lambda f: (0, begin + f, 0, 0)),
            pl.BlockSpec((sources, 1, rows, channels), lambda f: (0, f, 0, 0)),
            vmem,
        ],
        out_specs=(pl.BlockSpec((1,) + shape[1:], lambda f: (f, 0, 0)), vmem),
        compiler_params=pltpu.CompilerParams(vmem_limit_bytes=16 * MIB),
        name="left_sides",
    )(early, late, done)


def cross_kernel(scale, begin, stacked, me, left, *rest):
    out, done, slots, sems = rest[-4:]
    done[...] = jnp.zeros_like(done)
    step = pl.program_id(0)
    sources, _, rows, channels = rest[0].shape[-4:]
    depth = sources * rows
    blocks = rest[0].shape[0] if stacked else (len(rest) - 5) // 2
    tile = min(256, channels)
    width = slots.shape[-1]

    def leave(n):
        at = 0 if stacked else pl.multiple_of(channels * (me[0] ^ n), 128)
        return pltpu.make_async_copy(slots.at[n], out.at[begin + step, :, :, pl.ds(at, width)], sems.at[n])

    for n in range(blocks):
        if stacked:
            pair = [rest[0][n], rest[1][n]]
            slot, at = 0, channels * n
        else:
            pair = [rest[2 * n][...], rest[2 * n + 1][...]]
            slot, at = n, 0
        if at == 0:

            @pl.when(step > 0)
            def _():
                leave(slot).wait()

        right = jnp.concatenate([one[:, 0].reshape(depth, channels) for one in pair], axis=0)
        for j in range(0, channels, tile):
            for r in range(0, 2 * channels, tile):
                both = matmul(left[0, r : r + tile, :], right[:, j : j + tile]) * scale
                slots[slot, r // channels, r % channels : r % channels + tile, at + j : at + j + tile] = both.astype(BF16)
        if at + channels == width:
            leave(slot).start()

    @pl.when(step == pl.num_programs(0) - 1)
    def _():
        for slot in range(slots.shape[0]):
            leave(slot).wait()


def cross_products(left, early, late, result, begin, bins):
    sources, count, rows, channels = late[0].shape
    stacked = not isinstance(late[1], list)
    blocks = late[1].shape[0] if stacked else len(late[1]) + 1
    shape = (bins, 2, channels, blocks * channels)
    specs = [
        pl.BlockSpec((sources, 1, rows, channels), lambda f: (0, begin + f, 0, 0)),
        pl.BlockSpec((sources, 1, rows, channels), lambda f: (0, f, 0, 0)),
    ]
    operands = [lax.axis_index("chan").astype(jnp.int32).reshape(1), left]
    in_specs = [pl.BlockSpec(memory_space=pltpu.SMEM), pl.BlockSpec((1,) + left.shape[1:], lambda f: (f, 0, 0))]
    if stacked:
        operands += [early[1], late[1]]
        in_specs += [
            pl.BlockSpec((blocks, sources, 1, rows, channels), lambda f: (0, 0, begin + f, 0, 0)),
            pl.BlockSpec((blocks, sources, 1, rows, channels), lambda f: (0, 0, f, 0, 0)),
        ]
    else:
        for pair in zip([early[0]] + early[1], [late[0]] + late[1]):
            operands += pair
            in_specs += specs
    if result is None:
        result, aliases = operands[0], {}
    else:
        aliases = {len(operands): 0}
    operands.append(result)
    in_specs.append(pl.BlockSpec(memory_space=pl.ANY))
    depth = 2 * sources * rows
    return pl.pallas_call(
        functools.partial(cross_kernel, 2.0 / depth, begin, stacked),
        grid=(count,),
        out_shape=(jax.ShapeDtypeStruct(shape, BF16), jax.ShapeDtypeStruct((8, 128), F32)),
        in_specs=in_specs,
        out_specs=(
            pl.BlockSpec(memory_space=pl.ANY),
            pl.BlockSpec(memory_space=pltpu.VMEM),
        ),
        scratch_shapes=[
            pltpu.VMEM((1, 2, channels, blocks * channels) if stacked else (blocks, 2, channels, channels), BF16),
            pltpu.SemaphoreType.DMA((1 if stacked else blocks,)),
        ],
        input_output_aliases=aliases,
        compiler_params=pltpu.CompilerParams(vmem_limit_bytes=24 * MIB),
        cost_estimate=pl.CostEstimate(
            flops=4 * count * channels * blocks * channels * depth,
            bytes_accessed=4 * count * channels * blocks * channels,
            transcendentals=0,
        ),
        name="cross_products",
    )(*operands)


def swapped(shard, axis, bit):
    devices = lax.axis_size(axis)
    return lax.ppermute(shard, axis, [(i, i ^ bit) for i in range(devices)])


def fan(shard, axis, bit):
    held = {0: shard}
    while bit:
        held.update({n | bit: swapped(block, axis, bit) for n, block in list(held.items())})
        bit //= 2
    return held


def after_kernel(shard, done, out):
    out[...] = shard[...]


def after(shard, done):
    if done is None:
        return shard
    vmem = pl.BlockSpec(memory_space=pltpu.VMEM)
    return pl.pallas_call(
        after_kernel,
        out_shape=jax.ShapeDtypeStruct(shard.shape, shard.dtype),
        in_specs=[vmem, vmem],
        out_specs=vmem,
        compiler_params=pltpu.CompilerParams(vmem_limit_bytes=8 * MIB),
        name="after",
    )(shard, done)


def per_device(record, whitening, offsets, window_valid):
    devices = lax.axis_size("tm")
    blocks = lax.axis_size("chan")
    stacked = blocks & (blocks - 1) != 0 or record.shape[0] % 128 != 0
    top = blocks // 2
    bins = BINS // devices

    def exchanged(chunk):
        return lax.all_to_all(chunk, "tm", split_axis=0, concat_axis=0, tiled=True)

    def spread(mine, ready):
        if stacked:
            return mine, lax.all_gather(mine, "chan", axis=0, tiled=False)
        near = fan(mine, "chan", top // 2)
        far = after(swapped(mine, "chan", top), ready)
        found = near | {n | top: block for n, block in fan(far, "chan", top // 2).items()}
        return mine, [found[n] for n in range(1, blocks)]

    inbox = from_behind(outbox(record, offsets, window_valid), "tm", 1)
    transform, rise, fall = tables(whitening)
    parts, done = border_parts(record, inbox, transform, rise, fall)
    parts = from_behind(parts, "tm", -1)
    views = record, inbox, offsets, window_valid, transform, rise, fall
    (early,), _ = own_spectra(*views, done, devices, 0)
    late, done = own_spectra(*views, parts, devices, 1)
    early = after(exchanged(early), done)
    late = [exchanged(chunk) for chunk in late]
    early = spread(early, late[-1])
    result, begin, ready = None, 0, None
    for mine in late:
        left, _ = left_sides(early[0], mine, begin, done)
        result, done = cross_products(left, early, spread(mine, ready), result, begin, bins)
        begin, ready = begin + mine.shape[1], done
    return result


def solution(mesh):
    in_specs = (P("chan", "tm"), P(), P("tm"), P("tm"))
    out_specs = P("tm", None, "chan", None)
    return jax.shard_map(
        per_device, mesh=mesh, in_specs=in_specs, out_specs=out_specs, check_vma=False
    )
```

```python
import functools
import math

import jax
import jax.numpy as jnp
import numpy as np
from jax import lax
from jax.experimental import pallas as pl
from jax.experimental.pallas import tpu as pltpu
from jax.sharding import PartitionSpec as P

L = 2048
HOP = 512
JITTER = 256
TAPS = 65
BINS = 64
K0 = 64
RIM = 128
GROUP = L // HOP
EDGE = RIM + JITTER
LANES = 2 * BINS
MIB = 1 << 20
F32 = jnp.float32
BF16 = jnp.bfloat16


def from_behind(shard, axis, by):
    devices = lax.axis_size(axis)
    pairs = [(i, i + by) for i in range(devices) if 0 <= i + by < devices]
    return lax.ppermute(shard, axis, pairs)


def phase_table():
    sample = np.arange(L) - (TAPS - 1)
    angles = 2.0 * np.pi * np.mod(sample[:, None] * (K0 + np.arange(BINS))[None, :], L) / L
    return (np.concatenate([np.cos(angles), -np.sin(angles)], axis=1) / math.sqrt(L)).astype(np.float32)


def matmul(a, b):
    return jnp.dot(a, b, preferred_element_type=F32)


def turn(values, place):
    lane = lax.broadcasted_iota(jnp.int32, (8, LANES), 1)
    bins = K0 + (lane & (BINS - 1))
    angles = ((bins * (place + L)) & (L - 1)).astype(F32) * (2.0 * math.pi / L)
    sine = jnp.sin(angles)
    sine = jnp.where(lane < BINS, -sine, sine)
    return values * jnp.cos(angles)[:1] + pltpu.roll(values, BINS, 1) * sine[:1]


def edge_table(rise, fall, offset):
    start = JITTER - offset
    return jnp.concatenate([rise[pl.ds(start, RIM), :], fall[pl.ds(start, JITTER), :]], axis=0).astype(BF16)


def across(values):
    channels = values.shape[0]
    if channels % 128:
        values = jnp.pad(values, ((0, 128 - channels), (0, 0)))
    return values.T


def outbox_kernel(offsets, valid, record, out):
    top = record[0:8, :]
    row = lax.broadcasted_iota(jnp.int32, top.shape, 0)
    lane = lax.broadcasted_iota(jnp.int32, top.shape, 1)
    first = offsets.shape[0] - GROUP
    for q in range(GROUP):
        top = jnp.where((row == 0) & (lane == q), offsets[first + q].astype(F32), top)
        top = jnp.where((row == 0) & (lane == GROUP + q), valid[first + q].astype(F32), top)
    out[...] = jnp.concatenate([top, record[8:, :]], axis=0).astype(BF16)


def outbox(record, offsets, valid):
    channels, slab = record.shape
    smem = pl.BlockSpec(memory_space=pltpu.SMEM)
    return pl.pallas_call(
        outbox_kernel,
        grid=(1,),
        out_shape=jax.ShapeDtypeStruct((channels, RIM), BF16),
        in_specs=[smem, smem, pl.BlockSpec((channels, RIM), lambda i: (0, slab // RIM - 1))],
        out_specs=pl.BlockSpec(memory_space=pltpu.VMEM),
        compiler_params=pltpu.CompilerParams(vmem_limit_bytes=60 * MIB),
        name="outbox",
    )(offsets, valid, record)


def tables_kernel(taps, table, blocks, rise, fall, padded):
    padded[0 : TAPS - 1, :] = jnp.zeros((TAPS - 1, LANES), F32)
    padded[TAPS - 1 :, :] = table[TAPS - 1 : TAPS - 1 + padded.shape[0] - (TAPS - 1), :]
    ramp = jnp.zeros((TAPS - 1, LANES), F32)
    gain = jnp.zeros((1, LANES), F32)
    for m in range(TAPS):
        tap = taps[m]
        ramp = ramp + tap * padded[m : m + TAPS - 1, :]
        gain = gain + tap * padded[TAPS - 1 + m : TAPS + m, :]
    gain = jnp.broadcast_to(gain * math.sqrt(L), (8, LANES))
    lane = lax.broadcasted_iota(jnp.int32, (8, LANES), 1)
    swapped = pltpu.roll(gain, BINS, 1)
    gain_re = jnp.where(lane < BINS, gain, swapped)[:1]
    gain_im = jnp.where(lane < BINS, -swapped, gain)[:1]
    columns = table[...]
    pure = columns * gain_re + pltpu.roll(columns, BINS, 1) * gain_im
    blocks[...] = pure.astype(BF16)
    rise[...] = jnp.zeros_like(rise)
    rise[rise.shape[0] - (TAPS - 1) :, :] = -ramp
    ahead = JITTER - (TAPS - 1)
    fall[0:ahead, :] = pure[L - ahead :]
    fall[ahead:JITTER, :] = pure[: TAPS - 1] - ramp
    fall[JITTER:, :] = jnp.zeros((fall.shape[0] - JITTER, LANES), F32)


def tables(whitening):
    vmem = pl.BlockSpec(memory_space=pltpu.VMEM)
    return pl.pallas_call(
        tables_kernel,
        out_shape=(
            jax.ShapeDtypeStruct((L, LANES), BF16),
            jax.ShapeDtypeStruct((EDGE, LANES), F32),
            jax.ShapeDtypeStruct((2 * JITTER, LANES), F32),
        ),
        in_specs=[pl.BlockSpec(memory_space=pltpu.SMEM), vmem],
        out_specs=(vmem, vmem, vmem),
        scratch_shapes=[pltpu.VMEM((2 * TAPS + 6, LANES), F32)],
        compiler_params=pltpu.CompilerParams(vmem_limit_bytes=16 * MIB),
        name="tables",
    )(whitening, phase_table())


def border_kernel(inbox, record, blocks, rise, fall, parts, done, collected):
    channels = record.shape[0]
    done[...] = jnp.zeros_like(done)
    head = inbox[0:16, :].astype(F32)[:1]
    lane = lax.broadcasted_iota(jnp.int32, (1, LANES), 1)

    def told(at):
        return jnp.sum(jnp.where(lane == at, head, 0.0)).astype(jnp.int32)

    before = jnp.zeros((channels, LANES), F32)
    for q in range(GROUP):
        offset = told(q)
        edges = edge_table(rise, fall, offset)
        if q == 0:
            part = matmul(record[:, 0:JITTER].astype(BF16), edges[RIM:])
        else:
            part = matmul(record[:, HOP * q - RIM : HOP * q + JITTER].astype(BF16), edges)
        place = HOP * q + offset - (TAPS - 1)
        part = (part + turn(before, place)) * told(GROUP + q).astype(F32)
        upright = across(part)
        for c in range(collected.shape[0]):
            piece = upright[:, 128 * c : 128 * c + 128]
            collected[c, pl.ds(q, BINS, stride=2 * GROUP), :] = piece[:BINS]
            collected[c, pl.ds(GROUP + q, BINS, stride=2 * GROUP), :] = piece[BINS:]
        if q < GROUP - 1:
            before = before + matmul(
                record[:, HOP * q : HOP * q + HOP].astype(BF16), blocks[HOP * q : HOP * q + HOP, :]
            )
    width = min(128, channels)
    for c in range(collected.shape[0]):
        block = collected[c].reshape(BINS, 2 * GROUP, 128).astype(BF16)
        parts[:, :, width * c : width * c + width] = block[:, :, :width]


def border_parts(record, inbox, blocks, rise, fall):
    channels = record.shape[0]
    vmem = pl.BlockSpec(memory_space=pltpu.VMEM)
    lead = L - HOP + JITTER
    return pl.pallas_call(
        border_kernel,
        grid=(1,),
        out_shape=(jax.ShapeDtypeStruct((BINS, 2 * GROUP, channels), BF16), jax.ShapeDtypeStruct((8, 128), F32)),
        in_specs=[vmem, pl.BlockSpec((channels, lead), lambda i: (0, 0)), vmem, vmem, vmem],
        out_specs=(vmem, vmem),
        scratch_shapes=[pltpu.VMEM((max(channels // 128, 1), 2 * GROUP * BINS, 128), F32)],
        compiler_params=pltpu.CompilerParams(vmem_limit_bytes=50 * MIB),
        cost_estimate=pl.CostEstimate(
            flops=2 * channels * LANES * 3072, bytes_accessed=4 * channels * lead, transcendentals=0
        ),
        name="border_parts",
    )(inbox, record, blocks, rise, fall)


def spectra_kernel(first, span, offsets, valid, record, rim, blocks, rise, fall, parts, *rest):
    *outs, done, samples, later, collected, sems = rest
    channels, slab = record.shape
    windows = GROUP * span
    tail = L - HOP + JITTER
    done[...] = jnp.zeros_like(done)
    end = RIM + L * span
    base = L * first
    fetches = [(base + HOP * i, RIM + HOP * i, HOP) for i in range(GROUP * span)]
    if first == 0:
        samples[:, 0:RIM] = rim[...].astype(F32)
    else:
        fetches[0] = (base - RIM, 0, RIM + HOP)
    more = base + L * span < slab
    if more:
        fetches += [(base + HOP * i, RIM + HOP * i, HOP) for i in range(GROUP * span, GROUP * (span + 1) - 1)]
        left = tail - HOP * (GROUP - 1)
        fetches.append((base + L * span + tail - left, end + tail - left, left))
    else:
        samples[:, end:] = jnp.zeros((channels, tail), F32)
    copies = [
        pltpu.make_async_copy(record.at[:, pl.ds(src, size)], samples.at[:, pl.ds(dst, size)], sems.at[i])
        for i, (src, dst, size) in enumerate(fetches)
    ]
    for copy in copies:
        copy.start()

    def arrived(i):
        if i < len(copies):
            copies[i].wait()

    def block_sums(s):
        found = []
        for i in range(GROUP if s < span else GROUP - 1):
            arrived(GROUP * s + i)
            found.append(
                matmul(
                    samples[:, RIM + L * s + HOP * i : RIM + L * s + HOP * i + HOP].astype(BF16),
                    blocks[HOP * i : HOP * i + HOP, :],
                )
            )
        return found

    def keep(found):
        total = found[GROUP - 1]
        later[GROUP - 1] = total
        for q in range(GROUP - 2, -1, -1):
            total = total + found[q]
            later[q] = total

    keep(block_sums(0))
    for s in range(span):
        found = block_sums(s + 1) if s + 1 < span or more else []
        if s + 1 == span and more:
            arrived(len(copies) - 1)
        before = None
        for q in range(GROUP):
            w = GROUP * s + q
            offset = offsets[GROUP * first + w]
            begin = HOP * w
            ends = samples[:, begin + L : begin + L + EDGE] - samples[:, begin : begin + EDGE]
            part = matmul(ends.astype(BF16), edge_table(rise, fall, offset))
            total = later[q] if before is None else later[q] + before
            part = (part + turn(total, HOP * q + offset - (TAPS - 1))) * valid[GROUP * first + w].astype(F32)
            upright = across(part)
            for c in range(collected.shape[0]):
                piece = upright[:, 128 * c : 128 * c + 128]
                collected[c, pl.ds(w, BINS, stride=2 * windows), :] = piece[:BINS]
                collected[c, pl.ds(windows + w, BINS, stride=2 * windows), :] = piece[BINS:]
            if found and q < GROUP - 1:
                before = found[q] if before is None else before + found[q]
        if s + 1 < span:
            keep(found)

    width = min(128, channels)
    for c in range(collected.shape[0]):
        lanes = slice(width * c, width * c + width)
        block = collected[c].reshape(BINS, 2 * windows, 128)[:, :, :width]
        if not more:
            block = with_parts(block, parts[:, :, lanes].astype(F32))
        block = block.astype(BF16)
        for group in range(outs[0].shape[0]):
            begin = group * BINS // outs[0].shape[0]
            for out in outs:
                out[group, :, :, lanes] = block[begin : begin + out.shape[1]]
                begin += out.shape[1]


def with_parts(block, part):
    windows = block.shape[1] // 2
    row = lax.broadcasted_iota(jnp.int32, part.shape, 1)
    moved = jnp.concatenate([part[:, GROUP:], part[:, :GROUP]], axis=1)
    pieces = []
    for ri, extra in enumerate((moved, part)):
        end = windows * ri + windows
        if windows > 2 * GROUP:
            pieces.append(block[:, windows * ri : end - 2 * GROUP])
        pieces.append(block[:, end - 2 * GROUP : end] + jnp.where(row >= GROUP, extra, 0.0))
    return jnp.concatenate(pieces, axis=1)


def chunk_sizes(bins):
    return [bins - 3 * bins // 8, 3 * bins // 8]


def own_spectra(record, rim, offsets, valid, transform, rise, fall, parts, devices, half):
    channels, slab = record.shape
    span = slab // L // 2
    windows = GROUP * span
    sizes = chunk_sizes(BINS // devices) if half else [BINS // devices]
    smem = pl.BlockSpec(memory_space=pltpu.SMEM)
    vmem = pl.BlockSpec(memory_space=pltpu.VMEM)
    *chunks, done = pl.pallas_call(
        functools.partial(spectra_kernel, span * half, span),
        out_shape=tuple(jax.ShapeDtypeStruct((devices, count, 2 * windows, channels), BF16) for count in sizes)
        + (jax.ShapeDtypeStruct((8, 128), F32),),
        in_specs=[smem, smem, pl.BlockSpec(memory_space=pl.ANY), vmem, vmem, vmem, vmem, vmem],
        out_specs=(vmem,) * (len(sizes) + 1),
        scratch_shapes=[
            pltpu.VMEM((channels, RIM + L * span + L - HOP + JITTER), F32),
            pltpu.VMEM((GROUP, channels, LANES), F32),
            pltpu.VMEM((max(channels // 128, 1), LANES * windows, 128), F32),
            pltpu.SemaphoreType.DMA((GROUP * (span + 1),)),
        ],
        compiler_params=pltpu.CompilerParams(vmem_limit_bytes=50 * MIB),
        cost_estimate=pl.CostEstimate(
            flops=2 * channels * LANES * 896 * windows, bytes_accessed=2 * channels * slab, transcendentals=0
        ),
        name=f"own_spectra_{half}",
    )(offsets, valid, record, rim, transform, rise, fall, parts)
    return chunks, done


def left_kernel(early, late, done, out, ready):
    ready[...] = jnp.zeros_like(ready)
    sources, _, rows, channels = early.shape
    depth = sources * rows
    half = rows // 2
    for i, own in enumerate((early, late)):
        straight = own[:, 0].astype(F32)
        turned = jnp.concatenate([straight[:, half:], -straight[:, :half]], axis=1)
        for j, side in enumerate((straight, turned)):
            out[0, channels * j : channels * j + channels, depth * i : depth * i + depth] = (
                side.reshape(depth, channels).T.astype(BF16)
            )


def left_sides(early, late, begin, done):
    sources, count, rows, channels = late.shape
    shape = (count, 2 * channels, 2 * sources * rows)
    vmem = pl.BlockSpec(memory_space=pltpu.VMEM)
    return pl.pallas_call(
        left_kernel,
        grid=(count,),
        out_shape=(jax.ShapeDtypeStruct(shape, BF16), jax.ShapeDtypeStruct((8, 128), F32)),
        in_specs=[
            pl.BlockSpec((sources, 1, rows, channels), lambda f: (0, begin + f, 0, 0)),
            pl.BlockSpec((sources, 1, rows, channels), lambda f: (0, f, 0, 0)),
            vmem,
        ],
        out_specs=(pl.BlockSpec((1,) + shape[1:], lambda f: (f, 0, 0)), vmem),
        compiler_params=pltpu.CompilerParams(vmem_limit_bytes=16 * MIB),
        name="left_sides",
    )(early, late, done)


def cross_kernel(scale, side, me, left, *rest):
    out, done = rest[-2:]
    done[...] = jnp.zeros_like(done)
    sources, _, rows, channels = rest[0].shape[-4:]
    depth = sources * rows
    blocks = out.shape[3] // channels
    tile = min(256, channels)
    for n in range(blocks):
        if side is None:
            pair = [rest[0][n], rest[1][n]]
            at = channels * n
        else:
            pair = [rest[2 * n][...], rest[2 * n + 1][...]]
            at = pl.multiple_of(channels * ((me[0] ^ n) & (blocks - 1)), 128)
        right = jnp.concatenate([one[:, 0].reshape(depth, channels) for one in pair], axis=0)
        for j in range(0, channels, tile):
            for r in range(0, 2 * channels, tile):
                both = matmul(left[0, r : r + tile, :], right[:, j : j + tile]) * scale
                out[0, r // channels, r % channels : r % channels + tile, pl.ds(at + j, tile)] = both.astype(BF16)


def cross_products(left, early, late, result, begin, bins, blocks, side):
    sources, count, rows, channels = (late if side is None else late[0]).shape[-4:]
    columns = blocks if side is None else len(late)
    shape = (bins, 2, channels, blocks * channels)
    operands = [lax.axis_index("chan").astype(jnp.int32).reshape(1), left]
    in_specs = [pl.BlockSpec((1,) + left.shape[1:], lambda f, me: (f, 0, 0))]
    if side is None:
        operands += [early, late]
        in_specs += [
            pl.BlockSpec((blocks, sources, 1, rows, channels), lambda f, me: (0, 0, begin + f, 0, 0)),
            pl.BlockSpec((blocks, sources, 1, rows, channels), lambda f, me: (0, 0, f, 0, 0)),
        ]
    else:
        for pair in zip(early, late):
            operands += pair
            in_specs += [
                pl.BlockSpec((sources, 1, rows, channels), lambda f, me: (0, begin + f, 0, 0)),
                pl.BlockSpec((sources, 1, rows, channels), lambda f, me: (0, f, 0, 0)),
            ]
    if result is None:
        result, aliases = operands[1], {}
    else:
        aliases = {len(operands): 0}
    operands.append(result)
    in_specs.append(pl.BlockSpec(memory_space=pl.ANY))
    depth = 2 * sources * rows

    def place(f, me):
        return begin + f, 0, 0, 0 if side is None else (me[0] // columns) ^ side

    return pl.pallas_call(
        functools.partial(cross_kernel, 2.0 / depth, side),
        grid_spec=pltpu.PrefetchScalarGridSpec(
            num_scalar_prefetch=1,
            grid=(count,),
            in_specs=in_specs,
            out_specs=(
                pl.BlockSpec((1, 2, channels, columns * channels), place),
                pl.BlockSpec((8, 128), lambda f, me: (0, 0)),
            ),
        ),
        out_shape=(jax.ShapeDtypeStruct(shape, BF16), jax.ShapeDtypeStruct((8, 128), F32)),
        input_output_aliases=aliases,
        compiler_params=pltpu.CompilerParams(vmem_limit_bytes=24 * MIB),
        cost_estimate=pl.CostEstimate(
            flops=4 * count * channels * columns * channels * depth,
            bytes_accessed=4 * count * channels * columns * channels,
            transcendentals=0,
        ),
        name="cross_products",
    )(*operands)


def swapped(shard, axis, bit):
    devices = lax.axis_size(axis)
    return lax.ppermute(shard, axis, [(i, i ^ bit) for i in range(devices)])


def fan(shard, axis, bit):
    held = {0: shard}
    while bit:
        held.update({n | bit: swapped(block, axis, bit) for n, block in list(held.items())})
        bit //= 2
    return held


def after_kernel(shard, done, out):
    out[...] = shard[...]


def after(shard, done):
    if done is None:
        return shard
    vmem = pl.BlockSpec(memory_space=pltpu.VMEM)
    return pl.pallas_call(
        after_kernel,
        out_shape=jax.ShapeDtypeStruct(shard.shape, shard.dtype),
        in_specs=[vmem, vmem],
        out_specs=vmem,
        compiler_params=pltpu.CompilerParams(vmem_limit_bytes=8 * MIB),
        name="after",
    )(shard, done)


def per_device(record, whitening, offsets, window_valid):
    devices = lax.axis_size("tm")
    blocks = lax.axis_size("chan")
    stacked = blocks & (blocks - 1) != 0 or record.shape[0] % 128 != 0
    top = blocks // 2
    bins = BINS // devices

    def exchanged(chunk):
        return lax.all_to_all(chunk, "tm", split_axis=0, concat_axis=0, tiled=True)

    def fanned(shard):
        held = fan(shard, "chan", top // 2)
        return [held[n] for n in range(top)]

    inbox = from_behind(outbox(record, offsets, window_valid), "tm", 1)
    transform, rise, fall = tables(whitening)
    parts, done = border_parts(record, inbox, transform, rise, fall)
    parts = from_behind(parts, "tm", -1)
    views = record, inbox, offsets, window_valid, transform, rise, fall
    (early,), _ = own_spectra(*views, done, devices, 0)
    late, done = own_spectra(*views, parts, devices, 1)
    early = after(exchanged(after(early, parts)), done)
    result, begin, rest = None, 0, []
    near_early = None if stacked else fanned(early)
    far_early = None if stacked else swapped(early, "chan", top)
    for p, chunk in enumerate(late):
        mine = exchanged(chunk)
        if stacked:
            left, _ = left_sides(early, mine, begin, done)
            both = [lax.all_gather(one, "chan", axis=0, tiled=False) for one in (early, mine)]
            result, _ = cross_products(left, *both, result, begin, bins, blocks, None)
        else:
            mine = after(mine, done) if p else mine
            far, near = swapped(mine, "chan", top), fanned(mine)
            left, _ = left_sides(early, mine, begin, done)
            result, done = cross_products(left, near_early, near, result, begin, bins, blocks, 0)
            rest.append((left, far, begin))
        begin += mine.shape[1]
    if not stacked:
        far_early, ready = fanned(after(far_early, mine)), None
        for left, far, begin in rest:
            far = fanned(after(far, ready))
            result, ready = cross_products(left, far_early, far, result, begin, bins, blocks, 1)
    return result


def solution(mesh):
    in_specs = (P("chan", "tm"), P(), P("tm"), P("tm"))
    out_specs = P("tm", None, "chan", None)
    return jax.shard_map(
        per_device, mesh=mesh, in_specs=in_specs, out_specs=out_specs, check_vma=False
    )
```

```python
import functools
import math

import jax
import jax.numpy as jnp
import numpy as np
from jax import lax
from jax.experimental import pallas as pl
from jax.experimental.pallas import tpu as pltpu
from jax.sharding import PartitionSpec as P

L = 2048
HOP = 512
JITTER = 256
TAPS = 65
BINS = 64
K0 = 64
RIM = 128
GROUP = L // HOP
EDGE = RIM + JITTER
LANES = 2 * BINS
MIB = 1 << 20
F32 = jnp.float32
BF16 = jnp.bfloat16


def from_behind(shard, axis, by):
    devices = lax.axis_size(axis)
    pairs = [(i, i + by) for i in range(devices) if 0 <= i + by < devices]
    return lax.ppermute(shard, axis, pairs)


def phase_table():
    sample = np.arange(L) - (TAPS - 1)
    angles = 2.0 * np.pi * np.mod(sample[:, None] * (K0 + np.arange(BINS))[None, :], L) / L
    return (np.concatenate([np.cos(angles), -np.sin(angles)], axis=1) / math.sqrt(L)).astype(np.float32)


def matmul(a, b):
    return jnp.dot(a, b, preferred_element_type=F32)


def turn(values, place):
    lane = lax.broadcasted_iota(jnp.int32, (8, LANES), 1)
    bins = K0 + (lane & (BINS - 1))
    angles = ((bins * (place + L)) & (L - 1)).astype(F32) * (2.0 * math.pi / L)
    sine = jnp.sin(angles)
    sine = jnp.where(lane < BINS, -sine, sine)
    return values * jnp.cos(angles)[:1] + pltpu.roll(values, BINS, 1) * sine[:1]


def edge_table(rise, fall, offset):
    start = JITTER - offset
    return jnp.concatenate([rise[pl.ds(start, RIM), :], fall[pl.ds(start, JITTER), :]], axis=0).astype(BF16)


def across(values):
    channels = values.shape[0]
    if channels % 128:
        values = jnp.pad(values, ((0, 128 - channels), (0, 0)))
    return values.T


def outbox_kernel(offsets, valid, record, out):
    top = record[0:8, :]
    row = lax.broadcasted_iota(jnp.int32, top.shape, 0)
    lane = lax.broadcasted_iota(jnp.int32, top.shape, 1)
    first = offsets.shape[0] - GROUP
    for q in range(GROUP):
        top = jnp.where((row == 0) & (lane == q), offsets[first + q].astype(F32), top)
        top = jnp.where((row == 0) & (lane == GROUP + q), valid[first + q].astype(F32), top)
    out[...] = jnp.concatenate([top, record[8:, :]], axis=0).astype(BF16)


def outbox(record, offsets, valid):
    channels, slab = record.shape
    smem = pl.BlockSpec(memory_space=pltpu.SMEM)
    return pl.pallas_call(
        outbox_kernel,
        grid=(1,),
        out_shape=jax.ShapeDtypeStruct((channels, RIM), BF16),
        in_specs=[smem, smem, pl.BlockSpec((channels, RIM), lambda i: (0, slab // RIM - 1))],
        out_specs=pl.BlockSpec(memory_space=pltpu.VMEM),
        compiler_params=pltpu.CompilerParams(vmem_limit_bytes=60 * MIB),
        name="outbox",
    )(offsets, valid, record)


def tables_kernel(taps, table, blocks, rise, fall, padded):
    padded[0 : TAPS - 1, :] = jnp.zeros((TAPS - 1, LANES), F32)
    padded[TAPS - 1 :, :] = table[TAPS - 1 : TAPS - 1 + padded.shape[0] - (TAPS - 1), :]
    ramp = jnp.zeros((TAPS - 1, LANES), F32)
    gain = jnp.zeros((1, LANES), F32)
    for m in range(TAPS):
        tap = taps[m]
        ramp = ramp + tap * padded[m : m + TAPS - 1, :]
        gain = gain + tap * padded[TAPS - 1 + m : TAPS + m, :]
    gain = jnp.broadcast_to(gain * math.sqrt(L), (8, LANES))
    lane = lax.broadcasted_iota(jnp.int32, (8, LANES), 1)
    swapped = pltpu.roll(gain, BINS, 1)
    gain_re = jnp.where(lane < BINS, gain, swapped)[:1]
    gain_im = jnp.where(lane < BINS, -swapped, gain)[:1]
    columns = table[...]
    pure = columns * gain_re + pltpu.roll(columns, BINS, 1) * gain_im
    blocks[...] = pure.astype(BF16)
    rise[...] = jnp.zeros_like(rise)
    rise[rise.shape[0] - (TAPS - 1) :, :] = -ramp
    ahead = JITTER - (TAPS - 1)
    fall[0:ahead, :] = pure[L - ahead :]
    fall[ahead:JITTER, :] = pure[: TAPS - 1] - ramp
    fall[JITTER:, :] = jnp.zeros((fall.shape[0] - JITTER, LANES), F32)


def tables(whitening):
    vmem = pl.BlockSpec(memory_space=pltpu.VMEM)
    return pl.pallas_call(
        tables_kernel,
        out_shape=(
            jax.ShapeDtypeStruct((L, LANES), BF16),
            jax.ShapeDtypeStruct((EDGE, LANES), F32),
            jax.ShapeDtypeStruct((2 * JITTER, LANES), F32),
        ),
        in_specs=[pl.BlockSpec(memory_space=pltpu.SMEM), vmem],
        out_specs=(vmem, vmem, vmem),
        scratch_shapes=[pltpu.VMEM((2 * TAPS + 6, LANES), F32)],
        compiler_params=pltpu.CompilerParams(vmem_limit_bytes=16 * MIB),
        name="tables",
    )(whitening, phase_table())


def border_kernel(inbox, record, blocks, rise, fall, parts, done, collected):
    channels = record.shape[0]
    done[...] = jnp.zeros_like(done)
    head = inbox[0:16, :].astype(F32)[:1]
    lane = lax.broadcasted_iota(jnp.int32, (1, LANES), 1)

    def told(at):
        return jnp.sum(jnp.where(lane == at, head, 0.0)).astype(jnp.int32)

    before = jnp.zeros((channels, LANES), F32)
    for q in range(GROUP):
        offset = told(q)
        edges = edge_table(rise, fall, offset)
        if q == 0:
            part = matmul(record[:, 0:JITTER].astype(BF16), edges[RIM:])
        else:
            part = matmul(record[:, HOP * q - RIM : HOP * q + JITTER].astype(BF16), edges)
        place = HOP * q + offset - (TAPS - 1)
        part = (part + turn(before, place)) * told(GROUP + q).astype(F32)
        upright = across(part)
        for c in range(collected.shape[0]):
            piece = upright[:, 128 * c : 128 * c + 128]
            collected[c, pl.ds(q, BINS, stride=2 * GROUP), :] = piece[:BINS]
            collected[c, pl.ds(GROUP + q, BINS, stride=2 * GROUP), :] = piece[BINS:]
        if q < GROUP - 1:
            before = before + matmul(
                record[:, HOP * q : HOP * q + HOP].astype(BF16), blocks[HOP * q : HOP * q + HOP, :]
            )
    width = min(128, channels)
    for c in range(collected.shape[0]):
        block = collected[c].reshape(BINS, 2 * GROUP, 128).astype(BF16)
        parts[:, :, width * c : width * c + width] = block[:, :, :width]


def border_parts(record, inbox, blocks, rise, fall):
    channels = record.shape[0]
    vmem = pl.BlockSpec(memory_space=pltpu.VMEM)
    lead = L - HOP + JITTER
    return pl.pallas_call(
        border_kernel,
        grid=(1,),
        out_shape=(jax.ShapeDtypeStruct((BINS, 2 * GROUP, channels), BF16), jax.ShapeDtypeStruct((8, 128), F32)),
        in_specs=[vmem, pl.BlockSpec((channels, lead), lambda i: (0, 0)), vmem, vmem, vmem],
        out_specs=(vmem, vmem),
        scratch_shapes=[pltpu.VMEM((max(channels // 128, 1), 2 * GROUP * BINS, 128), F32)],
        compiler_params=pltpu.CompilerParams(vmem_limit_bytes=50 * MIB),
        cost_estimate=pl.CostEstimate(
            flops=2 * channels * LANES * 3072, bytes_accessed=4 * channels * lead, transcendentals=0
        ),
        name="border_parts",
    )(inbox, record, blocks, rise, fall)


def spectra_kernel(first, span, offsets, valid, record, rim, blocks, rise, fall, parts, *rest):
    *outs, done, samples, later, collected, sems = rest
    channels, slab = record.shape
    windows = GROUP * span
    tail = L - HOP + JITTER
    done[...] = jnp.zeros_like(done)
    end = RIM + L * span
    base = L * first
    fetches = [(base + HOP * i, RIM + HOP * i, HOP) for i in range(GROUP * span)]
    if first == 0:
        samples[:, 0:RIM] = rim[...].astype(F32)
    else:
        fetches[0] = (base - RIM, 0, RIM + HOP)
    more = base + L * span < slab
    if more:
        fetches += [(base + HOP * i, RIM + HOP * i, HOP) for i in range(GROUP * span, GROUP * (span + 1) - 1)]
        left = tail - HOP * (GROUP - 1)
        fetches.append((base + L * span + tail - left, end + tail - left, left))
    else:
        samples[:, end:] = jnp.zeros((channels, tail), F32)
    copies = [
        pltpu.make_async_copy(record.at[:, pl.ds(src, size)], samples.at[:, pl.ds(dst, size)], sems.at[i])
        for i, (src, dst, size) in enumerate(fetches)
    ]
    for copy in copies:
        copy.start()

    def arrived(i):
        if i < len(copies):
            copies[i].wait()

    def block_sums(s):
        found = []
        for i in range(GROUP if s < span else GROUP - 1):
            arrived(GROUP * s + i)
            found.append(
                matmul(
                    samples[:, RIM + L * s + HOP * i : RIM + L * s + HOP * i + HOP].astype(BF16),
                    blocks[HOP * i : HOP * i + HOP, :],
                )
            )
        return found

    def keep(found):
        total = found[GROUP - 1]
        later[GROUP - 1] = total
        for q in range(GROUP - 2, -1, -1):
            total = total + found[q]
            later[q] = total

    keep(block_sums(0))
    for s in range(span):
        found = block_sums(s + 1) if s + 1 < span or more else []
        if s + 1 == span and more:
            arrived(len(copies) - 1)
        before = None
        for q in range(GROUP):
            w = GROUP * s + q
            offset = offsets[GROUP * first + w]
            begin = HOP * w
            ends = samples[:, begin + L : begin + L + EDGE] - samples[:, begin : begin + EDGE]
            part = matmul(ends.astype(BF16), edge_table(rise, fall, offset))
            total = later[q] if before is None else later[q] + before
            part = (part + turn(total, HOP * q + offset - (TAPS - 1))) * valid[GROUP * first + w].astype(F32)
            upright = across(part)
            for c in range(collected.shape[0]):
                piece = upright[:, 128 * c : 128 * c + 128]
                collected[c, pl.ds(w, BINS, stride=2 * windows), :] = piece[:BINS]
                collected[c, pl.ds(windows + w, BINS, stride=2 * windows), :] = piece[BINS:]
            if found and q < GROUP - 1:
                before = found[q] if before is None else before + found[q]
        if s + 1 < span:
            keep(found)

    width = min(128, channels)
    for c in range(collected.shape[0]):
        lanes = slice(width * c, width * c + width)
        block = collected[c].reshape(BINS, 2 * windows, 128)[:, :, :width]
        if not more:
            block = with_parts(block, parts[:, :, lanes].astype(F32))
        block = block.astype(BF16)
        for group in range(outs[0].shape[0]):
            begin = group * BINS // outs[0].shape[0]
            for out in outs:
                out[group, :, :, lanes] = block[begin : begin + out.shape[1]]
                begin += out.shape[1]


def with_parts(block, part):
    windows = block.shape[1] // 2
    row = lax.broadcasted_iota(jnp.int32, part.shape, 1)
    moved = jnp.concatenate([part[:, GROUP:], part[:, :GROUP]], axis=1)
    pieces = []
    for ri, extra in enumerate((moved, part)):
        end = windows * ri + windows
        if windows > 2 * GROUP:
            pieces.append(block[:, windows * ri : end - 2 * GROUP])
        pieces.append(block[:, end - 2 * GROUP : end] + jnp.where(row >= GROUP, extra, 0.0))
    return jnp.concatenate(pieces, axis=1)


def chunk_sizes(bins):
    return [bins - 3 * bins // 8, 3 * bins // 8]


def own_spectra(record, rim, offsets, valid, transform, rise, fall, parts, devices, half):
    channels, slab = record.shape
    span = slab // L // 2
    windows = GROUP * span
    sizes = chunk_sizes(BINS // devices) if half else [BINS // devices]
    smem = pl.BlockSpec(memory_space=pltpu.SMEM)
    vmem = pl.BlockSpec(memory_space=pltpu.VMEM)
    *chunks, done = pl.pallas_call(
        functools.partial(spectra_kernel, span * half, span),
        out_shape=tuple(jax.ShapeDtypeStruct((devices, count, 2 * windows, channels), BF16) for count in sizes)
        + (jax.ShapeDtypeStruct((8, 128), F32),),
        in_specs=[smem, smem, pl.BlockSpec(memory_space=pl.ANY), vmem, vmem, vmem, vmem, vmem],
        out_specs=(vmem,) * (len(sizes) + 1),
        scratch_shapes=[
            pltpu.VMEM((channels, RIM + L * span + L - HOP + JITTER), F32),
            pltpu.VMEM((GROUP, channels, LANES), F32),
            pltpu.VMEM((max(channels // 128, 1), LANES * windows, 128), F32),
            pltpu.SemaphoreType.DMA((GROUP * (span + 1),)),
        ],
        compiler_params=pltpu.CompilerParams(vmem_limit_bytes=50 * MIB),
        cost_estimate=pl.CostEstimate(
            flops=2 * channels * LANES * 896 * windows,
            bytes_accessed=(32 if half else 4) * channels * slab,
            transcendentals=0,
        ),
        name=f"own_spectra_{half}",
    )(offsets, valid, record, rim, transform, rise, fall, parts)
    return chunks, done


def left_kernel(early, late, done, out, ready):
    ready[...] = jnp.zeros_like(ready)
    sources, _, rows, channels = early.shape
    depth = sources * rows
    half = rows // 2
    for i, own in enumerate((early, late)):
        straight = own[:, 0].astype(F32)
        turned = jnp.concatenate([straight[:, half:], -straight[:, :half]], axis=1)
        for j, side in enumerate((straight, turned)):
            out[0, channels * j : channels * j + channels, depth * i : depth * i + depth] = (
                side.reshape(depth, channels).T.astype(BF16)
            )


def left_sides(early, late, begin, done):
    sources, count, rows, channels = late.shape
    shape = (count, 2 * channels, 2 * sources * rows)
    vmem = pl.BlockSpec(memory_space=pltpu.VMEM)
    return pl.pallas_call(
        left_kernel,
        grid=(count,),
        out_shape=(jax.ShapeDtypeStruct(shape, BF16), jax.ShapeDtypeStruct((8, 128), F32)),
        in_specs=[
            pl.BlockSpec((sources, 1, rows, channels), lambda f: (0, begin + f, 0, 0)),
            pl.BlockSpec((sources, 1, rows, channels), lambda f: (0, f, 0, 0)),
            vmem,
        ],
        out_specs=(pl.BlockSpec((1,) + shape[1:], lambda f: (f, 0, 0)), vmem),
        compiler_params=pltpu.CompilerParams(vmem_limit_bytes=16 * MIB),
        name="left_sides",
    )(early, late, done)


def cross_kernel(scale, side, me, left, *rest):
    out, done = rest[-2:]
    done[...] = jnp.zeros_like(done)
    sources, _, rows, channels = rest[0].shape[-4:]
    depth = sources * rows
    blocks = out.shape[3] // channels
    tile = min(256, channels)
    for n in range(blocks):
        if side is None:
            pair = [rest[0][n], rest[1][n]]
            at = channels * n
        else:
            pair = [rest[2 * n][...], rest[2 * n + 1][...]]
            at = pl.multiple_of(channels * ((me[0] ^ n) & (blocks - 1)), 128)
        right = jnp.concatenate([one[:, 0].reshape(depth, channels) for one in pair], axis=0)
        for j in range(0, channels, tile):
            for r in range(0, 2 * channels, tile):
                both = matmul(left[0, r : r + tile, :], right[:, j : j + tile]) * scale
                out[0, r // channels, r % channels : r % channels + tile, pl.ds(at + j, tile)] = both.astype(BF16)


def cross_products(left, early, late, result, begin, bins, blocks, side):
    sources, count, rows, channels = (late if side is None else late[0]).shape[-4:]
    columns = blocks if side is None else len(late)
    shape = (bins, 2, channels, blocks * channels)
    operands = [lax.axis_index("chan").astype(jnp.int32).reshape(1), left]
    in_specs = [pl.BlockSpec((1,) + left.shape[1:], lambda f, me: (f, 0, 0))]
    if side is None:
        operands += [early, late]
        in_specs += [
            pl.BlockSpec((blocks, sources, 1, rows, channels), lambda f, me: (0, 0, begin + f, 0, 0)),
            pl.BlockSpec((blocks, sources, 1, rows, channels), lambda f, me: (0, 0, f, 0, 0)),
        ]
    else:
        for pair in zip(early, late):
            operands += pair
            in_specs += [
                pl.BlockSpec((sources, 1, rows, channels), lambda f, me: (0, begin + f, 0, 0)),
                pl.BlockSpec((sources, 1, rows, channels), lambda f, me: (0, f, 0, 0)),
            ]
    if result is None:
        result, aliases = operands[1], {}
    else:
        aliases = {len(operands): 0}
    operands.append(result)
    in_specs.append(pl.BlockSpec(memory_space=pl.ANY))
    depth = 2 * sources * rows

    def place(f, me):
        return begin + f, 0, 0, 0 if side is None else (me[0] // columns) ^ side

    return pl.pallas_call(
        functools.partial(cross_kernel, 2.0 / depth, side),
        grid_spec=pltpu.PrefetchScalarGridSpec(
            num_scalar_prefetch=1,
            grid=(count,),
            in_specs=in_specs,
            out_specs=(
                pl.BlockSpec((1, 2, channels, columns * channels), place),
                pl.BlockSpec((8, 128), lambda f, me: (0, 0)),
            ),
        ),
        out_shape=(jax.ShapeDtypeStruct(shape, BF16), jax.ShapeDtypeStruct((8, 128), F32)),
        input_output_aliases=aliases,
        compiler_params=pltpu.CompilerParams(vmem_limit_bytes=24 * MIB),
        cost_estimate=pl.CostEstimate(
            flops=4 * count * channels * columns * channels * depth,
            bytes_accessed=4 * count * channels * columns * channels,
            transcendentals=0,
        ),
        name="cross_products",
    )(*operands)


def swapped(shard, axis, bit):
    devices = lax.axis_size(axis)
    return lax.ppermute(shard, axis, [(i, i ^ bit) for i in range(devices)])


def fan(shard, axis, bit):
    held = {0: shard}
    while bit:
        held.update({n | bit: swapped(block, axis, bit) for n, block in list(held.items())})
        bit //= 2
    return held


def after_kernel(shard, done, out):
    out[...] = shard[...]


def after(shard, done):
    if done is None:
        return shard
    vmem = pl.BlockSpec(memory_space=pltpu.VMEM)
    return pl.pallas_call(
        after_kernel,
        out_shape=jax.ShapeDtypeStruct(shard.shape, shard.dtype),
        in_specs=[vmem, vmem],
        out_specs=vmem,
        compiler_params=pltpu.CompilerParams(vmem_limit_bytes=8 * MIB),
        name="after",
    )(shard, done)


def untouched_kernel(shard, done, out):
    pass


def after_in_place(shard, done):
    anywhere = pl.BlockSpec(memory_space=pl.ANY)
    return pl.pallas_call(
        untouched_kernel,
        out_shape=jax.ShapeDtypeStruct(shard.shape, shard.dtype),
        in_specs=[anywhere, pl.BlockSpec(memory_space=pltpu.VMEM)],
        out_specs=anywhere,
        input_output_aliases={0: 0},
        name="after_in_place",
    )(shard, done)


def per_device(record, whitening, offsets, window_valid):
    devices = lax.axis_size("tm")
    blocks = lax.axis_size("chan")
    stacked = blocks & (blocks - 1) != 0 or record.shape[0] % 128 != 0
    top = blocks // 2
    bins = BINS // devices

    def exchanged(chunk):
        return lax.all_to_all(chunk, "tm", split_axis=0, concat_axis=0, tiled=True)

    def fanned(shard):
        held = fan(shard, "chan", top // 2)
        return [held[n] for n in range(top)]

    inbox = from_behind(outbox(record, offsets, window_valid), "tm", 1)
    transform, rise, fall = tables(whitening)
    parts, done = border_parts(record, inbox, transform, rise, fall)
    parts = from_behind(parts, "tm", -1)
    views = record, inbox, offsets, window_valid, transform, rise, fall
    (early,), _ = own_spectra(*views, done, devices, 0)
    late, done = own_spectra(*views, parts, devices, 1)
    early = after(exchanged(early), done)
    result, begin, rest = None, 0, []
    near_early = None if stacked else fanned(early)
    far_early = None if stacked else swapped(early, "chan", top)
    for p, chunk in enumerate(late):
        mine = exchanged(chunk)
        if stacked:
            left, _ = left_sides(early, mine, begin, done)
            both = [lax.all_gather(one, "chan", axis=0, tiled=False) for one in (early, mine)]
            result, _ = cross_products(left, *both, result, begin, bins, blocks, None)
        else:
            mine = after(mine, done) if p else mine
            far, near = swapped(mine, "chan", top), fanned(mine)
            left, _ = left_sides(early, mine, begin, done)
            result, done = cross_products(left, near_early, near, result, begin, bins, blocks, 0)
            rest.append((left, far, begin))
        begin += mine.shape[1]
    if not stacked:
        far_early = fanned(after_in_place(far_early, done))
        for left, far, begin in rest:
            far = fanned(after(far, done))
            result, done = cross_products(left, far_early, far, result, begin, bins, blocks, 1)
    return result


def solution(mesh):
    in_specs = (P("chan", "tm"), P(), P("tm"), P("tm"))
    out_specs = P("tm", None, "chan", None)
    return jax.shard_map(
        per_device, mesh=mesh, in_specs=in_specs, out_specs=out_specs, check_vma=False
    )
```

```python
import functools
import math

import jax
import jax.numpy as jnp
import numpy as np
from jax import lax
from jax.experimental import pallas as pl
from jax.experimental.pallas import tpu as pltpu
from jax.sharding import PartitionSpec as P

L = 2048
HOP = 512
JITTER = 256
TAPS = 65
BINS = 64
K0 = 64
RIM = 128
GROUP = L // HOP
EDGE = RIM + JITTER
LANES = 2 * BINS
MIB = 1 << 20
F32 = jnp.float32
BF16 = jnp.bfloat16


def from_behind(shard, axis, by):
    devices = lax.axis_size(axis)
    pairs = [(i, i + by) for i in range(devices) if 0 <= i + by < devices]
    return lax.ppermute(shard, axis, pairs)


def phase_table():
    sample = np.arange(L) - (TAPS - 1)
    angles = 2.0 * np.pi * np.mod(sample[:, None] * (K0 + np.arange(BINS))[None, :], L) / L
    return (np.concatenate([np.cos(angles), -np.sin(angles)], axis=1) / math.sqrt(L)).astype(np.float32)


def matmul(a, b):
    return jnp.dot(a, b, preferred_element_type=F32)


def turn(values, place):
    lane = lax.broadcasted_iota(jnp.int32, (8, LANES), 1)
    bins = K0 + (lane & (BINS - 1))
    angles = ((bins * (place + L)) & (L - 1)).astype(F32) * (2.0 * math.pi / L)
    sine = jnp.sin(angles)
    sine = jnp.where(lane < BINS, -sine, sine)
    return values * jnp.cos(angles)[:1] + pltpu.roll(values, BINS, 1) * sine[:1]


def edge_table(rise, fall, offset):
    start = JITTER - offset
    return jnp.concatenate([rise[pl.ds(start, RIM), :], fall[pl.ds(start, JITTER), :]], axis=0).astype(BF16)


def across(values):
    channels = values.shape[0]
    if channels % 128:
        values = jnp.pad(values, ((0, 128 - channels), (0, 0)))
    return values.T


def outbox_kernel(offsets, valid, record, out):
    top = record[0:8, :]
    row = lax.broadcasted_iota(jnp.int32, top.shape, 0)
    lane = lax.broadcasted_iota(jnp.int32, top.shape, 1)
    first = offsets.shape[0] - GROUP
    for q in range(GROUP):
        top = jnp.where((row == 0) & (lane == q), offsets[first + q].astype(F32), top)
        top = jnp.where((row == 0) & (lane == GROUP + q), valid[first + q].astype(F32), top)
    out[...] = jnp.concatenate([top, record[8:, :]], axis=0).astype(BF16)


def outbox(record, offsets, valid):
    channels, slab = record.shape
    smem = pl.BlockSpec(memory_space=pltpu.SMEM)
    return pl.pallas_call(
        outbox_kernel,
        grid=(1,),
        out_shape=jax.ShapeDtypeStruct((channels, RIM), BF16),
        in_specs=[smem, smem, pl.BlockSpec((channels, RIM), lambda i: (0, slab // RIM - 1))],
        out_specs=pl.BlockSpec(memory_space=pltpu.VMEM),
        compiler_params=pltpu.CompilerParams(vmem_limit_bytes=60 * MIB),
        name="outbox",
    )(offsets, valid, record)


def tables_kernel(taps, table, blocks, rise, fall, padded):
    padded[0 : TAPS - 1, :] = jnp.zeros((TAPS - 1, LANES), F32)
    padded[TAPS - 1 :, :] = table[TAPS - 1 : TAPS - 1 + padded.shape[0] - (TAPS - 1), :]
    ramp = jnp.zeros((TAPS - 1, LANES), F32)
    gain = jnp.zeros((1, LANES), F32)
    for m in range(TAPS):
        tap = taps[m]
        ramp = ramp + tap * padded[m : m + TAPS - 1, :]
        gain = gain + tap * padded[TAPS - 1 + m : TAPS + m, :]
    gain = jnp.broadcast_to(gain * math.sqrt(L), (8, LANES))
    lane = lax.broadcasted_iota(jnp.int32, (8, LANES), 1)
    swapped = pltpu.roll(gain, BINS, 1)
    gain_re = jnp.where(lane < BINS, gain, swapped)[:1]
    gain_im = jnp.where(lane < BINS, -swapped, gain)[:1]
    columns = table[...]
    pure = columns * gain_re + pltpu.roll(columns, BINS, 1) * gain_im
    blocks[...] = pure.astype(BF16)
    rise[...] = jnp.zeros_like(rise)
    rise[rise.shape[0] - (TAPS - 1) :, :] = -ramp
    ahead = JITTER - (TAPS - 1)
    fall[0:ahead, :] = pure[L - ahead :]
    fall[ahead:JITTER, :] = pure[: TAPS - 1] - ramp
    fall[JITTER:, :] = jnp.zeros((fall.shape[0] - JITTER, LANES), F32)


def tables(whitening):
    vmem = pl.BlockSpec(memory_space=pltpu.VMEM)
    return pl.pallas_call(
        tables_kernel,
        out_shape=(
            jax.ShapeDtypeStruct((L, LANES), BF16),
            jax.ShapeDtypeStruct((EDGE, LANES), F32),
            jax.ShapeDtypeStruct((2 * JITTER, LANES), F32),
        ),
        in_specs=[pl.BlockSpec(memory_space=pltpu.SMEM), vmem],
        out_specs=(vmem, vmem, vmem),
        scratch_shapes=[pltpu.VMEM((2 * TAPS + 6, LANES), F32)],
        compiler_params=pltpu.CompilerParams(vmem_limit_bytes=16 * MIB),
        name="tables",
    )(whitening, phase_table())


def border_kernel(inbox, record, blocks, rise, fall, parts, done, collected):
    channels = record.shape[0]
    done[...] = jnp.zeros_like(done)
    head = inbox[0:16, :].astype(F32)[:1]
    lane = lax.broadcasted_iota(jnp.int32, (1, LANES), 1)

    def told(at):
        return jnp.sum(jnp.where(lane == at, head, 0.0)).astype(jnp.int32)

    before = jnp.zeros((channels, LANES), F32)
    for q in range(GROUP):
        offset = told(q)
        edges = edge_table(rise, fall, offset)
        if q == 0:
            part = matmul(record[:, 0:JITTER].astype(BF16), edges[RIM:])
        else:
            part = matmul(record[:, HOP * q - RIM : HOP * q + JITTER].astype(BF16), edges)
        place = HOP * q + offset - (TAPS - 1)
        part = (part + turn(before, place)) * told(GROUP + q).astype(F32)
        upright = across(part)
        for c in range(collected.shape[0]):
            piece = upright[:, 128 * c : 128 * c + 128]
            collected[c, pl.ds(q, BINS, stride=2 * GROUP), :] = piece[:BINS]
            collected[c, pl.ds(GROUP + q, BINS, stride=2 * GROUP), :] = piece[BINS:]
        if q < GROUP - 1:
            before = before + matmul(
                record[:, HOP * q : HOP * q + HOP].astype(BF16), blocks[HOP * q : HOP * q + HOP, :]
            )
    width = min(128, channels)
    for c in range(collected.shape[0]):
        block = collected[c].reshape(BINS, 2 * GROUP, 128).astype(BF16)
        parts[:, :, width * c : width * c + width] = block[:, :, :width]


def border_parts(record, inbox, blocks, rise, fall):
    channels = record.shape[0]
    vmem = pl.BlockSpec(memory_space=pltpu.VMEM)
    lead = L - HOP + JITTER
    return pl.pallas_call(
        border_kernel,
        grid=(1,),
        out_shape=(jax.ShapeDtypeStruct((BINS, 2 * GROUP, channels), BF16), jax.ShapeDtypeStruct((8, 128), F32)),
        in_specs=[vmem, pl.BlockSpec((channels, lead), lambda i: (0, 0)), vmem, vmem, vmem],
        out_specs=(vmem, vmem),
        scratch_shapes=[pltpu.VMEM((max(channels // 128, 1), 2 * GROUP * BINS, 128), F32)],
        compiler_params=pltpu.CompilerParams(vmem_limit_bytes=50 * MIB),
        cost_estimate=pl.CostEstimate(
            flops=2 * channels * LANES * 3072, bytes_accessed=4 * channels * lead, transcendentals=0
        ),
        name="border_parts",
    )(inbox, record, blocks, rise, fall)


def spectra_kernel(offsets, valid, record, rim, blocks, rise, fall, order, out, samples, later, collected, sems):
    channels, slab = record.shape
    steps = slab // L
    windows = GROUP * steps

    def fetch(s):
        return pltpu.make_async_copy(
            record.at[:, pl.ds(L * s, L)], samples.at[:, pl.ds(RIM + L * s, L)], sems.at[s]
        )

    for s in range(steps):
        fetch(s).start()
    samples[:, 0:RIM] = rim[...].astype(F32)
    samples[:, RIM + slab :] = jnp.zeros((channels, samples.shape[1] - RIM - slab), F32)

    def block_sums(s):
        found = []
        for i in range(GROUP):
            begin = pl.multiple_of(RIM + L * s + HOP * i, 128)
            found.append(
                matmul(samples[:, pl.ds(begin, HOP)].astype(BF16), blocks[HOP * i : HOP * i + HOP, :])
            )
        return found

    def keep(found):
        total = found[GROUP - 1]
        later[GROUP - 1] = total
        for q in range(GROUP - 2, -1, -1):
            total = total + found[q]
            later[q] = total

    def one_window(w, q, before):
        offset = offsets[w]
        begin = pl.multiple_of(HOP * w, 128)
        ends = samples[:, pl.ds(begin + L, EDGE)] - samples[:, pl.ds(begin, EDGE)]
        part = matmul(ends.astype(BF16), edge_table(rise, fall, offset))
        total = later[q] if before is None else later[q] + before
        part = (part + turn(total, HOP * q + offset - (TAPS - 1))) * valid[w].astype(F32)
        upright = across(part)
        for c in range(collected.shape[0]):
            piece = upright[:, 128 * c : 128 * c + 128]
            collected[c, pl.ds(w, BINS, stride=2 * windows), :] = piece[:BINS]
            collected[c, pl.ds(windows + w, BINS, stride=2 * windows), :] = piece[BINS:]

    fetch(0).wait()
    keep(block_sums(0))

    @pl.loop(0, steps - 1)
    def _(s):
        fetch(s + 1).wait()
        found = block_sums(s + 1)
        before = None
        for q in range(GROUP):
            one_window(GROUP * s + q, q, before)
            before = found[q] if before is None else before + found[q]
        keep(found)

    for q in range(GROUP):
        one_window(GROUP * (steps - 1) + q, q, None)

    width = min(128, channels)
    for c in range(collected.shape[0]):
        block = collected[c].reshape(BINS, 2 * windows, 128).astype(BF16)
        out[:, :, width * c : width * c + width] = block[:, :, :width]


def own_spectra(record, rim, offsets, valid, transform, rise, fall, order):
    channels, slab = record.shape
    windows = offsets.shape[0]
    smem = pl.BlockSpec(memory_space=pltpu.SMEM)
    vmem = pl.BlockSpec(memory_space=pltpu.VMEM)
    return pl.pallas_call(
        spectra_kernel,
        out_shape=jax.ShapeDtypeStruct((BINS, 2 * windows, channels), BF16),
        in_specs=[smem, smem, pl.BlockSpec(memory_space=pl.ANY), vmem, vmem, vmem, vmem, vmem],
        out_specs=vmem,
        scratch_shapes=[
            pltpu.VMEM((channels, RIM + slab + L - HOP + JITTER), F32),
            pltpu.VMEM((GROUP, channels, LANES), F32),
            pltpu.VMEM((max(channels // 128, 1), LANES * windows, 128), F32),
            pltpu.SemaphoreType.DMA((slab // L,)),
        ],
        compiler_params=pltpu.CompilerParams(vmem_limit_bytes=50 * MIB),
        cost_estimate=pl.CostEstimate(
            flops=2 * channels * LANES * 896 * windows, bytes_accessed=4 * channels * slab, transcendentals=0
        ),
        name="own_spectra",
    )(offsets, valid, record, rim, transform, rise, fall, order)


def with_parts(block, part):
    windows = block.shape[1] // 2
    row = lax.broadcasted_iota(jnp.int32, part.shape, 1)
    moved = jnp.concatenate([part[:, GROUP:], part[:, :GROUP]], axis=1)
    pieces = []
    for ri, extra in enumerate((moved, part)):
        end = windows * ri + windows
        pieces.append(block[:, windows * ri : end - 2 * GROUP])
        pieces.append(block[:, end - 2 * GROUP : end] + jnp.where(row >= GROUP, extra, 0.0))
    return jnp.concatenate(pieces, axis=1)


def join_kernel(own, parts, *chunks):
    devices = chunks[0].shape[0]
    for group in range(devices):
        begin = group * BINS // devices
        end = begin + BINS // devices
        joined = with_parts(own[begin:end].astype(F32), parts[begin:end].astype(F32)).astype(BF16)
        at = 0
        for chunk in chunks:
            chunk[group] = joined[at : at + chunk.shape[1]]
            at += chunk.shape[1]


def chunk_sizes(bins):
    count = min(3, bins)
    return [(bins + count - 1 - c) // count for c in range(count)]


def joined_chunks(own, parts, devices):
    _, rows, channels = own.shape
    vmem = pl.BlockSpec(memory_space=pltpu.VMEM)
    shapes = [(devices, count, rows, channels) for count in chunk_sizes(BINS // devices)]
    return pl.pallas_call(
        join_kernel,
        out_shape=tuple(jax.ShapeDtypeStruct(shape, BF16) for shape in shapes),
        in_specs=[vmem, vmem],
        out_specs=(vmem,) * len(shapes),
        compiler_params=pltpu.CompilerParams(vmem_limit_bytes=16 * MIB),
        name="joined_chunks",
    )(own, parts)


def left_kernel(own, out):
    sources, _, rows, channels = own.shape
    depth = sources * rows
    half = rows // 2
    straight = own[:, 0].astype(F32)
    turned = jnp.concatenate([straight[:, half:], -straight[:, :half]], axis=1)
    out[0, :channels] = straight.reshape(depth, channels).T.astype(BF16)
    out[0, channels:] = turned.reshape(depth, channels).T.astype(BF16)


def left_sides(own):
    sources, count, rows, channels = own.shape
    shape = (count, 2 * channels, sources * rows)
    return pl.pallas_call(
        left_kernel,
        grid=(count,),
        out_shape=jax.ShapeDtypeStruct(shape, BF16),
        in_specs=[pl.BlockSpec((sources, 1, rows, channels), lambda f: (0, f, 0, 0))],
        out_specs=pl.BlockSpec((1,) + shape[1:], lambda f: (f, 0, 0)),
        compiler_params=pltpu.CompilerParams(vmem_limit_bytes=16 * MIB),
        name="left_sides",
    )(own)


def cross_kernel(scale, side, me, left, *rest):
    out, done = rest[-2:]
    done[...] = jnp.zeros_like(done)
    sources, _, rows, channels = rest[0].shape[-4:]
    blocks = out.shape[3] // channels
    tile = min(256, channels)
    for n in range(blocks):
        if side is None:
            right, at = rest[0][n], channels * n
        else:
            right, at = rest[n][...], pl.multiple_of(channels * ((me[0] ^ n) & (blocks - 1)), 128)
        right = right[:, 0].reshape(sources * rows, channels)
        for j in range(0, channels, tile):
            for r in range(0, 2 * channels, tile):
                both = matmul(left[0, r : r + tile, :], right[:, j : j + tile]) * scale
                out[0, r // channels, r % channels : r % channels + tile, pl.ds(at + j, tile)] = both.astype(BF16)


def cross_products(left, right, result, begin, bins, blocks, side):
    sources, count, rows, channels = (right if side is None else right[0]).shape[-4:]
    columns = blocks if side is None else len(right)
    shape = (bins, 2, channels, blocks * channels)
    operands = [lax.axis_index("chan").astype(jnp.int32).reshape(1), left]
    in_specs = [pl.BlockSpec((1,) + left.shape[1:], lambda f, me: (f, 0, 0))]
    if side is None:
        operands.append(right)
        in_specs.append(pl.BlockSpec((blocks, sources, 1, rows, channels), lambda f, me: (0, 0, f, 0, 0)))
    else:
        operands += right
        in_specs += [pl.BlockSpec((sources, 1, rows, channels), lambda f, me: (0, f, 0, 0))] * columns
    if result is None:
        result, aliases = operands[1], {}
    else:
        aliases = {len(operands): 0}
    operands.append(result)
    in_specs.append(pl.BlockSpec(memory_space=pl.ANY))

    def place(f, me):
        return begin + f, 0, 0, 0 if side is None else (me[0] // columns) ^ side

    return pl.pallas_call(
        functools.partial(cross_kernel, 2.0 / (sources * rows), side),
        grid_spec=pltpu.PrefetchScalarGridSpec(
            num_scalar_prefetch=1,
            grid=(count,),
            in_specs=in_specs,
            out_specs=(
                pl.BlockSpec((1, 2, channels, columns * channels), place),
                pl.BlockSpec((8, 128), lambda f, me: (0, 0)),
            ),
        ),
        out_shape=(jax.ShapeDtypeStruct(shape, BF16), jax.ShapeDtypeStruct((8, 128), F32)),
        input_output_aliases=aliases,
        compiler_params=pltpu.CompilerParams(vmem_limit_bytes=24 * MIB),
        cost_estimate=pl.CostEstimate(
            flops=4 * count * channels * columns * channels * sources * rows,
            bytes_accessed=4 * count * channels * columns * channels,
            transcendentals=0,
        ),
        name="cross_products",
    )(*operands)


def swapped(shard, axis, bit):
    devices = lax.axis_size(axis)
    return lax.ppermute(shard, axis, [(i, i ^ bit) for i in range(devices)])


def fan(shard, axis, bit):
    held = {0: shard}
    while bit:
        held.update({n | bit: swapped(block, axis, bit) for n, block in list(held.items())})
        bit //= 2
    return held


def after_kernel(shard, done, out):
    out[...] = shard[...]


def after(shard, done):
    if done is None:
        return shard
    vmem = pl.BlockSpec(memory_space=pltpu.VMEM)
    return pl.pallas_call(
        after_kernel,
        out_shape=jax.ShapeDtypeStruct(shard.shape, shard.dtype),
        in_specs=[vmem, vmem],
        out_specs=vmem,
        compiler_params=pltpu.CompilerParams(vmem_limit_bytes=8 * MIB),
        name="after",
    )(shard, done)


def per_device(record, whitening, offsets, window_valid):
    devices = lax.axis_size("tm")
    blocks = lax.axis_size("chan")
    stacked = blocks & (blocks - 1) != 0 or record.shape[0] % 128 != 0
    top = blocks // 2
    bins = BINS // devices

    def exchanged(chunk):
        return lax.all_to_all(chunk, "tm", split_axis=0, concat_axis=0, tiled=True)

    def fanned(shard):
        held = fan(shard, "chan", top // 2)
        return [held[n] for n in range(top)]

    inbox = from_behind(outbox(record, offsets, window_valid), "tm", 1)
    transform, rise, fall = tables(whitening)
    parts, done = border_parts(record, inbox, transform, rise, fall)
    parts = from_behind(parts, "tm", -1)
    own = own_spectra(record, inbox, offsets, window_valid, transform, rise, fall, done)
    chunks = joined_chunks(own, parts, devices)
    begins = [sum(chunk.shape[1] for chunk in chunks[:p]) for p in range(len(chunks))]
    result, near, far, left, done = None, [], [], [], None

    def cross(p, side):
        right = near[p] if side == 0 else far[p]
        return cross_products(left[p], right, result, begins[p], bins, blocks, side)

    for p, chunk in enumerate(chunks):
        mine = exchanged(chunk)
        if stacked:
            right = lax.all_gather(mine, "chan", axis=0, tiled=False)
            result, _ = cross_products(left_sides(mine), right, result, begins[p], bins, blocks, None)
            continue
        mine = after(mine, done)
        far.append(swapped(mine, "chan", top))
        near.append(fanned(mine))
        left.append(left_sides(mine))
        if p == 1:
            far[0] = after(far[0], mine)
        result, done = cross(p, 0)
        if p:
            far[p - 1] = fanned(far[p - 1])
            result, done = cross(p - 1, 1)
    if not stacked:
        far[-1] = fanned(after(far[-1], done))
        result, _ = cross(len(chunks) - 1, 1)
    return result


def solution(mesh):
    in_specs = (P("chan", "tm"), P(), P("tm"), P("tm"))
    out_specs = P("tm", None, "chan", None)
    return jax.shard_map(
        per_device, mesh=mesh, in_specs=in_specs, out_specs=out_specs, check_vma=False
    )
```

```python
import functools
import math

import jax
import jax.numpy as jnp
import numpy as np
from jax import lax
from jax.experimental import pallas as pl
from jax.experimental.pallas import tpu as pltpu
from jax.sharding import PartitionSpec as P

L = 2048
HOP = 512
JITTER = 256
TAPS = 65
BINS = 64
K0 = 64
RIM = 128
GROUP = L // HOP
EDGE = RIM + JITTER
LANES = 2 * BINS
MIB = 1 << 20
F32 = jnp.float32
BF16 = jnp.bfloat16


def from_behind(shard, axis, by):
    devices = lax.axis_size(axis)
    pairs = [(i, i + by) for i in range(devices) if 0 <= i + by < devices]
    return lax.ppermute(shard, axis, pairs)


def phase_table():
    sample = np.arange(L) - (TAPS - 1)
    angles = 2.0 * np.pi * np.mod(sample[:, None] * (K0 + np.arange(BINS))[None, :], L) / L
    return (np.concatenate([np.cos(angles), -np.sin(angles)], axis=1) / math.sqrt(L)).astype(np.float32)


def matmul(a, b):
    return jnp.dot(a, b, preferred_element_type=F32)


def turn(values, place):
    lane = lax.broadcasted_iota(jnp.int32, (8, LANES), 1)
    bins = K0 + (lane & (BINS - 1))
    angles = ((bins * (place + L)) & (L - 1)).astype(F32) * (2.0 * math.pi / L)
    sine = jnp.sin(angles)
    sine = jnp.where(lane < BINS, -sine, sine)
    return values * jnp.cos(angles)[:1] + pltpu.roll(values, BINS, 1) * sine[:1]


def edge_table(rise, fall, offset):
    start = JITTER - offset
    return jnp.concatenate([rise[pl.ds(start, RIM), :], fall[pl.ds(start, JITTER), :]], axis=0).astype(BF16)


def across(values):
    channels = values.shape[0]
    if channels % 128:
        values = jnp.pad(values, ((0, 128 - channels), (0, 0)))
    return values.T


def outbox_kernel(offsets, valid, record, out):
    top = record[0:8, :]
    row = lax.broadcasted_iota(jnp.int32, top.shape, 0)
    lane = lax.broadcasted_iota(jnp.int32, top.shape, 1)
    first = offsets.shape[0] - GROUP
    for q in range(GROUP):
        top = jnp.where((row == 0) & (lane == q), offsets[first + q].astype(F32), top)
        top = jnp.where((row == 0) & (lane == GROUP + q), valid[first + q].astype(F32), top)
    out[...] = jnp.concatenate([top, record[8:, :]], axis=0).astype(BF16)


def outbox(record, offsets, valid):
    channels, slab = record.shape
    smem = pl.BlockSpec(memory_space=pltpu.SMEM)
    return pl.pallas_call(
        outbox_kernel,
        grid=(1,),
        out_shape=jax.ShapeDtypeStruct((channels, RIM), BF16),
        in_specs=[smem, smem, pl.BlockSpec((channels, RIM), lambda i: (0, slab // RIM - 1))],
        out_specs=pl.BlockSpec(memory_space=pltpu.VMEM),
        compiler_params=pltpu.CompilerParams(vmem_limit_bytes=60 * MIB),
        name="outbox",
    )(offsets, valid, record)


def tables_kernel(taps, table, blocks, rise, fall, padded):
    padded[0 : TAPS - 1, :] = jnp.zeros((TAPS - 1, LANES), F32)
    padded[TAPS - 1 :, :] = table[TAPS - 1 : TAPS - 1 + padded.shape[0] - (TAPS - 1), :]
    ramp = jnp.zeros((TAPS - 1, LANES), F32)
    gain = jnp.zeros((1, LANES), F32)
    for m in range(TAPS):
        tap = taps[m]
        ramp = ramp + tap * padded[m : m + TAPS - 1, :]
        gain = gain + tap * padded[TAPS - 1 + m : TAPS + m, :]
    gain = jnp.broadcast_to(gain * math.sqrt(L), (8, LANES))
    lane = lax.broadcasted_iota(jnp.int32, (8, LANES), 1)
    swapped = pltpu.roll(gain, BINS, 1)
    gain_re = jnp.where(lane < BINS, gain, swapped)[:1]
    gain_im = jnp.where(lane < BINS, -swapped, gain)[:1]
    columns = table[...]
    pure = columns * gain_re + pltpu.roll(columns, BINS, 1) * gain_im
    blocks[...] = pure.astype(BF16)
    rise[...] = jnp.zeros_like(rise)
    rise[rise.shape[0] - (TAPS - 1) :, :] = -ramp
    ahead = JITTER - (TAPS - 1)
    fall[0:ahead, :] = pure[L - ahead :]
    fall[ahead:JITTER, :] = pure[: TAPS - 1] - ramp
    fall[JITTER:, :] = jnp.zeros((fall.shape[0] - JITTER, LANES), F32)


def tables(whitening):
    vmem = pl.BlockSpec(memory_space=pltpu.VMEM)
    return pl.pallas_call(
        tables_kernel,
        out_shape=(
            jax.ShapeDtypeStruct((L, LANES), BF16),
            jax.ShapeDtypeStruct((EDGE, LANES), F32),
            jax.ShapeDtypeStruct((2 * JITTER, LANES), F32),
        ),
        in_specs=[pl.BlockSpec(memory_space=pltpu.SMEM), vmem],
        out_specs=(vmem, vmem, vmem),
        scratch_shapes=[pltpu.VMEM((2 * TAPS + 6, LANES), F32)],
        compiler_params=pltpu.CompilerParams(vmem_limit_bytes=16 * MIB),
        name="tables",
    )(whitening, phase_table())


def border_kernel(inbox, record, blocks, rise, fall, parts, done, collected):
    channels = record.shape[0]
    done[...] = jnp.zeros_like(done)
    head = inbox[0:16, :].astype(F32)[:1]
    lane = lax.broadcasted_iota(jnp.int32, (1, LANES), 1)

    def told(at):
        return jnp.sum(jnp.where(lane == at, head, 0.0)).astype(jnp.int32)

    before = jnp.zeros((channels, LANES), F32)
    for q in range(GROUP):
        offset = told(q)
        edges = edge_table(rise, fall, offset)
        if q == 0:
            part = matmul(record[:, 0:JITTER].astype(BF16), edges[RIM:])
        else:
            part = matmul(record[:, HOP * q - RIM : HOP * q + JITTER].astype(BF16), edges)
        place = HOP * q + offset - (TAPS - 1)
        part = (part + turn(before, place)) * told(GROUP + q).astype(F32)
        upright = across(part)
        for c in range(collected.shape[0]):
            piece = upright[:, 128 * c : 128 * c + 128]
            collected[c, pl.ds(q, BINS, stride=2 * GROUP), :] = piece[:BINS]
            collected[c, pl.ds(GROUP + q, BINS, stride=2 * GROUP), :] = piece[BINS:]
        if q < GROUP - 1:
            before = before + matmul(
                record[:, HOP * q : HOP * q + HOP].astype(BF16), blocks[HOP * q : HOP * q + HOP, :]
            )
    width = min(128, channels)
    for c in range(collected.shape[0]):
        block = collected[c].reshape(BINS, 2 * GROUP, 128).astype(BF16)
        parts[:, :, width * c : width * c + width] = block[:, :, :width]


def border_parts(record, inbox, blocks, rise, fall):
    channels = record.shape[0]
    vmem = pl.BlockSpec(memory_space=pltpu.VMEM)
    lead = L - HOP + JITTER
    return pl.pallas_call(
        border_kernel,
        grid=(1,),
        out_shape=(jax.ShapeDtypeStruct((BINS, 2 * GROUP, channels), BF16), jax.ShapeDtypeStruct((8, 128), F32)),
        in_specs=[vmem, pl.BlockSpec((channels, lead), lambda i: (0, 0)), vmem, vmem, vmem],
        out_specs=(vmem, vmem),
        scratch_shapes=[pltpu.VMEM((max(channels // 128, 1), 2 * GROUP * BINS, 128), F32)],
        compiler_params=pltpu.CompilerParams(vmem_limit_bytes=50 * MIB),
        cost_estimate=pl.CostEstimate(
            flops=2 * channels * LANES * 3072, bytes_accessed=4 * channels * lead, transcendentals=0
        ),
        name="border_parts",
    )(inbox, record, blocks, rise, fall)


def spectra_kernel(offsets, valid, record, rim, blocks, rise, fall, order, out, samples, later, collected, sems):
    channels, slab = record.shape
    steps = slab // L
    windows = GROUP * steps

    def fetch(s):
        return pltpu.make_async_copy(
            record.at[:, pl.ds(L * s, L)], samples.at[:, pl.ds(RIM + L * s, L)], sems.at[s]
        )

    for s in range(steps):
        fetch(s).start()
    samples[:, 0:RIM] = rim[...].astype(F32)
    samples[:, RIM + slab :] = jnp.zeros((channels, samples.shape[1] - RIM - slab), F32)

    def block_sums(s):
        found = []
        for i in range(GROUP):
            begin = pl.multiple_of(RIM + L * s + HOP * i, 128)
            found.append(
                matmul(samples[:, pl.ds(begin, HOP)].astype(BF16), blocks[HOP * i : HOP * i + HOP, :])
            )
        return found

    def keep(found):
        total = found[GROUP - 1]
        later[GROUP - 1] = total
        for q in range(GROUP - 2, -1, -1):
            total = total + found[q]
            later[q] = total

    def one_window(w, q, before):
        offset = offsets[w]
        begin = pl.multiple_of(HOP * w, 128)
        ends = samples[:, pl.ds(begin + L, EDGE)] - samples[:, pl.ds(begin, EDGE)]
        part = matmul(ends.astype(BF16), edge_table(rise, fall, offset))
        total = later[q] if before is None else later[q] + before
        part = (part + turn(total, HOP * q + offset - (TAPS - 1))) * valid[w].astype(F32)
        upright = across(part)
        for c in range(collected.shape[0]):
            collected[c, pl.ds(w, LANES, stride=windows), :] = upright[:, 128 * c : 128 * c + 128]

    fetch(0).wait()
    keep(block_sums(0))

    @pl.loop(0, steps - 1)
    def _(s):
        fetch(s + 1).wait()
        found = block_sums(s + 1)
        before = None
        for q in range(GROUP):
            one_window(GROUP * s + q, q, before)
            before = found[q] if before is None else before + found[q]
        keep(found)

    for q in range(GROUP):
        one_window(GROUP * (steps - 1) + q, q, None)

    width = min(128, channels)
    for c in range(collected.shape[0]):
        block = collected[c].reshape(LANES, windows, 128).astype(BF16)
        for ri in range(2):
            part = block[BINS * ri : BINS * ri + BINS, :, :width]
            out[:, windows * ri : windows * ri + windows, width * c : width * c + width] = part


def own_spectra(record, rim, offsets, valid, transform, rise, fall, order):
    channels, slab = record.shape
    windows = offsets.shape[0]
    smem = pl.BlockSpec(memory_space=pltpu.SMEM)
    vmem = pl.BlockSpec(memory_space=pltpu.VMEM)
    return pl.pallas_call(
        spectra_kernel,
        out_shape=jax.ShapeDtypeStruct((BINS, 2 * windows, channels), BF16),
        in_specs=[smem, smem, pl.BlockSpec(memory_space=pl.ANY), vmem, vmem, vmem, vmem, vmem],
        out_specs=vmem,
        scratch_shapes=[
            pltpu.VMEM((channels, RIM + slab + L - HOP + JITTER), F32),
            pltpu.VMEM((GROUP, channels, LANES), F32),
            pltpu.VMEM((max(channels // 128, 1), LANES * windows, 128), F32),
            pltpu.SemaphoreType.DMA((slab // L,)),
        ],
        compiler_params=pltpu.CompilerParams(vmem_limit_bytes=50 * MIB),
        cost_estimate=pl.CostEstimate(
            flops=2 * channels * LANES * 896 * windows, bytes_accessed=4 * channels * slab, transcendentals=0
        ),
        name="own_spectra",
    )(offsets, valid, record, rim, transform, rise, fall, order)


def with_parts(block, part):
    windows = block.shape[1] // 2
    row = lax.broadcasted_iota(jnp.int32, part.shape, 1)
    moved = jnp.concatenate([part[:, GROUP:], part[:, :GROUP]], axis=1)
    pieces = []
    for ri, extra in enumerate((moved, part)):
        end = windows * ri + windows
        pieces.append(block[:, windows * ri : end - 2 * GROUP])
        pieces.append(block[:, end - 2 * GROUP : end] + jnp.where(row >= GROUP, extra, 0.0))
    return jnp.concatenate(pieces, axis=1)


def join_kernel(own, parts, *chunks):
    devices = chunks[0].shape[0]
    for group in range(devices):
        begin = group * BINS // devices
        end = begin + BINS // devices
        joined = with_parts(own[begin:end].astype(F32), parts[begin:end].astype(F32)).astype(BF16)
        at = 0
        for chunk in chunks:
            chunk[group] = joined[at : at + chunk.shape[1]]
            at += chunk.shape[1]


def chunk_sizes(bins):
    count = min(3, bins)
    return [(bins + count - 1 - c) // count for c in range(count)]


def joined_chunks(own, parts, devices):
    _, rows, channels = own.shape
    vmem = pl.BlockSpec(memory_space=pltpu.VMEM)
    shapes = [(devices, count, rows, channels) for count in chunk_sizes(BINS // devices)]
    return pl.pallas_call(
        join_kernel,
        out_shape=tuple(jax.ShapeDtypeStruct(shape, BF16) for shape in shapes),
        in_specs=[vmem, vmem],
        out_specs=(vmem,) * len(shapes),
        compiler_params=pltpu.CompilerParams(vmem_limit_bytes=16 * MIB),
        name="joined_chunks",
    )(own, parts)


def left_kernel(own, out):
    sources, _, rows, channels = own.shape
    depth = sources * rows
    half = rows // 2
    straight = own[:, 0].astype(F32)
    turned = jnp.concatenate([straight[:, half:], -straight[:, :half]], axis=1)
    out[0, :channels] = straight.reshape(depth, channels).T.astype(BF16)
    out[0, channels:] = turned.reshape(depth, channels).T.astype(BF16)


def left_sides(own):
    sources, count, rows, channels = own.shape
    shape = (count, 2 * channels, sources * rows)
    return pl.pallas_call(
        left_kernel,
        grid=(count,),
        out_shape=jax.ShapeDtypeStruct(shape, BF16),
        in_specs=[pl.BlockSpec((sources, 1, rows, channels), lambda f: (0, f, 0, 0))],
        out_specs=pl.BlockSpec((1,) + shape[1:], lambda f: (f, 0, 0)),
        compiler_params=pltpu.CompilerParams(vmem_limit_bytes=16 * MIB),
        name="left_sides",
    )(own)


def cross_kernel(scale, side, me, left, *rest):
    out, done = rest[-2:]
    done[...] = jnp.zeros_like(done)
    sources, _, rows, channels = rest[0].shape[-4:]
    blocks = out.shape[3] // channels
    tile = min(256, channels)
    for n in range(blocks):
        if side is None:
            right, at = rest[0][n], channels * n
        else:
            right, at = rest[n][...], pl.multiple_of(channels * ((me[0] ^ n) & (blocks - 1)), 128)
        right = right[:, 0].reshape(sources * rows, channels)
        for j in range(0, channels, tile):
            for r in range(0, 2 * channels, tile):
                both = matmul(left[0, r : r + tile, :], right[:, j : j + tile]) * scale
                out[0, r // channels, r % channels : r % channels + tile, pl.ds(at + j, tile)] = both.astype(BF16)


def cross_products(left, right, result, begin, bins, blocks, side):
    sources, count, rows, channels = (right if side is None else right[0]).shape[-4:]
    columns = blocks if side is None else len(right)
    shape = (bins, 2, channels, blocks * channels)
    operands = [lax.axis_index("chan").astype(jnp.int32).reshape(1), left]
    in_specs = [pl.BlockSpec((1,) + left.shape[1:], lambda f, me: (f, 0, 0))]
    if side is None:
        operands.append(right)
        in_specs.append(pl.BlockSpec((blocks, sources, 1, rows, channels), lambda f, me: (0, 0, f, 0, 0)))
    else:
        operands += right
        in_specs += [pl.BlockSpec((sources, 1, rows, channels), lambda f, me: (0, f, 0, 0))] * columns
    if result is None:
        result, aliases = operands[1], {}
    else:
        aliases = {len(operands): 0}
    operands.append(result)
    in_specs.append(pl.BlockSpec(memory_space=pl.ANY))

    def place(f, me):
        return begin + f, 0, 0, 0 if side is None else (me[0] // columns) ^ side

    return pl.pallas_call(
        functools.partial(cross_kernel, 2.0 / (sources * rows), side),
        grid_spec=pltpu.PrefetchScalarGridSpec(
            num_scalar_prefetch=1,
            grid=(count,),
            in_specs=in_specs,
            out_specs=(
                pl.BlockSpec((1, 2, channels, columns * channels), place),
                pl.BlockSpec((8, 128), lambda f, me: (0, 0)),
            ),
        ),
        out_shape=(jax.ShapeDtypeStruct(shape, BF16), jax.ShapeDtypeStruct((8, 128), F32)),
        input_output_aliases=aliases,
        compiler_params=pltpu.CompilerParams(vmem_limit_bytes=24 * MIB),
        cost_estimate=pl.CostEstimate(
            flops=4 * count * channels * columns * channels * sources * rows,
            bytes_accessed=4 * count * channels * columns * channels,
            transcendentals=0,
        ),
        name="cross_products",
    )(*operands)


def swapped(shard, axis, bit):
    devices = lax.axis_size(axis)
    return lax.ppermute(shard, axis, [(i, i ^ bit) for i in range(devices)])


def fan(shard, axis, bit):
    held = {0: shard}
    while bit:
        held.update({n | bit: swapped(block, axis, bit) for n, block in list(held.items())})
        bit //= 2
    return held


def after_kernel(shard, done, out):
    out[...] = shard[...]


def after(shard, done):
    if done is None:
        return shard
    vmem = pl.BlockSpec(memory_space=pltpu.VMEM)
    return pl.pallas_call(
        after_kernel,
        out_shape=jax.ShapeDtypeStruct(shard.shape, shard.dtype),
        in_specs=[vmem, vmem],
        out_specs=vmem,
        compiler_params=pltpu.CompilerParams(vmem_limit_bytes=8 * MIB),
        name="after",
    )(shard, done)


def per_device(record, whitening, offsets, window_valid):
    devices = lax.axis_size("tm")
    blocks = lax.axis_size("chan")
    stacked = blocks & (blocks - 1) != 0 or record.shape[0] % 128 != 0
    top = blocks // 2
    bins = BINS // devices

    def exchanged(chunk):
        return lax.all_to_all(chunk, "tm", split_axis=0, concat_axis=0, tiled=True)

    def fanned(shard):
        held = fan(shard, "chan", top // 2)
        return [held[n] for n in range(top)]

    inbox = from_behind(outbox(record, offsets, window_valid), "tm", 1)
    transform, rise, fall = tables(whitening)
    parts, done = border_parts(record, inbox, transform, rise, fall)
    parts = from_behind(parts, "tm", -1)
    own = own_spectra(record, inbox, offsets, window_valid, transform, rise, fall, done)
    chunks = joined_chunks(own, parts, devices)
    begins = [sum(chunk.shape[1] for chunk in chunks[:p]) for p in range(len(chunks))]
    result, near, far, left, done = None, [], [], [], None

    def cross(p, side):
        right = near[p] if side == 0 else far[p]
        return cross_products(left[p], right, result, begins[p], bins, blocks, side)

    for p, chunk in enumerate(chunks):
        mine = exchanged(chunk)
        if stacked:
            right = lax.all_gather(mine, "chan", axis=0, tiled=False)
            result, _ = cross_products(left_sides(mine), right, result, begins[p], bins, blocks, None)
            continue
        mine = after(mine, done)
        far.append(swapped(mine, "chan", top))
        near.append(fanned(mine))
        left.append(left_sides(mine))
        ready = done
        result, done = cross(p, 0)
        if p:
            far[p - 1] = fanned(after(far[p - 1], ready) if p > 1 else far[p - 1])
            result, done = cross(p - 1, 1)
    if not stacked:
        far[-1] = fanned(after(far[-1], done))
        result, _ = cross(len(chunks) - 1, 1)
    return result


def solution(mesh):
    in_specs = (P("chan", "tm"), P(), P("tm"), P("tm"))
    out_specs = P("tm", None, "chan", None)
    return jax.shard_map(
        per_device, mesh=mesh, in_specs=in_specs, out_specs=out_specs, check_vma=False
    )
```

```python
import functools
import math

import jax
import jax.numpy as jnp
import numpy as np
from jax import lax
from jax.experimental import pallas as pl
from jax.experimental.pallas import tpu as pltpu
from jax.sharding import PartitionSpec as P

L = 2048
HOP = 512
JITTER = 256
TAPS = 65
BINS = 64
K0 = 64
RIM = 128
GROUP = L // HOP
EDGE = RIM + JITTER
LANES = 2 * BINS
MIB = 1 << 20
F32 = jnp.float32
BF16 = jnp.bfloat16


def from_behind(shard, axis, by):
    devices = lax.axis_size(axis)
    pairs = [(i, i + by) for i in range(devices) if 0 <= i + by < devices]
    return lax.ppermute(shard, axis, pairs)


def phase_table():
    sample = np.arange(L) - (TAPS - 1)
    angles = 2.0 * np.pi * np.mod(sample[:, None] * (K0 + np.arange(BINS))[None, :], L) / L
    return (np.concatenate([np.cos(angles), -np.sin(angles)], axis=1) / math.sqrt(L)).astype(np.float32)


def matmul(a, b):
    return jnp.dot(a, b, preferred_element_type=F32)


def rotations(places):
    rows = -(-len(places) // 8) * 8
    row = lax.broadcasted_iota(jnp.int32, (rows, LANES), 0)
    lane = lax.broadcasted_iota(jnp.int32, (rows, LANES), 1)
    place = jnp.zeros((rows, LANES), jnp.int32)
    for i, one in enumerate(places):
        place = jnp.where(row == i, one + L, place)
    bins = K0 + (lane & (BINS - 1))
    angles = ((bins * place) & (L - 1)).astype(F32) * (2.0 * math.pi / L)
    sine = jnp.sin(angles)
    return jnp.cos(angles), jnp.where(lane < BINS, -sine, sine)


def turn(values, cosine, sine):
    return values * cosine + pltpu.roll(values, BINS, 1) * sine


def edge_table(rise, fall, offset):
    start = JITTER - offset
    return jnp.concatenate([rise[pl.ds(start, RIM), :], fall[pl.ds(start, JITTER), :]], axis=0).astype(BF16)


def across(values):
    channels = values.shape[0]
    if channels % 128:
        values = jnp.pad(values, ((0, 128 - channels), (0, 0)))
    return values.T


def outbox_kernel(offsets, valid, record, out):
    top = record[0:8, :]
    row = lax.broadcasted_iota(jnp.int32, top.shape, 0)
    lane = lax.broadcasted_iota(jnp.int32, top.shape, 1)
    first = offsets.shape[0] - GROUP
    for q in range(GROUP):
        top = jnp.where((row == 0) & (lane == q), offsets[first + q].astype(F32), top)
        top = jnp.where((row == 0) & (lane == GROUP + q), valid[first + q].astype(F32), top)
    out[...] = jnp.concatenate([top, record[8:, :]], axis=0).astype(BF16)


def outbox(record, offsets, valid):
    channels, slab = record.shape
    smem = pl.BlockSpec(memory_space=pltpu.SMEM)
    return pl.pallas_call(
        outbox_kernel,
        grid=(1,),
        out_shape=jax.ShapeDtypeStruct((channels, RIM), BF16),
        in_specs=[smem, smem, pl.BlockSpec((channels, RIM), lambda i: (0, slab // RIM - 1))],
        out_specs=pl.BlockSpec(memory_space=pltpu.VMEM),
        compiler_params=pltpu.CompilerParams(vmem_limit_bytes=60 * MIB),
        name="outbox",
    )(offsets, valid, record)


def tables_kernel(taps, offsets, table, blocks, rise, fall, turns, padded):
    windows = offsets.shape[0]
    turns[0], turns[1] = rotations([HOP * w + offsets[w] - (TAPS - 1) for w in range(windows)])
    padded[0 : TAPS - 1, :] = jnp.zeros((TAPS - 1, LANES), F32)
    padded[TAPS - 1 :, :] = table[TAPS - 1 : TAPS - 1 + padded.shape[0] - (TAPS - 1), :]
    ramp = jnp.zeros((TAPS - 1, LANES), F32)
    gain = jnp.zeros((1, LANES), F32)
    for m in range(TAPS):
        tap = taps[m]
        ramp = ramp + tap * padded[m : m + TAPS - 1, :]
        gain = gain + tap * padded[TAPS - 1 + m : TAPS + m, :]
    gain = jnp.broadcast_to(gain * math.sqrt(L), (8, LANES))
    lane = lax.broadcasted_iota(jnp.int32, (8, LANES), 1)
    swapped = pltpu.roll(gain, BINS, 1)
    gain_re = jnp.where(lane < BINS, gain, swapped)[:1]
    gain_im = jnp.where(lane < BINS, -swapped, gain)[:1]
    columns = table[...]
    pure = columns * gain_re + pltpu.roll(columns, BINS, 1) * gain_im
    blocks[...] = pure.astype(BF16)
    rise[...] = jnp.zeros_like(rise)
    rise[rise.shape[0] - (TAPS - 1) :, :] = -ramp
    ahead = JITTER - (TAPS - 1)
    fall[0:ahead, :] = pure[L - ahead :]
    fall[ahead:JITTER, :] = pure[: TAPS - 1] - ramp
    fall[JITTER:, :] = jnp.zeros((fall.shape[0] - JITTER, LANES), F32)


def tables(whitening, offsets):
    smem = pl.BlockSpec(memory_space=pltpu.SMEM)
    vmem = pl.BlockSpec(memory_space=pltpu.VMEM)
    return pl.pallas_call(
        tables_kernel,
        out_shape=(
            jax.ShapeDtypeStruct((L, LANES), BF16),
            jax.ShapeDtypeStruct((EDGE, LANES), F32),
            jax.ShapeDtypeStruct((2 * JITTER, LANES), F32),
            jax.ShapeDtypeStruct((2, offsets.shape[0], LANES), F32),
        ),
        in_specs=[smem, smem, vmem],
        out_specs=(vmem, vmem, vmem, vmem),
        scratch_shapes=[pltpu.VMEM((2 * TAPS + 6, LANES), F32)],
        compiler_params=pltpu.CompilerParams(vmem_limit_bytes=16 * MIB),
        name="tables",
    )(whitening, offsets, phase_table())


def border_kernel(inbox, record, blocks, rise, fall, parts, done, collected):
    channels = record.shape[0]
    done[...] = jnp.zeros_like(done)
    head = inbox[0:16, :].astype(F32)[:1]
    lane = lax.broadcasted_iota(jnp.int32, (1, LANES), 1)

    def told(at):
        return jnp.sum(jnp.where(lane == at, head, 0.0)).astype(jnp.int32)

    offsets = [told(q) for q in range(GROUP)]
    cosines, sines = rotations([HOP * q + offsets[q] - (TAPS - 1) for q in range(GROUP)])
    before = jnp.zeros((channels, LANES), F32)
    for q in range(GROUP):
        offset = offsets[q]
        edges = edge_table(rise, fall, offset)
        if q == 0:
            part = matmul(record[:, 0:JITTER].astype(BF16), edges[RIM:])
        else:
            part = matmul(record[:, HOP * q - RIM : HOP * q + JITTER].astype(BF16), edges)
        part = (part + turn(before, cosines[q : q + 1], sines[q : q + 1])) * told(GROUP + q).astype(F32)
        upright = across(part)
        for c in range(collected.shape[0]):
            piece = upright[:, 128 * c : 128 * c + 128]
            collected[c, pl.ds(q, BINS, stride=2 * GROUP), :] = piece[:BINS]
            collected[c, pl.ds(GROUP + q, BINS, stride=2 * GROUP), :] = piece[BINS:]
        if q < GROUP - 1:
            before = before + matmul(
                record[:, HOP * q : HOP * q + HOP].astype(BF16), blocks[HOP * q : HOP * q + HOP, :]
            )
    width = min(128, channels)
    for c in range(collected.shape[0]):
        block = collected[c].reshape(BINS, 2 * GROUP, 128).astype(BF16)
        parts[:, :, width * c : width * c + width] = block[:, :, :width]


def border_parts(record, inbox, blocks, rise, fall):
    channels = record.shape[0]
    vmem = pl.BlockSpec(memory_space=pltpu.VMEM)
    lead = L - HOP + JITTER
    return pl.pallas_call(
        border_kernel,
        grid=(1,),
        out_shape=(jax.ShapeDtypeStruct((BINS, 2 * GROUP, channels), BF16), jax.ShapeDtypeStruct((8, 128), F32)),
        in_specs=[vmem, pl.BlockSpec((channels, lead), lambda i: (0, 0)), vmem, vmem, vmem],
        out_specs=(vmem, vmem),
        scratch_shapes=[pltpu.VMEM((max(channels // 128, 1), 2 * GROUP * BINS, 128), F32)],
        compiler_params=pltpu.CompilerParams(vmem_limit_bytes=50 * MIB),
        cost_estimate=pl.CostEstimate(
            flops=2 * channels * LANES * 3072, bytes_accessed=4 * channels * lead, transcendentals=0
        ),
        name="border_parts",
    )(inbox, record, blocks, rise, fall)


def spectra_kernel(offsets, valid, record, rim, blocks, rise, fall, turns, order, out, samples, later, collected, sems):
    channels, slab = record.shape
    steps = slab // L
    windows = GROUP * steps

    def fetch(s):
        return pltpu.make_async_copy(
            record.at[:, pl.ds(L * s, L)], samples.at[:, pl.ds(RIM + L * s, L)], sems.at[s]
        )

    for s in range(steps):
        fetch(s).start()
    samples[:, 0:RIM] = rim[...].astype(F32)
    samples[:, RIM + slab :] = jnp.zeros((channels, samples.shape[1] - RIM - slab), F32)

    def block_sums(s):
        found = []
        for i in range(GROUP):
            begin = pl.multiple_of(RIM + L * s + HOP * i, 128)
            found.append(
                matmul(samples[:, pl.ds(begin, HOP)].astype(BF16), blocks[HOP * i : HOP * i + HOP, :])
            )
        return found

    def keep(found):
        total = found[GROUP - 1]
        later[GROUP - 1] = total
        for q in range(GROUP - 2, -1, -1):
            total = total + found[q]
            later[q] = total

    def one_window(w, q, before):
        offset = offsets[w]
        begin = pl.multiple_of(HOP * w, 128)
        ends = samples[:, pl.ds(begin + L, EDGE)] - samples[:, pl.ds(begin, EDGE)]
        part = matmul(ends.astype(BF16), edge_table(rise, fall, offset))
        total = later[q] if before is None else later[q] + before
        part = (part + turn(total, turns[0, pl.ds(w, 1)], turns[1, pl.ds(w, 1)])) * valid[w].astype(F32)
        upright = across(part)
        for c in range(collected.shape[0]):
            collected[c, pl.ds(w, LANES, stride=windows), :] = upright[:, 128 * c : 128 * c + 128]

    fetch(0).wait()
    keep(block_sums(0))

    @pl.loop(0, steps - 1)
    def _(s):
        fetch(s + 1).wait()
        found = block_sums(s + 1)
        before = None
        for q in range(GROUP):
            one_window(GROUP * s + q, q, before)
            before = found[q] if before is None else before + found[q]
        keep(found)

    for q in range(GROUP):
        one_window(GROUP * (steps - 1) + q, q, None)

    width = min(128, channels)
    for c in range(collected.shape[0]):
        block = collected[c].reshape(LANES, windows, 128).astype(BF16)
        for ri in range(2):
            part = block[BINS * ri : BINS * ri + BINS, :, :width]
            out[:, windows * ri : windows * ri + windows, width * c : width * c + width] = part


def own_spectra(record, rim, offsets, valid, transform, rise, fall, turns, order):
    channels, slab = record.shape
    windows = offsets.shape[0]
    smem = pl.BlockSpec(memory_space=pltpu.SMEM)
    vmem = pl.BlockSpec(memory_space=pltpu.VMEM)
    return pl.pallas_call(
        spectra_kernel,
        out_shape=jax.ShapeDtypeStruct((BINS, 2 * windows, channels), BF16),
        in_specs=[smem, smem, pl.BlockSpec(memory_space=pl.ANY), vmem, vmem, vmem, vmem, vmem, vmem],
        out_specs=vmem,
        scratch_shapes=[
            pltpu.VMEM((channels, RIM + slab + L - HOP + JITTER), F32),
            pltpu.VMEM((GROUP, channels, LANES), F32),
            pltpu.VMEM((max(channels // 128, 1), LANES * windows, 128), F32),
            pltpu.SemaphoreType.DMA((slab // L,)),
        ],
        compiler_params=pltpu.CompilerParams(vmem_limit_bytes=50 * MIB),
        cost_estimate=pl.CostEstimate(
            flops=2 * channels * LANES * 896 * windows, bytes_accessed=4 * channels * slab, transcendentals=0
        ),
        name="own_spectra",
    )(offsets, valid, record, rim, transform, rise, fall, turns, order)


def with_parts(block, part):
    windows = block.shape[1] // 2
    row = lax.broadcasted_iota(jnp.int32, part.shape, 1)
    moved = jnp.concatenate([part[:, GROUP:], part[:, :GROUP]], axis=1)
    pieces = []
    for ri, extra in enumerate((moved, part)):
        end = windows * ri + windows
        pieces.append(block[:, windows * ri : end - 2 * GROUP])
        pieces.append(block[:, end - 2 * GROUP : end] + jnp.where(row >= GROUP, extra, 0.0))
    return jnp.concatenate(pieces, axis=1)


def join_kernel(own, parts, *chunks):
    devices = chunks[0].shape[0]
    for group in range(devices):
        begin = group * BINS // devices
        end = begin + BINS // devices
        joined = with_parts(own[begin:end].astype(F32), parts[begin:end].astype(F32)).astype(BF16)
        at = 0
        for chunk in chunks:
            chunk[group] = joined[at : at + chunk.shape[1]]
            at += chunk.shape[1]


def chunk_sizes(bins):
    sizes = [-(-bins // 2), 3 * bins // 8]
    return [size for size in sizes + [bins - sum(sizes)] if size]


def joined_chunks(own, parts, devices):
    _, rows, channels = own.shape
    vmem = pl.BlockSpec(memory_space=pltpu.VMEM)
    shapes = [(devices, count, rows, channels) for count in chunk_sizes(BINS // devices)]
    return pl.pallas_call(
        join_kernel,
        out_shape=tuple(jax.ShapeDtypeStruct(shape, BF16) for shape in shapes),
        in_specs=[vmem, vmem],
        out_specs=(vmem,) * len(shapes),
        compiler_params=pltpu.CompilerParams(vmem_limit_bytes=16 * MIB),
        name="joined_chunks",
    )(own, parts)


def left_kernel(own, out):
    sources, _, rows, channels = own.shape
    depth = sources * rows
    half = rows // 2
    straight = own[:, 0].astype(F32)
    turned = jnp.concatenate([straight[:, half:], -straight[:, :half]], axis=1)
    out[0, :channels] = straight.reshape(depth, channels).T.astype(BF16)
    out[0, channels:] = turned.reshape(depth, channels).T.astype(BF16)


def left_sides(own):
    sources, count, rows, channels = own.shape
    shape = (count, 2 * channels, sources * rows)
    return pl.pallas_call(
        left_kernel,
        grid=(count,),
        out_shape=jax.ShapeDtypeStruct(shape, BF16),
        in_specs=[pl.BlockSpec((sources, 1, rows, channels), lambda f: (0, f, 0, 0))],
        out_specs=pl.BlockSpec((1,) + shape[1:], lambda f: (f, 0, 0)),
        compiler_params=pltpu.CompilerParams(vmem_limit_bytes=16 * MIB),
        name="left_sides",
    )(own)


def cross_kernel(scale, side, me, left, *rest):
    out, done = rest[-2:]
    done[...] = jnp.zeros_like(done)
    sources, _, rows, channels = rest[0].shape[-4:]
    blocks = out.shape[3] // channels
    tile = min(256, channels)
    for n in range(blocks):
        if side is None:
            right, at = rest[0][n], channels * n
        else:
            right, at = rest[n][...], pl.multiple_of(channels * ((me[0] ^ n) & (blocks - 1)), 128)
        right = right[:, 0].reshape(sources * rows, channels)
        for j in range(0, channels, tile):
            for r in range(0, 2 * channels, tile):
                both = matmul(left[0, r : r + tile, :], right[:, j : j + tile]) * scale
                out[0, r // channels, r % channels : r % channels + tile, pl.ds(at + j, tile)] = both.astype(BF16)


def cross_products(left, right, result, begin, bins, blocks, side):
    sources, count, rows, channels = (right if side is None else right[0]).shape[-4:]
    columns = blocks if side is None else len(right)
    shape = (bins, 2, channels, blocks * channels)
    operands = [lax.axis_index("chan").astype(jnp.int32).reshape(1), left]
    in_specs = [pl.BlockSpec((1,) + left.shape[1:], lambda f, me: (f, 0, 0))]
    if side is None:
        operands.append(right)
        in_specs.append(pl.BlockSpec((blocks, sources, 1, rows, channels), lambda f, me: (0, 0, f, 0, 0)))
    else:
        operands += right
        in_specs += [pl.BlockSpec((sources, 1, rows, channels), lambda f, me: (0, f, 0, 0))] * columns
    if result is None:
        result, aliases = operands[1], {}
    else:
        aliases = {len(operands): 0}
    operands.append(result)
    in_specs.append(pl.BlockSpec(memory_space=pl.ANY))

    def place(f, me):
        return begin + f, 0, 0, 0 if side is None else (me[0] // columns) ^ side

    return pl.pallas_call(
        functools.partial(cross_kernel, 2.0 / (sources * rows), side),
        grid_spec=pltpu.PrefetchScalarGridSpec(
            num_scalar_prefetch=1,
            grid=(count,),
            in_specs=in_specs,
            out_specs=(
                pl.BlockSpec((1, 2, channels, columns * channels), place),
                pl.BlockSpec((8, 128), lambda f, me: (0, 0)),
            ),
        ),
        out_shape=(jax.ShapeDtypeStruct(shape, BF16), jax.ShapeDtypeStruct((8, 128), F32)),
        input_output_aliases=aliases,
        compiler_params=pltpu.CompilerParams(vmem_limit_bytes=24 * MIB),
        cost_estimate=pl.CostEstimate(
            flops=4 * count * channels * columns * channels * sources * rows,
            bytes_accessed=4 * count * channels * columns * channels,
            transcendentals=0,
        ),
        name="cross_products",
    )(*operands)


def swapped(shard, axis, bit):
    devices = lax.axis_size(axis)
    return lax.ppermute(shard, axis, [(i, i ^ bit) for i in range(devices)])


def fan(shard, axis, bit):
    held = {0: shard}
    while bit:
        held.update({n | bit: swapped(block, axis, bit) for n, block in list(held.items())})
        bit //= 2
    return held


def after_kernel(shard, done, out):
    out[...] = shard[...]


def after(shard, done):
    if done is None:
        return shard
    vmem = pl.BlockSpec(memory_space=pltpu.VMEM)
    return pl.pallas_call(
        after_kernel,
        out_shape=jax.ShapeDtypeStruct(shard.shape, shard.dtype),
        in_specs=[vmem, vmem],
        out_specs=vmem,
        compiler_params=pltpu.CompilerParams(vmem_limit_bytes=8 * MIB),
        name="after",
    )(shard, done)


def per_device(record, whitening, offsets, window_valid):
    devices = lax.axis_size("tm")
    blocks = lax.axis_size("chan")
    stacked = blocks & (blocks - 1) != 0 or record.shape[0] % 128 != 0
    top = blocks // 2
    bins = BINS // devices

    def exchanged(chunk):
        return lax.all_to_all(chunk, "tm", split_axis=0, concat_axis=0, tiled=True)

    def fanned(shard):
        held = fan(shard, "chan", top // 2)
        return [held[n] for n in range(top)]

    inbox = from_behind(outbox(record, offsets, window_valid), "tm", 1)
    transform, rise, fall, turns = tables(whitening, offsets)
    parts, done = border_parts(record, inbox, transform, rise, fall)
    parts = from_behind(parts, "tm", -1)
    own = own_spectra(record, inbox, offsets, window_valid, transform, rise, fall, turns, done)
    chunks = joined_chunks(own, parts, devices)
    begins = [sum(chunk.shape[1] for chunk in chunks[:p]) for p in range(len(chunks))]
    result, near, far, left, done = None, [], [], [], None

    def cross(p, side):
        right = near[p] if side == 0 else far[p]
        return cross_products(left[p], right, result, begins[p], bins, blocks, side)

    for p, chunk in enumerate(chunks):
        mine = exchanged(chunk)
        if stacked:
            right = lax.all_gather(mine, "chan", axis=0, tiled=False)
            result, _ = cross_products(left_sides(mine), right, result, begins[p], bins, blocks, None)
            continue
        mine = after(mine, done)
        far.append(swapped(mine, "chan", top))
        near.append(fanned(mine))
        left.append(left_sides(mine))
        ready = done
        result, done = cross(p, 0)
        if p:
            far[p - 1] = fanned(after(far[p - 1], ready) if p > 1 else far[p - 1])
            result, done = cross(p - 1, 1)
    if not stacked:
        far[-1] = fanned(after(far[-1], done))
        result, _ = cross(len(chunks) - 1, 1)
    return result


def solution(mesh):
    in_specs = (P("chan", "tm"), P(), P("tm"), P("tm"))
    out_specs = P("tm", None, "chan", None)
    return jax.shard_map(
        per_device, mesh=mesh, in_specs=in_specs, out_specs=out_specs, check_vma=False
    )
```

```python
import functools
import math

import jax
import jax.numpy as jnp
import numpy as np
from jax import lax
from jax.experimental import pallas as pl
from jax.experimental.pallas import tpu as pltpu
from jax.sharding import PartitionSpec as P

L = 2048
HOP = 512
JITTER = 256
TAPS = 65
BINS = 64
K0 = 64
RIM = 128
GROUP = L // HOP
EDGE = RIM + JITTER
LANES = 2 * BINS
MIB = 1 << 20
FIRST = 1
F32 = jnp.float32
BF16 = jnp.bfloat16


def from_behind(shard, axis, by):
    devices = lax.axis_size(axis)
    pairs = [(i, i + by) for i in range(devices) if 0 <= i + by < devices]
    return lax.ppermute(shard, axis, pairs)


def phase_table():
    sample = np.arange(L) - (TAPS - 1)
    angles = 2.0 * np.pi * np.mod(sample[:, None] * (K0 + np.arange(BINS))[None, :], L) / L
    return (np.concatenate([np.cos(angles), -np.sin(angles)], axis=1) / math.sqrt(L)).astype(np.float32)


def matmul(a, b):
    return jnp.dot(a, b, preferred_element_type=F32)


def rotations(places):
    rows = -(-len(places) // 8) * 8
    row = lax.broadcasted_iota(jnp.int32, (rows, LANES), 0)
    lane = lax.broadcasted_iota(jnp.int32, (rows, LANES), 1)
    place = jnp.zeros((rows, LANES), jnp.int32)
    for i, one in enumerate(places):
        place = jnp.where(row == i, one + L, place)
    bins = K0 + (lane & (BINS - 1))
    angles = ((bins * place) & (L - 1)).astype(F32) * (2.0 * math.pi / L)
    sine = jnp.sin(angles)
    return jnp.cos(angles), jnp.where(lane < BINS, -sine, sine)


def turn(values, cosine, sine):
    return values * cosine + pltpu.roll(values, BINS, 1) * sine


def edge_table(rise, fall, offset):
    start = JITTER - offset
    return jnp.concatenate([rise[pl.ds(start, RIM), :], fall[pl.ds(start, JITTER), :]], axis=0).astype(BF16)


def across(values):
    channels = values.shape[0]
    if channels % 128:
        values = jnp.pad(values, ((0, 128 - channels), (0, 0)))
    return values.T


def outbox_kernel(offsets, valid, record, out):
    top = record[0:8, :]
    row = lax.broadcasted_iota(jnp.int32, top.shape, 0)
    lane = lax.broadcasted_iota(jnp.int32, top.shape, 1)
    first = offsets.shape[0] - GROUP
    for q in range(GROUP):
        top = jnp.where((row == 0) & (lane == q), offsets[first + q].astype(F32), top)
        top = jnp.where((row == 0) & (lane == GROUP + q), valid[first + q].astype(F32), top)
    out[...] = jnp.concatenate([top, record[8:, :]], axis=0).astype(BF16)


def outbox(record, offsets, valid):
    channels, slab = record.shape
    smem = pl.BlockSpec(memory_space=pltpu.SMEM)
    return pl.pallas_call(
        outbox_kernel,
        grid=(1,),
        out_shape=jax.ShapeDtypeStruct((channels, RIM), BF16),
        in_specs=[smem, smem, pl.BlockSpec((channels, RIM), lambda i: (0, slab // RIM - 1))],
        out_specs=pl.BlockSpec(memory_space=pltpu.VMEM),
        compiler_params=pltpu.CompilerParams(vmem_limit_bytes=60 * MIB),
        name="outbox",
    )(offsets, valid, record)


def tables_kernel(taps, offsets, table, blocks, rise, fall, turns, padded):
    windows = offsets.shape[0]
    turns[0], turns[1] = rotations([HOP * w + offsets[w] - (TAPS - 1) for w in range(windows)])
    padded[0 : TAPS - 1, :] = jnp.zeros((TAPS - 1, LANES), F32)
    padded[TAPS - 1 :, :] = table[TAPS - 1 : TAPS - 1 + padded.shape[0] - (TAPS - 1), :]
    ramp = jnp.zeros((TAPS - 1, LANES), F32)
    gain = jnp.zeros((1, LANES), F32)
    for m in range(TAPS):
        tap = taps[m]
        ramp = ramp + tap * padded[m : m + TAPS - 1, :]
        gain = gain + tap * padded[TAPS - 1 + m : TAPS + m, :]
    gain = jnp.broadcast_to(gain * math.sqrt(L), (8, LANES))
    lane = lax.broadcasted_iota(jnp.int32, (8, LANES), 1)
    swapped = pltpu.roll(gain, BINS, 1)
    gain_re = jnp.where(lane < BINS, gain, swapped)[:1]
    gain_im = jnp.where(lane < BINS, -swapped, gain)[:1]
    columns = table[...]
    pure = columns * gain_re + pltpu.roll(columns, BINS, 1) * gain_im
    blocks[...] = pure.astype(BF16)
    rise[...] = jnp.zeros_like(rise)
    rise[rise.shape[0] - (TAPS - 1) :, :] = -ramp
    ahead = JITTER - (TAPS - 1)
    fall[0:ahead, :] = pure[L - ahead :]
    fall[ahead:JITTER, :] = pure[: TAPS - 1] - ramp
    fall[JITTER:, :] = jnp.zeros((fall.shape[0] - JITTER, LANES), F32)


def tables(whitening, offsets):
    smem = pl.BlockSpec(memory_space=pltpu.SMEM)
    vmem = pl.BlockSpec(memory_space=pltpu.VMEM)
    return pl.pallas_call(
        tables_kernel,
        out_shape=(
            jax.ShapeDtypeStruct((L, LANES), BF16),
            jax.ShapeDtypeStruct((EDGE, LANES), F32),
            jax.ShapeDtypeStruct((2 * JITTER, LANES), F32),
            jax.ShapeDtypeStruct((2, offsets.shape[0], LANES), F32),
        ),
        in_specs=[smem, smem, vmem],
        out_specs=(vmem, vmem, vmem, vmem),
        scratch_shapes=[pltpu.VMEM((2 * TAPS + 6, LANES), F32)],
        compiler_params=pltpu.CompilerParams(vmem_limit_bytes=16 * MIB),
        name="tables",
    )(whitening, offsets, phase_table())


def border_kernel(inbox, record, blocks, rise, fall, parts, done, collected):
    channels = record.shape[0]
    done[...] = jnp.zeros_like(done)
    head = inbox[0:16, :].astype(F32)[:1]
    lane = lax.broadcasted_iota(jnp.int32, (1, LANES), 1)

    def told(at):
        return jnp.sum(jnp.where(lane == at, head, 0.0)).astype(jnp.int32)

    offsets = [told(q) for q in range(GROUP)]
    cosines, sines = rotations([HOP * q + offsets[q] - (TAPS - 1) for q in range(GROUP)])
    before = jnp.zeros((channels, LANES), F32)
    for q in range(GROUP):
        offset = offsets[q]
        edges = edge_table(rise, fall, offset)
        if q == 0:
            part = matmul(record[:, 0:JITTER].astype(BF16), edges[RIM:])
        else:
            part = matmul(record[:, HOP * q - RIM : HOP * q + JITTER].astype(BF16), edges)
        part = (part + turn(before, cosines[q : q + 1], sines[q : q + 1])) * told(GROUP + q).astype(F32)
        upright = across(part)
        for c in range(collected.shape[0]):
            piece = upright[:, 128 * c : 128 * c + 128]
            collected[c, pl.ds(q, BINS, stride=2 * GROUP), :] = piece[:BINS]
            collected[c, pl.ds(GROUP + q, BINS, stride=2 * GROUP), :] = piece[BINS:]
        if q < GROUP - 1:
            before = before + matmul(
                record[:, HOP * q : HOP * q + HOP].astype(BF16), blocks[HOP * q : HOP * q + HOP, :]
            )
    width = min(128, channels)
    for c in range(collected.shape[0]):
        block = collected[c].reshape(BINS, 2 * GROUP, 128).astype(BF16)
        parts[:, :, width * c : width * c + width] = block[:, :, :width]


def border_parts(record, inbox, blocks, rise, fall):
    channels = record.shape[0]
    vmem = pl.BlockSpec(memory_space=pltpu.VMEM)
    lead = L - HOP + JITTER
    return pl.pallas_call(
        border_kernel,
        grid=(1,),
        out_shape=(jax.ShapeDtypeStruct((BINS, 2 * GROUP, channels), BF16), jax.ShapeDtypeStruct((8, 128), F32)),
        in_specs=[vmem, pl.BlockSpec((channels, lead), lambda i: (0, 0)), vmem, vmem, vmem],
        out_specs=(vmem, vmem),
        scratch_shapes=[pltpu.VMEM((max(channels // 128, 1), 2 * GROUP * BINS, 128), F32)],
        compiler_params=pltpu.CompilerParams(vmem_limit_bytes=50 * MIB),
        cost_estimate=pl.CostEstimate(
            flops=2 * channels * LANES * 3072, bytes_accessed=4 * channels * lead, transcendentals=0
        ),
        name="border_parts",
    )(inbox, record, blocks, rise, fall)


def spectra_kernel(offsets, valid, record, rim, blocks, rise, fall, turns, order, out, samples, later, collected, sems):
    channels, slab = record.shape
    steps = slab // L
    windows = GROUP * steps

    def fetch(s):
        return pltpu.make_async_copy(
            record.at[:, pl.ds(L * s, L)], samples.at[:, pl.ds(RIM + L * s, L)], sems.at[s]
        )

    for s in range(steps):
        fetch(s).start()
    samples[:, 0:RIM] = rim[...].astype(F32)
    samples[:, RIM + slab :] = jnp.zeros((channels, samples.shape[1] - RIM - slab), F32)

    def block_sums(s):
        found = []
        for i in range(GROUP):
            begin = pl.multiple_of(RIM + L * s + HOP * i, 128)
            found.append(
                matmul(samples[:, pl.ds(begin, HOP)].astype(BF16), blocks[HOP * i : HOP * i + HOP, :])
            )
        return found

    def keep(found):
        total = found[GROUP - 1]
        later[GROUP - 1] = total
        for q in range(GROUP - 2, -1, -1):
            total = total + found[q]
            later[q] = total

    def one_window(w, q, before):
        offset = offsets[w]
        begin = pl.multiple_of(HOP * w, 128)
        ends = samples[:, pl.ds(begin + L, EDGE)] - samples[:, pl.ds(begin, EDGE)]
        part = matmul(ends.astype(BF16), edge_table(rise, fall, offset))
        total = later[q] if before is None else later[q] + before
        part = (part + turn(total, turns[0, pl.ds(w, 1)], turns[1, pl.ds(w, 1)])) * valid[w].astype(F32)
        upright = across(part)
        for c in range(collected.shape[0]):
            collected[c, pl.ds(w, LANES, stride=windows), :] = upright[:, 128 * c : 128 * c + 128]

    fetch(0).wait()
    keep(block_sums(0))

    @pl.loop(0, steps - 1)
    def _(s):
        fetch(s + 1).wait()
        found = block_sums(s + 1)
        before = None
        for q in range(GROUP):
            one_window(GROUP * s + q, q, before)
            before = found[q] if before is None else before + found[q]
        keep(found)

    for q in range(GROUP):
        one_window(GROUP * (steps - 1) + q, q, None)

    width = min(128, channels)
    for c in range(collected.shape[0]):
        block = collected[c].reshape(LANES, windows, 128).astype(BF16)
        for ri in range(2):
            part = block[BINS * ri : BINS * ri + BINS, :, :width]
            out[:, windows * ri : windows * ri + windows, width * c : width * c + width] = part


def own_spectra(record, rim, offsets, valid, transform, rise, fall, turns, order):
    channels, slab = record.shape
    windows = offsets.shape[0]
    smem = pl.BlockSpec(memory_space=pltpu.SMEM)
    vmem = pl.BlockSpec(memory_space=pltpu.VMEM)
    return pl.pallas_call(
        spectra_kernel,
        out_shape=jax.ShapeDtypeStruct((BINS, 2 * windows, channels), BF16),
        in_specs=[smem, smem, pl.BlockSpec(memory_space=pl.ANY), vmem, vmem, vmem, vmem, vmem, vmem],
        out_specs=vmem,
        scratch_shapes=[
            pltpu.VMEM((channels, RIM + slab + L - HOP + JITTER), F32),
            pltpu.VMEM((GROUP, channels, LANES), F32),
            pltpu.VMEM((max(channels // 128, 1), LANES * windows, 128), F32),
            pltpu.SemaphoreType.DMA((slab // L,)),
        ],
        compiler_params=pltpu.CompilerParams(vmem_limit_bytes=50 * MIB),
        cost_estimate=pl.CostEstimate(
            flops=2 * channels * LANES * 896 * windows, bytes_accessed=4 * channels * slab, transcendentals=0
        ),
        name="own_spectra",
    )(offsets, valid, record, rim, transform, rise, fall, turns, order)


def with_parts(block, part):
    windows = block.shape[1] // 2
    row = lax.broadcasted_iota(jnp.int32, part.shape, 1)
    moved = jnp.concatenate([part[:, GROUP:], part[:, :GROUP]], axis=1)
    pieces = []
    for ri, extra in enumerate((moved, part)):
        end = windows * ri + windows
        pieces.append(block[:, windows * ri : end - 2 * GROUP])
        pieces.append(block[:, end - 2 * GROUP : end] + jnp.where(row >= GROUP, extra, 0.0))
    return jnp.concatenate(pieces, axis=1)


def join_kernel(own, parts, *chunks):
    devices = chunks[0].shape[0]
    total = sum(chunk.shape[1] for chunk in chunks)
    for group in range(devices):
        begin = group * BINS // devices
        joined = with_parts(
            own[begin : begin + total].astype(F32), parts[begin : begin + total].astype(F32)
        ).astype(BF16)
        at = 0
        for chunk in chunks:
            chunk[group] = joined[at : at + chunk.shape[1]]
            at += chunk.shape[1]


def chunk_sizes(bins):
    count = min(3, bins)
    return [(bins + count - 1 - c) // count for c in range(count)]


def joined_chunks(own, parts, devices, sizes):
    _, rows, channels = own.shape
    vmem = pl.BlockSpec(memory_space=pltpu.VMEM)
    return pl.pallas_call(
        join_kernel,
        out_shape=tuple(jax.ShapeDtypeStruct((devices, count, rows, channels), BF16) for count in sizes),
        in_specs=[vmem, vmem],
        out_specs=(vmem,) * len(sizes),
        compiler_params=pltpu.CompilerParams(vmem_limit_bytes=16 * MIB),
        name="joined_chunks",
    )(own, parts)


def pieces_kernel(skip, me, own, parts, done, *pieces):
    count = pieces[0].shape[0]
    bins = BINS // len(pieces)
    for d, piece in enumerate(pieces):
        mine = pl.ds((me[0] ^ d) * bins + skip, count)
        piece[...] = with_parts(own[mine].astype(F32), parts[mine].astype(F32)).astype(BF16)


def joined_pieces(own, parts, devices, skip, count, done):
    _, rows, channels = own.shape
    vmem = pl.BlockSpec(memory_space=pltpu.VMEM)
    return pl.pallas_call(
        functools.partial(pieces_kernel, skip),
        out_shape=(jax.ShapeDtypeStruct((count, rows, channels), BF16),) * devices,
        in_specs=[pl.BlockSpec(memory_space=pltpu.SMEM), vmem, vmem, vmem],
        out_specs=(vmem,) * devices,
        compiler_params=pltpu.CompilerParams(vmem_limit_bytes=16 * MIB),
        name="joined_pieces",
    )(lax.axis_index("tm").astype(jnp.int32).reshape(1), own, parts, done)


def stack_kernel(*refs):
    *pieces, _, out, done = refs
    done[...] = jnp.zeros_like(done)
    for d, piece in enumerate(pieces):
        out[d] = piece[...]


def stacked_pieces(pieces, done):
    vmem = pl.BlockSpec(memory_space=pltpu.VMEM)
    return pl.pallas_call(
        stack_kernel,
        out_shape=(
            jax.ShapeDtypeStruct((len(pieces),) + pieces[0].shape, BF16),
            jax.ShapeDtypeStruct((8, 128), F32),
        ),
        in_specs=[vmem] * (len(pieces) + 1),
        out_specs=(vmem, vmem),
        compiler_params=pltpu.CompilerParams(vmem_limit_bytes=16 * MIB),
        name="stacked_pieces",
    )(*pieces, done)


def left_kernel(own, out):
    sources, _, rows, channels = own.shape
    depth = sources * rows
    half = rows // 2
    straight = own[:, 0].astype(F32)
    turned = jnp.concatenate([straight[:, half:], -straight[:, :half]], axis=1)
    out[0, :channels] = straight.reshape(depth, channels).T.astype(BF16)
    out[0, channels:] = turned.reshape(depth, channels).T.astype(BF16)


def left_sides(own):
    sources, count, rows, channels = own.shape
    shape = (count, 2 * channels, sources * rows)
    return pl.pallas_call(
        left_kernel,
        grid=(count,),
        out_shape=jax.ShapeDtypeStruct(shape, BF16),
        in_specs=[pl.BlockSpec((sources, 1, rows, channels), lambda f: (0, f, 0, 0))],
        out_specs=pl.BlockSpec((1,) + shape[1:], lambda f: (f, 0, 0)),
        compiler_params=pltpu.CompilerParams(vmem_limit_bytes=16 * MIB),
        name="left_sides",
    )(own)


def cross_kernel(scale, side, me, left, *rest):
    out, done = rest[-2:]
    done[...] = jnp.zeros_like(done)
    sources, _, rows, channels = rest[0].shape[-4:]
    blocks = out.shape[3] // channels
    tile = min(256, channels)
    for n in range(blocks):
        if side is None:
            right, at = rest[0][n], channels * n
        else:
            right, at = rest[n][...], pl.multiple_of(channels * ((me[0] ^ n) & (blocks - 1)), 128)
        right = right[:, 0].reshape(sources * rows, channels)
        for j in range(0, channels, tile):
            for r in range(0, 2 * channels, tile):
                both = matmul(left[0, r : r + tile, :], right[:, j : j + tile]) * scale
                out[0, r // channels, r % channels : r % channels + tile, pl.ds(at + j, tile)] = both.astype(BF16)


def cross_products(left, right, result, begin, bins, blocks, side, ready=None):
    sources, count, rows, channels = (right if side is None else right[0]).shape[-4:]
    columns = blocks if side is None else len(right)
    shape = (bins, 2, channels, blocks * channels)
    operands = [lax.axis_index("chan").astype(jnp.int32).reshape(1), left]
    in_specs = [pl.BlockSpec((1,) + left.shape[1:], lambda f, me: (f, 0, 0))]
    if side is None:
        operands.append(right)
        in_specs.append(pl.BlockSpec((blocks, sources, 1, rows, channels), lambda f, me: (0, 0, f, 0, 0)))
    else:
        operands += right
        in_specs += [pl.BlockSpec((sources, 1, rows, channels), lambda f, me: (0, f, 0, 0))] * columns
    if result is None:
        result, aliases = operands[1], {}
    else:
        aliases = {len(operands): 0}
    operands.append(result)
    in_specs.append(pl.BlockSpec(memory_space=pl.ANY))
    if ready is not None:
        operands.append(ready)
        in_specs.append(pl.BlockSpec((8, 128), lambda f, me: (0, 0)))

    def place(f, me):
        return begin + f, 0, 0, 0 if side is None else (me[0] // columns) ^ side

    return pl.pallas_call(
        functools.partial(cross_kernel, 2.0 / (sources * rows), side),
        grid_spec=pltpu.PrefetchScalarGridSpec(
            num_scalar_prefetch=1,
            grid=(count,),
            in_specs=in_specs,
            out_specs=(
                pl.BlockSpec((1, 2, channels, columns * channels), place),
                pl.BlockSpec((8, 128), lambda f, me: (0, 0)),
            ),
        ),
        out_shape=(jax.ShapeDtypeStruct(shape, BF16), jax.ShapeDtypeStruct((8, 128), F32)),
        input_output_aliases=aliases,
        compiler_params=pltpu.CompilerParams(vmem_limit_bytes=24 * MIB),
        cost_estimate=pl.CostEstimate(
            flops=4 * count * channels * columns * channels * sources * rows,
            bytes_accessed=4 * count * channels * columns * channels,
            transcendentals=0,
        ),
        name="cross_products",
    )(*operands)


def swapped(shard, axis, bit):
    devices = lax.axis_size(axis)
    return lax.ppermute(shard, axis, [(i, i ^ bit) for i in range(devices)])


def fan(shard, axis, bit):
    held = {0: shard}
    while bit:
        held.update({n | bit: swapped(block, axis, bit) for n, block in list(held.items())})
        bit //= 2
    return held


def after_kernel(shard, *refs):
    refs[-1][...] = shard[...]


def after(shard, *done):
    if any(one is None for one in done):
        return shard
    vmem = pl.BlockSpec(memory_space=pltpu.VMEM)
    return pl.pallas_call(
        after_kernel,
        out_shape=jax.ShapeDtypeStruct(shard.shape, shard.dtype),
        in_specs=[vmem] * (len(done) + 1),
        out_specs=vmem,
        compiler_params=pltpu.CompilerParams(vmem_limit_bytes=8 * MIB),
        name="after",
    )(shard, *done)


def per_device(record, whitening, offsets, window_valid):
    devices = lax.axis_size("tm")
    blocks = lax.axis_size("chan")
    stacked = blocks & (blocks - 1) != 0 or record.shape[0] % 128 != 0
    top = blocks // 2
    bins = BINS // devices

    def exchanged(chunk):
        return lax.all_to_all(chunk, "tm", split_axis=0, concat_axis=0, tiled=True)

    def fanned(shard):
        held = fan(shard, "chan", top // 2)
        return [held[n] for n in range(top)]

    inbox = from_behind(outbox(record, offsets, window_valid), "tm", 1)
    transform, rise, fall, turns = tables(whitening, offsets)
    parts, done = border_parts(record, inbox, transform, rise, fall)
    parts = from_behind(parts, "tm", -1)
    own = own_spectra(record, inbox, offsets, window_valid, transform, rise, fall, turns, done)
    sizes = chunk_sizes(bins)
    begins = [sum(sizes[:p]) for p in range(len(sizes))]
    last = len(sizes) - 1
    paired = not stacked and devices & (devices - 1) == 0 and last > 1
    chunks = joined_chunks(own, parts, devices, sizes[:last] if paired else sizes)
    result, near, far, left, done = None, [], [], [], None

    def cross(p, side, ready=None):
        right = near[p] if side == 0 else far[p]
        return cross_products(left[p], right, result, begins[p], bins, blocks, side, ready)

    if stacked:
        for p, chunk in enumerate(chunks):
            mine = exchanged(chunk)
            right = lax.all_gather(mine, "chan", axis=0, tiled=False)
            result, _ = cross_products(left_sides(mine), right, result, begins[p], bins, blocks, None)
        return result
    for p in range(len(sizes)):
        if p == last and paired:
            mine, arrived = stacked_pieces(pieces, done)
        else:
            mine = after(exchanged(chunks[p]), *([pieces[FIRST], far[0][0]] if p and paired else [done]))
        far.append(swapped(mine, "chan", top))
        near.append(fanned(mine))
        left.append(left_sides(mine))
        if p == last and paired:
            far[0] = far[0][1]
            result, done = cross(0, 1, arrived)
            far[1:last] = [fanned(after(block, done)) for block in far[1:last]]
        result, done = cross(p, 0)
        if p == last and paired:
            for n in range(1, last):
                result, done = cross(n, 1)
        if p == 0 and paired:
            pieces = joined_pieces(own, parts, devices, begins[last], sizes[last], done)
            far[0] = far[0], fanned(far[0])
            pieces = [pieces[0]] + [swapped(pieces[d], "tm", d) for d in range(1, devices)]
        if p and not paired:
            far[p - 1] = fanned(far[p - 1])
            result, done = cross(p - 1, 1)
    far[-1] = fanned(after(far[-1], done))
    result, _ = cross(last, 1)
    return result


def solution(mesh):
    in_specs = (P("chan", "tm"), P(), P("tm"), P("tm"))
    out_specs = P("tm", None, "chan", None)
    return jax.shard_map(
        per_device, mesh=mesh, in_specs=in_specs, out_specs=out_specs, check_vma=False
    )
```

```python
import functools
import math

import jax
import jax.numpy as jnp
from jax import lax
from jax.experimental import pallas as pl
from jax.experimental.pallas import tpu as pltpu
from jax.sharding import PartitionSpec as P

L = 2048
HOP = 512
JITTER = 256
TAPS = 65
BINS = 64
K0 = 64
RIM = 128
GROUP = L // HOP
EDGE = RIM + JITTER
LANES = 2 * BINS
MIB = 1 << 20
F32 = jnp.float32
BF16 = jnp.bfloat16


def from_behind(shard, axis, by):
    devices = lax.axis_size(axis)
    pairs = [(i, i + by) for i in range(devices) if 0 <= i + by < devices]
    return lax.ppermute(shard, axis, pairs)


def matmul(a, b):
    return jnp.dot(a, b, preferred_element_type=F32)


def rotation(place):
    lane = lax.broadcasted_iota(jnp.int32, (8, LANES), 1)[:1]
    bins = K0 + (lane & (BINS - 1))
    angles = ((bins * place) & (L - 1)).astype(F32) * (2.0 * math.pi / L)
    sine = jnp.sin(angles)
    return jnp.cos(angles), jnp.where(lane < BINS, -sine, sine)


def turn(values, place):
    cosine, sine = rotation(jnp.full((8, LANES), place + L, jnp.int32))
    return values * cosine[:1] + pltpu.roll(values, BINS, 1) * sine[:1]


def edge_table(rise, fall, offset):
    start = JITTER - offset
    return jnp.concatenate([rise[pl.ds(start, RIM), :], fall[pl.ds(start, JITTER), :]], axis=0).astype(BF16)


def across(values):
    channels = values.shape[0]
    if channels % 128:
        values = jnp.pad(values, ((0, 128 - channels), (0, 0)))
    return values.T


def outbox_kernel(offsets, valid, record, out):
    top = record[0:8, :]
    row = lax.broadcasted_iota(jnp.int32, top.shape, 0)
    lane = lax.broadcasted_iota(jnp.int32, top.shape, 1)
    first = offsets.shape[0] - GROUP
    for q in range(GROUP):
        top = jnp.where((row == 0) & (lane == q), offsets[first + q].astype(F32), top)
        top = jnp.where((row == 0) & (lane == GROUP + q), valid[first + q].astype(F32), top)
    out[...] = jnp.concatenate([top, record[8:, :]], axis=0).astype(BF16)


def outbox(record, offsets, valid):
    channels, slab = record.shape
    smem = pl.BlockSpec(memory_space=pltpu.SMEM)
    return pl.pallas_call(
        outbox_kernel,
        grid=(1,),
        out_shape=jax.ShapeDtypeStruct((channels, RIM), BF16),
        in_specs=[smem, smem, pl.BlockSpec((channels, RIM), lambda i: (0, slab // RIM - 1))],
        out_specs=pl.BlockSpec(memory_space=pltpu.VMEM),
        compiler_params=pltpu.CompilerParams(vmem_limit_bytes=60 * MIB),
        name="outbox",
    )(offsets, valid, record)


def tables_kernel(taps, record, blocks, rise, fall, heads, sums, padded, lead, sem):
    fetch = pltpu.make_async_copy(record.at[:, pl.ds(0, lead.shape[1])], lead, sem)
    fetch.start()
    ramp_rows = TAPS - 1
    lane = lax.broadcasted_iota(jnp.int32, (8, LANES), 1)
    row = lax.broadcasted_iota(jnp.int32, (ramp_rows, LANES), 0)

    def phases(cosine, sine):
        half = lax.broadcasted_iota(jnp.int32, cosine.shape, 1) < BINS
        return jnp.where(half, cosine, sine * -1.0) * (1.0 / math.sqrt(L))

    first = phases(*rotation(row))
    padded[0:ramp_rows, :] = jnp.zeros((ramp_rows, LANES), F32)
    padded[ramp_rows : 2 * ramp_rows, :] = first
    padded[2 * ramp_rows :, :] = phases(*rotation(row[:8] + ramp_rows))
    ramp = jnp.zeros((ramp_rows, LANES), F32)
    gain = jnp.zeros((1, LANES), F32)
    for m in range(TAPS):
        tap = taps[m]
        ramp = ramp + tap * padded[m : m + ramp_rows, :]
        gain = gain + tap * padded[ramp_rows + m : TAPS + m, :]
    gain = jnp.broadcast_to(gain * math.sqrt(L), (8, LANES))
    swapped = pltpu.roll(gain, BINS, 1)
    gain_re = jnp.where(lane < BINS, gain, swapped)[:1]
    gain_im = jnp.where(lane < BINS, -swapped, gain)[:1]
    base = phases(*rotation(row + (L - ramp_rows)))
    base = base * gain_re + pltpu.roll(base, BINS, 1) * gain_im
    other = pltpu.roll(base, BINS, 1)
    steps = L // ramp_rows
    onward = lax.broadcasted_iota(jnp.int32, (steps, LANES), 0)
    cosines, sines = rotation(L - onward * ramp_rows)
    ahead = JITTER // ramp_rows - 1
    for a in range(steps):
        pure = base * cosines[a : a + 1] + other * sines[a : a + 1]
        blocks[a * ramp_rows : (a + 1) * ramp_rows, :] = pure.astype(BF16)
        if a >= steps - ahead:
            at = (a - steps + ahead) * ramp_rows
            fall[at : at + ramp_rows, :] = pure
        if a == 0:
            fall[ahead * ramp_rows : JITTER, :] = pure - ramp
    fall[JITTER:, :] = jnp.zeros((fall.shape[0] - JITTER, LANES), F32)
    rise[...] = jnp.zeros_like(rise)
    rise[rise.shape[0] - ramp_rows :, :] = -ramp
    fetch.wait()
    heads[...] = lead[...].astype(BF16)
    total = None
    for q in range(GROUP - 1):
        found = matmul(heads[:, HOP * q : HOP * q + HOP], blocks[HOP * q : HOP * q + HOP, :])
        total = found if total is None else total + found
        sums[q] = total


def tables(whitening, record):
    channels = record.shape[0]
    lead = L - HOP + JITTER
    vmem = pl.BlockSpec(memory_space=pltpu.VMEM)
    return pl.pallas_call(
        tables_kernel,
        out_shape=(
            jax.ShapeDtypeStruct((L, LANES), BF16),
            jax.ShapeDtypeStruct((EDGE, LANES), F32),
            jax.ShapeDtypeStruct((2 * JITTER, LANES), F32),
            jax.ShapeDtypeStruct((channels, lead), BF16),
            jax.ShapeDtypeStruct((GROUP - 1, channels, LANES), F32),
        ),
        in_specs=[pl.BlockSpec(memory_space=pltpu.SMEM), pl.BlockSpec(memory_space=pl.ANY)],
        out_specs=(vmem,) * 5,
        scratch_shapes=[
            pltpu.VMEM((2 * TAPS + 6, LANES), F32),
            pltpu.VMEM((channels, lead), F32),
            pltpu.SemaphoreType.DMA,
        ],
        compiler_params=pltpu.CompilerParams(vmem_limit_bytes=50 * MIB),
        name="tables",
    )(whitening, record)


def border_kernel(inbox, heads, sums, rise, fall, parts, done, collected):
    channels = heads.shape[0]
    done[...] = jnp.zeros_like(done)
    head = inbox[0:16, :].astype(F32)[:1]
    lane = lax.broadcasted_iota(jnp.int32, (1, LANES), 1)

    def told(at):
        return jnp.sum(jnp.where(lane == at, head, 0.0)).astype(jnp.int32)

    for q in range(GROUP):
        offset = told(q)
        edges = edge_table(rise, fall, offset)
        if q == 0:
            part = matmul(heads[:, 0:JITTER], edges[RIM:])
        else:
            part = matmul(heads[:, HOP * q - RIM : HOP * q + JITTER], edges)
            part = part + turn(sums[q - 1], HOP * q + offset - (TAPS - 1))
        upright = across(part * told(GROUP + q).astype(F32))
        for c in range(collected.shape[0]):
            piece = upright[:, 128 * c : 128 * c + 128]
            collected[c, pl.ds(q, BINS, stride=2 * GROUP), :] = piece[:BINS]
            collected[c, pl.ds(GROUP + q, BINS, stride=2 * GROUP), :] = piece[BINS:]
    width = min(128, channels)
    for c in range(collected.shape[0]):
        block = collected[c].reshape(BINS, 2 * GROUP, 128).astype(BF16)
        parts[:, :, width * c : width * c + width] = block[:, :, :width]


def border_parts(inbox, heads, sums, rise, fall):
    channels = heads.shape[0]
    vmem = pl.BlockSpec(memory_space=pltpu.VMEM)
    return pl.pallas_call(
        border_kernel,
        out_shape=(jax.ShapeDtypeStruct((BINS, 2 * GROUP, channels), BF16), jax.ShapeDtypeStruct((8, 128), F32)),
        in_specs=[vmem] * 5,
        out_specs=(vmem, vmem),
        scratch_shapes=[pltpu.VMEM((max(channels // 128, 1), 2 * GROUP * BINS, 128), F32)],
        compiler_params=pltpu.CompilerParams(vmem_limit_bytes=50 * MIB),
        cost_estimate=pl.CostEstimate(
            flops=2 * channels * LANES * 1536, bytes_accessed=8 * channels * L, transcendentals=0
        ),
        name="border_parts",
    )(inbox, heads, sums, rise, fall)


def spectra_kernel(offsets, valid, record, rim, blocks, rise, fall, order, out, samples, later, collected, sems):
    channels, slab = record.shape
    steps = slab // L
    windows = GROUP * steps

    def fetch(s):
        return pltpu.make_async_copy(
            record.at[:, pl.ds(L * s, L)], samples.at[:, pl.ds(RIM + L * s, L)], sems.at[s]
        )

    for s in range(steps):
        fetch(s).start()
    samples[:, 0:RIM] = rim[...].astype(F32)
    samples[:, RIM + slab :] = jnp.zeros((channels, samples.shape[1] - RIM - slab), F32)

    def block_sums(s):
        found = []
        for i in range(GROUP):
            begin = pl.multiple_of(RIM + L * s + HOP * i, 128)
            found.append(
                matmul(samples[:, pl.ds(begin, HOP)].astype(BF16), blocks[HOP * i : HOP * i + HOP, :])
            )
        return found

    def keep(found):
        total = found[GROUP - 1]
        later[GROUP - 1] = total
        for q in range(GROUP - 2, -1, -1):
            total = total + found[q]
            later[q] = total

    def one_window(w, q, before):
        offset = offsets[w]
        begin = pl.multiple_of(HOP * w, 128)
        ends = samples[:, pl.ds(begin + L, EDGE)] - samples[:, pl.ds(begin, EDGE)]
        part = matmul(ends.astype(BF16), edge_table(rise, fall, offset))
        total = later[q] if before is None else later[q] + before
        part = (part + turn(total, HOP * q + offset - (TAPS - 1))) * valid[w].astype(F32)
        upright = across(part)
        for c in range(collected.shape[0]):
            collected[c, pl.ds(w, LANES, stride=windows), :] = upright[:, 128 * c : 128 * c + 128]

    fetch(0).wait()
    keep(block_sums(0))

    @pl.loop(0, steps - 1)
    def _(s):
        fetch(s + 1).wait()
        found = block_sums(s + 1)
        before = None
        for q in range(GROUP):
            one_window(GROUP * s + q, q, before)
            before = found[q] if before is None else before + found[q]
        keep(found)

    for q in range(GROUP):
        one_window(GROUP * (steps - 1) + q, q, None)

    width = min(128, channels)
    for c in range(collected.shape[0]):
        block = collected[c].reshape(LANES, windows, 128).astype(BF16)
        for ri in range(2):
            part = block[BINS * ri : BINS * ri + BINS, :, :width]
            out[:, windows * ri : windows * ri + windows, width * c : width * c + width] = part


def own_spectra(record, rim, offsets, valid, transform, rise, fall, order):
    channels, slab = record.shape
    windows = offsets.shape[0]
    smem = pl.BlockSpec(memory_space=pltpu.SMEM)
    vmem = pl.BlockSpec(memory_space=pltpu.VMEM)
    return pl.pallas_call(
        spectra_kernel,
        out_shape=jax.ShapeDtypeStruct((BINS, 2 * windows, channels), BF16),
        in_specs=[smem, smem, pl.BlockSpec(memory_space=pl.ANY), vmem, vmem, vmem, vmem, vmem],
        out_specs=vmem,
        scratch_shapes=[
            pltpu.VMEM((channels, RIM + slab + L - HOP + JITTER), F32),
            pltpu.VMEM((GROUP, channels, LANES), F32),
            pltpu.VMEM((max(channels // 128, 1), LANES * windows, 128), F32),
            pltpu.SemaphoreType.DMA((slab // L,)),
        ],
        compiler_params=pltpu.CompilerParams(vmem_limit_bytes=50 * MIB),
        cost_estimate=pl.CostEstimate(
            flops=2 * channels * LANES * 896 * windows, bytes_accessed=4 * channels * slab, transcendentals=0
        ),
        name="own_spectra",
    )(offsets, valid, record, rim, transform, rise, fall, order)


def with_parts(block, part):
    windows = block.shape[1] // 2
    row = lax.broadcasted_iota(jnp.int32, part.shape, 1)
    moved = jnp.concatenate([part[:, GROUP:], part[:, :GROUP]], axis=1)
    pieces = []
    for ri, extra in enumerate((moved, part)):
        end = windows * ri + windows
        pieces.append(block[:, windows * ri : end - 2 * GROUP])
        pieces.append(block[:, end - 2 * GROUP : end] + jnp.where(row >= GROUP, extra, 0.0))
    return jnp.concatenate(pieces, axis=1)


def join_kernel(own, parts, *chunks):
    devices = chunks[0].shape[0]
    for group in range(devices):
        begin = group * BINS // devices
        end = begin + BINS // devices
        joined = with_parts(own[begin:end].astype(F32), parts[begin:end].astype(F32)).astype(BF16)
        at = 0
        for chunk in chunks:
            chunk[group] = joined[at : at + chunk.shape[1]]
            at += chunk.shape[1]


def chunk_sizes(bins):
    count = min(3, bins)
    return [(bins + count - 1 - c) // count for c in range(count)]


def joined_chunks(own, parts, devices):
    _, rows, channels = own.shape
    vmem = pl.BlockSpec(memory_space=pltpu.VMEM)
    shapes = [(devices, count, rows, channels) for count in chunk_sizes(BINS // devices)]
    return pl.pallas_call(
        join_kernel,
        out_shape=tuple(jax.ShapeDtypeStruct(shape, BF16) for shape in shapes),
        in_specs=[vmem, vmem],
        out_specs=(vmem,) * len(shapes),
        compiler_params=pltpu.CompilerParams(vmem_limit_bytes=16 * MIB),
        name="joined_chunks",
    )(own, parts)


def left_kernel(own, out):
    sources, _, rows, channels = own.shape
    depth = sources * rows
    half = rows // 2
    straight = own[:, 0].astype(F32)
    turned = jnp.concatenate([straight[:, half:], -straight[:, :half]], axis=1)
    out[0, :channels] = straight.reshape(depth, channels).T.astype(BF16)
    out[0, channels:] = turned.reshape(depth, channels).T.astype(BF16)


def left_sides(own):
    sources, count, rows, channels = own.shape
    shape = (count, 2 * channels, sources * rows)
    return pl.pallas_call(
        left_kernel,
        grid=(count,),
        out_shape=jax.ShapeDtypeStruct(shape, BF16),
        in_specs=[pl.BlockSpec((sources, 1, rows, channels), lambda f: (0, f, 0, 0))],
        out_specs=pl.BlockSpec((1,) + shape[1:], lambda f: (f, 0, 0)),
        compiler_params=pltpu.CompilerParams(vmem_limit_bytes=16 * MIB),
        name="left_sides",
    )(own)


def cross_kernel(scale, side, me, left, *rest):
    out, done = rest[-2:]
    done[...] = jnp.zeros_like(done)
    sources, _, rows, channels = rest[0].shape[-4:]
    blocks = out.shape[3] // channels
    tile = min(256, channels)
    for n in range(blocks):
        if side is None:
            right, at = rest[0][n], channels * n
        else:
            right, at = rest[n][...], pl.multiple_of(channels * ((me[0] ^ n) & (blocks - 1)), 128)
        right = right[:, 0].reshape(sources * rows, channels)
        for j in range(0, channels, tile):
            for r in range(0, 2 * channels, tile):
                both = matmul(left[0, r : r + tile, :], right[:, j : j + tile]) * scale
                out[0, r // channels, r % channels : r % channels + tile, pl.ds(at + j, tile)] = both.astype(BF16)


def cross_products(left, right, result, begin, bins, blocks, side):
    sources, count, rows, channels = (right if side is None else right[0]).shape[-4:]
    columns = blocks if side is None else len(right)
    shape = (bins, 2, channels, blocks * channels)
    operands = [lax.axis_index("chan").astype(jnp.int32).reshape(1), left]
    in_specs = [pl.BlockSpec((1,) + left.shape[1:], lambda f, me: (f, 0, 0))]
    if side is None:
        operands.append(right)
        in_specs.append(pl.BlockSpec((blocks, sources, 1, rows, channels), lambda f, me: (0, 0, f, 0, 0)))
    else:
        operands += right
        in_specs += [pl.BlockSpec((sources, 1, rows, channels), lambda f, me: (0, f, 0, 0))] * columns
    if result is None:
        result, aliases = operands[1], {}
    else:
        aliases = {len(operands): 0}
    operands.append(result)
    in_specs.append(pl.BlockSpec(memory_space=pl.ANY))

    def place(f, me):
        return begin + f, 0, 0, 0 if side is None else (me[0] // columns) ^ side

    return pl.pallas_call(
        functools.partial(cross_kernel, 2.0 / (sources * rows), side),
        grid_spec=pltpu.PrefetchScalarGridSpec(
            num_scalar_prefetch=1,
            grid=(count,),
            in_specs=in_specs,
            out_specs=(
                pl.BlockSpec((1, 2, channels, columns * channels), place),
                pl.BlockSpec((8, 128), lambda f, me: (0, 0)),
            ),
        ),
        out_shape=(jax.ShapeDtypeStruct(shape, BF16), jax.ShapeDtypeStruct((8, 128), F32)),
        input_output_aliases=aliases,
        compiler_params=pltpu.CompilerParams(vmem_limit_bytes=24 * MIB),
        cost_estimate=pl.CostEstimate(
            flops=4 * count * channels * columns * channels * sources * rows,
            bytes_accessed=4 * count * channels * columns * channels,
            transcendentals=0,
        ),
        name="cross_products",
    )(*operands)


def swapped(shard, axis, bit):
    devices = lax.axis_size(axis)
    return lax.ppermute(shard, axis, [(i, i ^ bit) for i in range(devices)])


def fan(shard, axis, bit):
    held = {0: shard}
    while bit:
        held.update({n | bit: swapped(block, axis, bit) for n, block in list(held.items())})
        bit //= 2
    return held


def after_kernel(shard, done, out):
    out[...] = shard[...]


def after(shard, done):
    if done is None:
        return shard
    vmem = pl.BlockSpec(memory_space=pltpu.VMEM)
    return pl.pallas_call(
        after_kernel,
        out_shape=jax.ShapeDtypeStruct(shard.shape, shard.dtype),
        in_specs=[vmem, vmem],
        out_specs=vmem,
        compiler_params=pltpu.CompilerParams(vmem_limit_bytes=8 * MIB),
        name="after",
    )(shard, done)


def per_device(record, whitening, offsets, window_valid):
    devices = lax.axis_size("tm")
    blocks = lax.axis_size("chan")
    stacked = blocks & (blocks - 1) != 0 or record.shape[0] % 128 != 0
    top = blocks // 2
    bins = BINS // devices

    def exchanged(chunk):
        return lax.all_to_all(chunk, "tm", split_axis=0, concat_axis=0, tiled=True)

    def fanned(shard):
        held = fan(shard, "chan", top // 2)
        return [held[n] for n in range(top)]

    inbox = from_behind(outbox(record, offsets, window_valid), "tm", 1)
    transform, rise, fall, heads, sums = tables(whitening, record)
    parts, done = border_parts(inbox, heads, sums, rise, fall)
    parts = from_behind(parts, "tm", -1)
    own = own_spectra(record, inbox, offsets, window_valid, transform, rise, fall, done)
    chunks = joined_chunks(own, parts, devices)
    begins = [sum(chunk.shape[1] for chunk in chunks[:p]) for p in range(len(chunks))]
    result, near, far, left, done = None, [], [], [], None

    def cross(p, side):
        right = near[p] if side == 0 else far[p]
        return cross_products(left[p], right, result, begins[p], bins, blocks, side)

    for p, chunk in enumerate(chunks):
        mine = exchanged(chunk)
        if stacked:
            right = lax.all_gather(mine, "chan", axis=0, tiled=False)
            result, _ = cross_products(left_sides(mine), right, result, begins[p], bins, blocks, None)
            continue
        mine = after(mine, done)
        far.append(swapped(mine, "chan", top))
        near.append(fanned(mine))
        left.append(left_sides(mine))
        ready = done
        result, done = cross(p, 0)
        if p:
            far[p - 1] = fanned(after(far[p - 1], ready) if p > 1 else far[p - 1])
            result, done = cross(p - 1, 1)
    if not stacked:
        far[-1] = fanned(after(far[-1], done))
        result, _ = cross(len(chunks) - 1, 1)
    return result


def solution(mesh):
    in_specs = (P("chan", "tm"), P(), P("tm"), P("tm"))
    out_specs = P("tm", None, "chan", None)
    return jax.shard_map(
        per_device, mesh=mesh, in_specs=in_specs, out_specs=out_specs, check_vma=False
    )
```

```python
import functools
import math

import jax
import jax.numpy as jnp
from jax import lax
from jax.experimental import pallas as pl
from jax.experimental.pallas import tpu as pltpu
from jax.sharding import PartitionSpec as P

L = 2048
HOP = 512
JITTER = 256
TAPS = 65
BINS = 64
K0 = 64
RIM = 128
GROUP = L // HOP
EDGE = RIM + JITTER
LANES = 2 * BINS
MIB = 1 << 20
F32 = jnp.float32
BF16 = jnp.bfloat16


def from_behind(shard, axis, by):
    devices = lax.axis_size(axis)
    pairs = [(i, i + by) for i in range(devices) if 0 <= i + by < devices]
    return lax.ppermute(shard, axis, pairs)


def matmul(a, b):
    return jnp.dot(a, b, preferred_element_type=F32)


def rotation(place):
    lane = lax.broadcasted_iota(jnp.int32, (8, LANES), 1)[:1]
    bins = K0 + (lane & (BINS - 1))
    angles = ((bins * place) & (L - 1)).astype(F32) * (2.0 * math.pi / L)
    sine = jnp.sin(angles)
    return jnp.cos(angles), jnp.where(lane < BINS, -sine, sine)


def turn(values, place):
    cosine, sine = rotation(jnp.full((8, LANES), place + L, jnp.int32))
    return values * cosine[:1] + pltpu.roll(values, BINS, 1) * sine[:1]


def edge_table(rise, fall, offset):
    start = JITTER - offset
    return jnp.concatenate([rise[pl.ds(start, RIM), :], fall[pl.ds(start, JITTER), :]], axis=0).astype(BF16)


def across(values):
    channels = values.shape[0]
    if channels % 128:
        values = jnp.pad(values, ((0, 128 - channels), (0, 0)))
    return values.T


def outbox_kernel(offsets, valid, whitening, record, out, taps):
    taps[...] = jnp.zeros_like(taps)
    for m in range(TAPS):
        taps[m : m + 1, :] = jnp.full((1, LANES), whitening[m], F32)
    top = record[0:8, :]
    row = lax.broadcasted_iota(jnp.int32, top.shape, 0)
    lane = lax.broadcasted_iota(jnp.int32, top.shape, 1)
    first = offsets.shape[0] - GROUP
    for q in range(GROUP):
        top = jnp.where((row == 0) & (lane == q), offsets[first + q].astype(F32), top)
        top = jnp.where((row == 0) & (lane == GROUP + q), valid[first + q].astype(F32), top)
    out[...] = jnp.concatenate([top, record[8:, :]], axis=0).astype(BF16)


def outbox(record, offsets, valid, whitening):
    channels, slab = record.shape
    smem = pl.BlockSpec(memory_space=pltpu.SMEM)
    return pl.pallas_call(
        outbox_kernel,
        grid=(1,),
        out_shape=(jax.ShapeDtypeStruct((channels, RIM), BF16), jax.ShapeDtypeStruct((TAPS + 7, LANES), F32)),
        in_specs=[smem, smem, smem, pl.BlockSpec((channels, RIM), lambda i: (0, slab // RIM - 1))],
        out_specs=(pl.BlockSpec(memory_space=pltpu.VMEM), pl.BlockSpec(memory_space=pltpu.VMEM)),
        compiler_params=pltpu.CompilerParams(vmem_limit_bytes=60 * MIB),
        name="outbox",
    )(offsets, valid, whitening, record)


def tables_kernel(taps, record, blocks, rise, fall, heads, sums, padded, lead, sem):
    fetch = pltpu.make_async_copy(record.at[:, pl.ds(0, lead.shape[1])], lead, sem)
    fetch.start()
    ramp_rows = TAPS - 1
    lane = lax.broadcasted_iota(jnp.int32, (8, LANES), 1)
    row = lax.broadcasted_iota(jnp.int32, (ramp_rows, LANES), 0)

    def phases(cosine, sine):
        half = lax.broadcasted_iota(jnp.int32, cosine.shape, 1) < BINS
        return jnp.where(half, cosine, sine * -1.0) * (1.0 / math.sqrt(L))

    first = phases(*rotation(row))
    padded[0:ramp_rows, :] = jnp.zeros((ramp_rows, LANES), F32)
    padded[ramp_rows : 2 * ramp_rows, :] = first
    padded[2 * ramp_rows :, :] = phases(*rotation(row[:8] + ramp_rows))
    ramp = jnp.zeros((ramp_rows, LANES), F32)
    gain = jnp.zeros((1, LANES), F32)
    for m in range(TAPS):
        tap = taps[m : m + 1, :]
        ramp = ramp + tap * padded[m : m + ramp_rows, :]
        gain = gain + tap * padded[ramp_rows + m : TAPS + m, :]
    gain = jnp.broadcast_to(gain * math.sqrt(L), (8, LANES))
    swapped = pltpu.roll(gain, BINS, 1)
    gain_re = jnp.where(lane < BINS, gain, swapped)[:1]
    gain_im = jnp.where(lane < BINS, -swapped, gain)[:1]
    cosine, sine = rotation(jnp.full((8, LANES), ramp_rows, jnp.int32))
    base = first * cosine[:1] + pltpu.roll(first, BINS, 1) * sine[:1]
    base = base * gain_re + pltpu.roll(base, BINS, 1) * gain_im
    other = pltpu.roll(base, BINS, 1)
    steps = L // ramp_rows
    onward = lax.broadcasted_iota(jnp.int32, (steps, LANES), 0)
    cosines, sines = rotation(L - onward * ramp_rows)
    ahead = JITTER // ramp_rows - 1
    for a in range(steps):
        pure = base * cosines[a : a + 1] + other * sines[a : a + 1]
        blocks[a * ramp_rows : (a + 1) * ramp_rows, :] = pure.astype(BF16)
        if a >= steps - ahead:
            at = (a - steps + ahead) * ramp_rows
            fall[at : at + ramp_rows, :] = pure
        if a == 0:
            fall[ahead * ramp_rows : JITTER, :] = pure - ramp
    fall[JITTER:, :] = jnp.zeros((fall.shape[0] - JITTER, LANES), F32)
    rise[...] = jnp.zeros_like(rise)
    rise[rise.shape[0] - ramp_rows :, :] = -ramp
    fetch.wait()
    heads[...] = lead[...].astype(BF16)
    total = None
    for q in range(GROUP - 1):
        found = matmul(heads[:, HOP * q : HOP * q + HOP], blocks[HOP * q : HOP * q + HOP, :])
        total = found if total is None else total + found
        sums[q] = total


def tables(taps, record):
    channels = record.shape[0]
    lead = L - HOP + JITTER
    vmem = pl.BlockSpec(memory_space=pltpu.VMEM)
    return pl.pallas_call(
        tables_kernel,
        out_shape=(
            jax.ShapeDtypeStruct((L, LANES), BF16),
            jax.ShapeDtypeStruct((EDGE, LANES), F32),
            jax.ShapeDtypeStruct((2 * JITTER, LANES), F32),
            jax.ShapeDtypeStruct((channels, lead), BF16),
            jax.ShapeDtypeStruct((GROUP - 1, channels, LANES), F32),
        ),
        in_specs=[vmem, pl.BlockSpec(memory_space=pl.ANY)],
        out_specs=(vmem,) * 5,
        scratch_shapes=[
            pltpu.VMEM((2 * TAPS + 6, LANES), F32),
            pltpu.VMEM((channels, lead), F32),
            pltpu.SemaphoreType.DMA,
        ],
        compiler_params=pltpu.CompilerParams(vmem_limit_bytes=50 * MIB),
        name="tables",
    )(taps, record)


def border_kernel(inbox, heads, sums, rise, fall, parts, done, collected):
    channels = heads.shape[0]
    done[...] = jnp.zeros_like(done)
    head = inbox[0:16, :].astype(F32)[:1]
    lane = lax.broadcasted_iota(jnp.int32, (1, LANES), 1)

    def told(at):
        return jnp.sum(jnp.where(lane == at, head, 0.0)).astype(jnp.int32)

    for q in range(GROUP):
        offset = told(q)
        edges = edge_table(rise, fall, offset)
        if q == 0:
            part = matmul(heads[:, 0:JITTER], edges[RIM:])
        else:
            part = matmul(heads[:, HOP * q - RIM : HOP * q + JITTER], edges)
            part = part + turn(sums[q - 1], HOP * q + offset - (TAPS - 1))
        upright = across(part * told(GROUP + q).astype(F32))
        for c in range(collected.shape[0]):
            piece = upright[:, 128 * c : 128 * c + 128]
            collected[c, pl.ds(q, BINS, stride=2 * GROUP), :] = piece[:BINS]
            collected[c, pl.ds(GROUP + q, BINS, stride=2 * GROUP), :] = piece[BINS:]
    width = min(128, channels)
    for c in range(collected.shape[0]):
        block = collected[c].reshape(BINS, 2 * GROUP, 128).astype(BF16)
        parts[:, :, width * c : width * c + width] = block[:, :, :width]


def border_parts(inbox, heads, sums, rise, fall):
    channels = heads.shape[0]
    vmem = pl.BlockSpec(memory_space=pltpu.VMEM)
    return pl.pallas_call(
        border_kernel,
        out_shape=(jax.ShapeDtypeStruct((BINS, 2 * GROUP, channels), BF16), jax.ShapeDtypeStruct((8, 128), F32)),
        in_specs=[vmem] * 5,
        out_specs=(vmem, vmem),
        scratch_shapes=[pltpu.VMEM((max(channels // 128, 1), 2 * GROUP * BINS, 128), F32)],
        compiler_params=pltpu.CompilerParams(vmem_limit_bytes=50 * MIB),
        cost_estimate=pl.CostEstimate(
            flops=2 * channels * LANES * 1536, bytes_accessed=8 * channels * L, transcendentals=0
        ),
        name="border_parts",
    )(inbox, heads, sums, rise, fall)


def spectra_kernel(offsets, valid, record, rim, blocks, rise, fall, order, out, samples, later, collected, sems):
    channels, slab = record.shape
    steps = slab // L
    windows = GROUP * steps

    def fetch(s):
        return pltpu.make_async_copy(
            record.at[:, pl.ds(L * s, L)], samples.at[:, pl.ds(RIM + L * s, L)], sems.at[s]
        )

    for s in range(steps):
        fetch(s).start()
    samples[:, 0:RIM] = rim[...].astype(F32)
    samples[:, RIM + slab :] = jnp.zeros((channels, samples.shape[1] - RIM - slab), F32)

    def block_sums(s):
        found = []
        for i in range(GROUP):
            begin = pl.multiple_of(RIM + L * s + HOP * i, 128)
            found.append(
                matmul(samples[:, pl.ds(begin, HOP)].astype(BF16), blocks[HOP * i : HOP * i + HOP, :])
            )
        return found

    def keep(found):
        total = found[GROUP - 1]
        later[GROUP - 1] = total
        for q in range(GROUP - 2, -1, -1):
            total = total + found[q]
            later[q] = total

    def one_window(w, q, before):
        offset = offsets[w]
        begin = pl.multiple_of(HOP * w, 128)
        ends = samples[:, pl.ds(begin + L, EDGE)] - samples[:, pl.ds(begin, EDGE)]
        part = matmul(ends.astype(BF16), edge_table(rise, fall, offset))
        total = later[q] if before is None else later[q] + before
        part = (part + turn(total, HOP * q + offset - (TAPS - 1))) * valid[w].astype(F32)
        upright = across(part)
        for c in range(collected.shape[0]):
            collected[c, pl.ds(w, LANES, stride=windows), :] = upright[:, 128 * c : 128 * c + 128]

    fetch(0).wait()
    keep(block_sums(0))

    @pl.loop(0, steps - 1)
    def _(s):
        fetch(s + 1).wait()
        found = block_sums(s + 1)
        before = None
        for q in range(GROUP):
            one_window(GROUP * s + q, q, before)
            before = found[q] if before is None else before + found[q]
        keep(found)

    for q in range(GROUP):
        one_window(GROUP * (steps - 1) + q, q, None)

    width = min(128, channels)
    for c in range(collected.shape[0]):
        block = collected[c].reshape(LANES, windows, 128).astype(BF16)
        for ri in range(2):
            part = block[BINS * ri : BINS * ri + BINS, :, :width]
            out[:, windows * ri : windows * ri + windows, width * c : width * c + width] = part


def own_spectra(record, rim, offsets, valid, transform, rise, fall, order):
    channels, slab = record.shape
    windows = offsets.shape[0]
    smem = pl.BlockSpec(memory_space=pltpu.SMEM)
    vmem = pl.BlockSpec(memory_space=pltpu.VMEM)
    return pl.pallas_call(
        spectra_kernel,
        out_shape=jax.ShapeDtypeStruct((BINS, 2 * windows, channels), BF16),
        in_specs=[smem, smem, pl.BlockSpec(memory_space=pl.ANY), vmem, vmem, vmem, vmem, vmem],
        out_specs=vmem,
        scratch_shapes=[
            pltpu.VMEM((channels, RIM + slab + L - HOP + JITTER), F32),
            pltpu.VMEM((GROUP, channels, LANES), F32),
            pltpu.VMEM((max(channels // 128, 1), LANES * windows, 128), F32),
            pltpu.SemaphoreType.DMA((slab // L,)),
        ],
        compiler_params=pltpu.CompilerParams(vmem_limit_bytes=50 * MIB),
        cost_estimate=pl.CostEstimate(
            flops=2 * channels * LANES * 896 * windows, bytes_accessed=4 * channels * slab, transcendentals=0
        ),
        name="own_spectra",
    )(offsets, valid, record, rim, transform, rise, fall, order)


def with_parts(block, part):
    windows = block.shape[1] // 2
    row = lax.broadcasted_iota(jnp.int32, part.shape, 1)
    moved = jnp.concatenate([part[:, GROUP:], part[:, :GROUP]], axis=1)
    pieces = []
    for ri, extra in enumerate((moved, part)):
        end = windows * ri + windows
        pieces.append(block[:, windows * ri : end - 2 * GROUP])
        pieces.append(block[:, end - 2 * GROUP : end] + jnp.where(row >= GROUP, extra, 0.0))
    return jnp.concatenate(pieces, axis=1)


def join_kernel(skip, own, parts, *chunks):
    *chunks, done = chunks
    done[...] = jnp.zeros_like(done)
    devices = chunks[0].shape[0]
    total = sum(chunk.shape[1] for chunk in chunks)
    for group in range(devices):
        begin = group * BINS // devices + skip
        end = begin + total
        joined = with_parts(own[begin:end].astype(F32), parts[begin:end].astype(F32)).astype(BF16)
        at = 0
        for chunk in chunks:
            chunk[group] = joined[at : at + chunk.shape[1]]
            at += chunk.shape[1]


def chunk_sizes(bins):
    count = min(3, bins)
    return [(bins + count - 1 - c) // count for c in range(count)]


def joined_chunks(own, parts, devices, skip, sizes):
    _, rows, channels = own.shape
    vmem = pl.BlockSpec(memory_space=pltpu.VMEM)
    *chunks, done = pl.pallas_call(
        functools.partial(join_kernel, skip),
        out_shape=tuple(jax.ShapeDtypeStruct((devices, count, rows, channels), BF16) for count in sizes)
        + (jax.ShapeDtypeStruct((8, 128), F32),),
        in_specs=[vmem, vmem],
        out_specs=(vmem,) * (len(sizes) + 1),
        compiler_params=pltpu.CompilerParams(vmem_limit_bytes=16 * MIB),
        name="joined_chunks",
    )(own, parts)
    return chunks, done


def left_kernel(own, out):
    sources, _, rows, channels = own.shape
    depth = sources * rows
    half = rows // 2
    straight = own[:, 0].astype(F32)
    turned = jnp.concatenate([straight[:, half:], -straight[:, :half]], axis=1)
    out[0, :channels] = straight.reshape(depth, channels).T.astype(BF16)
    out[0, channels:] = turned.reshape(depth, channels).T.astype(BF16)


def left_sides(own):
    sources, count, rows, channels = own.shape
    shape = (count, 2 * channels, sources * rows)
    return pl.pallas_call(
        left_kernel,
        grid=(count,),
        out_shape=jax.ShapeDtypeStruct(shape, BF16),
        in_specs=[pl.BlockSpec((sources, 1, rows, channels), lambda f: (0, f, 0, 0))],
        out_specs=pl.BlockSpec((1,) + shape[1:], lambda f: (f, 0, 0)),
        compiler_params=pltpu.CompilerParams(vmem_limit_bytes=16 * MIB),
        name="left_sides",
    )(own)


def cross_kernel(scale, stacked, me, left, *rest):
    out, done = rest[-2:]
    done[...] = jnp.zeros_like(done)
    sources, _, rows, channels = rest[0].shape[-4:]
    blocks = out.shape[3] // channels
    tile = min(256, channels)
    for n in range(blocks):
        if stacked:
            right, at = rest[0][n], channels * n
        else:
            right, at = rest[n][...], pl.multiple_of(channels * ((me[0] ^ n) & (blocks - 1)), 128)
        right = right[:, 0].reshape(sources * rows, channels)
        for j in range(0, channels, tile):
            for r in range(0, 2 * channels, tile):
                both = matmul(left[0, r : r + tile, :], right[:, j : j + tile]) * scale
                out[0, r // channels, r % channels : r % channels + tile, pl.ds(at + j, tile)] = both.astype(BF16)


def cross_products(left, right, result, begin, bins, blocks, first):
    sources, count, rows, channels = (right if first is None else right[0]).shape[-4:]
    columns = blocks if first is None else len(right)
    shape = (bins, 2, channels, blocks * channels)
    operands = [lax.axis_index("chan").astype(jnp.int32).reshape(1), left]
    in_specs = [pl.BlockSpec((1,) + left.shape[1:], lambda f, me: (f, 0, 0))]
    if first is None:
        operands.append(right)
        in_specs.append(pl.BlockSpec((blocks, sources, 1, rows, channels), lambda f, me: (0, 0, f, 0, 0)))
    else:
        operands += right
        in_specs += [pl.BlockSpec((sources, 1, rows, channels), lambda f, me: (0, f, 0, 0))] * columns
    if result is None:
        result, aliases = operands[1], {}
    else:
        aliases = {len(operands): 0}
    operands.append(result)
    in_specs.append(pl.BlockSpec(memory_space=pl.ANY))

    def place(f, me):
        return begin + f, 0, 0, 0 if first is None else (me[0] // columns) ^ (first // columns)

    return pl.pallas_call(
        functools.partial(cross_kernel, 2.0 / (sources * rows), first is None),
        grid_spec=pltpu.PrefetchScalarGridSpec(
            num_scalar_prefetch=1,
            grid=(count,),
            in_specs=in_specs,
            out_specs=(
                pl.BlockSpec((1, 2, channels, columns * channels), place),
                pl.BlockSpec((8, 128), lambda f, me: (0, 0)),
            ),
        ),
        out_shape=(jax.ShapeDtypeStruct(shape, BF16), jax.ShapeDtypeStruct((8, 128), F32)),
        input_output_aliases=aliases,
        compiler_params=pltpu.CompilerParams(vmem_limit_bytes=24 * MIB),
        cost_estimate=pl.CostEstimate(
            flops=4 * count * channels * columns * channels * sources * rows,
            bytes_accessed=4 * count * channels * columns * channels,
            transcendentals=0,
        ),
        name="cross_products",
    )(*operands)


def swapped(shard, axis, bit):
    devices = lax.axis_size(axis)
    return lax.ppermute(shard, axis, [(i, i ^ bit) for i in range(devices)])


def fan(shard, axis, bit):
    held = {0: shard}
    while bit:
        held.update({n | bit: swapped(block, axis, bit) for n, block in list(held.items())})
        bit //= 2
    return held


def after_kernel(shard, done, out):
    out[...] = shard[...]


def after(shard, done):
    if done is None:
        return shard
    vmem = pl.BlockSpec(memory_space=pltpu.VMEM)
    return pl.pallas_call(
        after_kernel,
        out_shape=jax.ShapeDtypeStruct(shard.shape, shard.dtype),
        in_specs=[vmem, vmem],
        out_specs=vmem,
        compiler_params=pltpu.CompilerParams(vmem_limit_bytes=8 * MIB),
        name="after",
    )(shard, done)


def per_device(record, whitening, offsets, window_valid):
    devices = lax.axis_size("tm")
    blocks = lax.axis_size("chan")
    stacked = blocks & (blocks - 1) != 0 or record.shape[0] % 128 != 0
    top = blocks // 2
    bins = BINS // devices

    def exchanged(chunk):
        return lax.all_to_all(chunk, "tm", split_axis=0, concat_axis=0, tiled=True)

    def fanned(shard):
        held = fan(shard, "chan", top // 2)
        return [held[n] for n in range(top)]

    inbox, taps = outbox(record, offsets, window_valid, whitening)
    inbox = from_behind(inbox, "tm", 1)
    transform, rise, fall, heads, sums = tables(taps, record)
    parts, done = border_parts(inbox, heads, sums, rise, fall)
    parts = from_behind(parts, "tm", -1)
    own = own_spectra(record, inbox, offsets, window_valid, transform, rise, fall, done)
    sizes = chunk_sizes(bins)
    begins = [sum(sizes[:p]) for p in range(len(sizes))]
    chunks, _ = joined_chunks(own, parts, devices, 0, sizes[:1])
    more, joined = joined_chunks(own, parts, devices, sizes[0], sizes[1:])
    chunks += more
    result, near, far, left, done = None, [], [], [], joined

    def cross(p, right, first):
        return cross_products(left[p], right, result, begins[p], bins, blocks, first)

    for p, chunk in enumerate(chunks):
        mine = exchanged(chunk)
        if stacked:
            right = lax.all_gather(mine, "chan", axis=0, tiled=False)
            result, _ = cross_products(left_sides(mine), right, result, begins[p], bins, blocks, None)
            continue
        mine = after(mine, done)
        far.append(swapped(mine, "chan", top))
        near.append(fanned(mine))
        left.append(left_sides(mine))
        ready = done
        result, done = cross(p, near[p], 0)
        if p:
            far[p - 1] = fanned(after(far[p - 1], ready) if p > 1 else far[p - 1])
            result, done = cross(p - 1, far[p - 1], top)
    if not stacked:
        for n, block in enumerate(fanned(after(far[-1], done))):
            result, _ = cross(len(chunks) - 1, [block], top + n)
    return result


def solution(mesh):
    in_specs = (P("chan", "tm"), P(), P("tm"), P("tm"))
    out_specs = P("tm", None, "chan", None)
    return jax.shard_map(
        per_device, mesh=mesh, in_specs=in_specs, out_specs=out_specs, check_vma=False
    )
```

```python
import functools
import math

import jax
import jax.numpy as jnp
from jax import lax
from jax.experimental import pallas as pl
from jax.experimental.pallas import tpu as pltpu
from jax.sharding import PartitionSpec as P

L = 2048
HOP = 512
JITTER = 256
TAPS = 65
BINS = 64
K0 = 64
RIM = 128
GROUP = L // HOP
EDGE = RIM + JITTER
LANES = 2 * BINS
MIB = 1 << 20
F32 = jnp.float32
BF16 = jnp.bfloat16


def from_behind(shard, axis, by):
    devices = lax.axis_size(axis)
    pairs = [(i, i + by) for i in range(devices) if 0 <= i + by < devices]
    return lax.ppermute(shard, axis, pairs)


def matmul(a, b):
    return jnp.dot(a, b, preferred_element_type=F32)


def rotation(place):
    lane = lax.broadcasted_iota(jnp.int32, (8, LANES), 1)[:1]
    bins = K0 + (lane & (BINS - 1))
    angles = ((bins * place) & (L - 1)).astype(F32) * (2.0 * math.pi / L)
    sine = jnp.sin(angles)
    return jnp.cos(angles), jnp.where(lane < BINS, -sine, sine)


def turn(values, place):
    cosine, sine = rotation(jnp.full((8, LANES), place + L, jnp.int32))
    return values * cosine[:1] + pltpu.roll(values, BINS, 1) * sine[:1]


def edge_table(rise, fall, offset):
    start = JITTER - offset
    return jnp.concatenate([rise[pl.ds(start, RIM), :], fall[pl.ds(start, JITTER), :]], axis=0).astype(BF16)


def across(values):
    channels = values.shape[0]
    if channels % 128:
        values = jnp.pad(values, ((0, 128 - channels), (0, 0)))
    return values.T


def outbox_kernel(offsets, valid, whitening, record, out, taps):
    taps[...] = jnp.zeros_like(taps)
    for m in range(TAPS):
        taps[m : m + 1, :] = jnp.full((1, LANES), whitening[m], F32)
    top = record[0:8, :]
    row = lax.broadcasted_iota(jnp.int32, top.shape, 0)
    lane = lax.broadcasted_iota(jnp.int32, top.shape, 1)
    first = offsets.shape[0] - GROUP
    for q in range(GROUP):
        top = jnp.where((row == 0) & (lane == q), offsets[first + q].astype(F32), top)
        top = jnp.where((row == 0) & (lane == GROUP + q), valid[first + q].astype(F32), top)
    out[...] = jnp.concatenate([top, record[8:, :]], axis=0).astype(BF16)


def outbox(record, offsets, valid, whitening):
    channels, slab = record.shape
    smem = pl.BlockSpec(memory_space=pltpu.SMEM)
    return pl.pallas_call(
        outbox_kernel,
        grid=(1,),
        out_shape=(jax.ShapeDtypeStruct((channels, RIM), BF16), jax.ShapeDtypeStruct((TAPS + 7, LANES), F32)),
        in_specs=[smem, smem, smem, pl.BlockSpec((channels, RIM), lambda i: (0, slab // RIM - 1))],
        out_specs=(pl.BlockSpec(memory_space=pltpu.VMEM), pl.BlockSpec(memory_space=pltpu.VMEM)),
        compiler_params=pltpu.CompilerParams(vmem_limit_bytes=60 * MIB),
        name="outbox",
    )(offsets, valid, whitening, record)


def tables_kernel(taps, record, blocks, rise, fall, heads, sums, padded, lead, sem):
    fetch = pltpu.make_async_copy(record.at[:, pl.ds(0, lead.shape[1])], lead, sem)
    fetch.start()
    ramp_rows = TAPS - 1
    lane = lax.broadcasted_iota(jnp.int32, (8, LANES), 1)
    row = lax.broadcasted_iota(jnp.int32, (ramp_rows, LANES), 0)

    def phases(cosine, sine):
        half = lax.broadcasted_iota(jnp.int32, cosine.shape, 1) < BINS
        return jnp.where(half, cosine, sine * -1.0) * (1.0 / math.sqrt(L))

    first = phases(*rotation(row))
    padded[0:ramp_rows, :] = jnp.zeros((ramp_rows, LANES), F32)
    padded[ramp_rows : 2 * ramp_rows, :] = first
    padded[2 * ramp_rows :, :] = phases(*rotation(row[:8] + ramp_rows))
    ramp = jnp.zeros((ramp_rows, LANES), F32)
    gain = jnp.zeros((1, LANES), F32)
    for m in range(TAPS):
        tap = taps[m : m + 1, :]
        ramp = ramp + tap * padded[m : m + ramp_rows, :]
        gain = gain + tap * padded[ramp_rows + m : TAPS + m, :]
    gain = jnp.broadcast_to(gain * math.sqrt(L), (8, LANES))
    swapped = pltpu.roll(gain, BINS, 1)
    gain_re = jnp.where(lane < BINS, gain, swapped)[:1]
    gain_im = jnp.where(lane < BINS, -swapped, gain)[:1]
    cosine, sine = rotation(jnp.full((8, LANES), ramp_rows, jnp.int32))
    base = first * cosine[:1] + pltpu.roll(first, BINS, 1) * sine[:1]
    base = base * gain_re + pltpu.roll(base, BINS, 1) * gain_im
    other = pltpu.roll(base, BINS, 1)
    steps = L // ramp_rows
    onward = lax.broadcasted_iota(jnp.int32, (steps, LANES), 0)
    cosines, sines = rotation(L - onward * ramp_rows)
    ahead = JITTER // ramp_rows - 1
    for a in range(steps):
        pure = base * cosines[a : a + 1] + other * sines[a : a + 1]
        blocks[a * ramp_rows : (a + 1) * ramp_rows, :] = pure.astype(BF16)
        if a >= steps - ahead:
            at = (a - steps + ahead) * ramp_rows
            fall[at : at + ramp_rows, :] = pure
        if a == 0:
            fall[ahead * ramp_rows : JITTER, :] = pure - ramp
    fall[JITTER:, :] = jnp.zeros((fall.shape[0] - JITTER, LANES), F32)
    rise[...] = jnp.zeros_like(rise)
    rise[rise.shape[0] - ramp_rows :, :] = -ramp
    fetch.wait()
    heads[...] = lead[...].astype(BF16)
    total = None
    for q in range(GROUP - 1):
        found = matmul(heads[:, HOP * q : HOP * q + HOP], blocks[HOP * q : HOP * q + HOP, :])
        total = found if total is None else total + found
        sums[q] = total


def tables(taps, record):
    channels = record.shape[0]
    lead = L - HOP + JITTER
    vmem = pl.BlockSpec(memory_space=pltpu.VMEM)
    return pl.pallas_call(
        tables_kernel,
        out_shape=(
            jax.ShapeDtypeStruct((L, LANES), BF16),
            jax.ShapeDtypeStruct((EDGE, LANES), F32),
            jax.ShapeDtypeStruct((2 * JITTER, LANES), F32),
            jax.ShapeDtypeStruct((channels, lead), BF16),
            jax.ShapeDtypeStruct((GROUP - 1, channels, LANES), F32),
        ),
        in_specs=[vmem, pl.BlockSpec(memory_space=pl.ANY)],
        out_specs=(vmem,) * 5,
        scratch_shapes=[
            pltpu.VMEM((2 * TAPS + 6, LANES), F32),
            pltpu.VMEM((channels, lead), F32),
            pltpu.SemaphoreType.DMA,
        ],
        compiler_params=pltpu.CompilerParams(vmem_limit_bytes=50 * MIB),
        name="tables",
    )(taps, record)


def border_kernel(inbox, heads, sums, rise, fall, parts, done, collected):
    channels = heads.shape[0]
    done[...] = jnp.zeros_like(done)
    head = inbox[0:16, :].astype(F32)[:1]
    lane = lax.broadcasted_iota(jnp.int32, (1, LANES), 1)

    def told(at):
        return jnp.sum(jnp.where(lane == at, head, 0.0)).astype(jnp.int32)

    for q in range(GROUP):
        offset = told(q)
        edges = edge_table(rise, fall, offset)
        if q == 0:
            part = matmul(heads[:, 0:JITTER], edges[RIM:])
        else:
            part = matmul(heads[:, HOP * q - RIM : HOP * q + JITTER], edges)
            part = part + turn(sums[q - 1], HOP * q + offset - (TAPS - 1))
        upright = across(part * told(GROUP + q).astype(F32))
        for c in range(collected.shape[0]):
            piece = upright[:, 128 * c : 128 * c + 128]
            collected[c, pl.ds(q, BINS, stride=2 * GROUP), :] = piece[:BINS]
            collected[c, pl.ds(GROUP + q, BINS, stride=2 * GROUP), :] = piece[BINS:]
    width = min(128, channels)
    for c in range(collected.shape[0]):
        block = collected[c].reshape(BINS, 2 * GROUP, 128).astype(BF16)
        parts[:, :, width * c : width * c + width] = block[:, :, :width]


def border_parts(inbox, heads, sums, rise, fall):
    channels = heads.shape[0]
    vmem = pl.BlockSpec(memory_space=pltpu.VMEM)
    return pl.pallas_call(
        border_kernel,
        out_shape=(jax.ShapeDtypeStruct((BINS, 2 * GROUP, channels), BF16), jax.ShapeDtypeStruct((8, 128), F32)),
        in_specs=[vmem] * 5,
        out_specs=(vmem, vmem),
        scratch_shapes=[pltpu.VMEM((max(channels // 128, 1), 2 * GROUP * BINS, 128), F32)],
        compiler_params=pltpu.CompilerParams(vmem_limit_bytes=50 * MIB),
        cost_estimate=pl.CostEstimate(
            flops=2 * channels * LANES * 1536, bytes_accessed=8 * channels * L, transcendentals=0
        ),
        name="border_parts",
    )(inbox, heads, sums, rise, fall)


def spectra_kernel(offsets, valid, record, rim, blocks, rise, fall, order, out, samples, later, collected, sems):
    channels, slab = record.shape
    steps = slab // L
    windows = GROUP * steps

    def fetch(s):
        return pltpu.make_async_copy(
            record.at[:, pl.ds(L * s, L)], samples.at[:, pl.ds(RIM + L * s, L)], sems.at[s]
        )

    for s in range(steps):
        fetch(s).start()
    samples[:, 0:RIM] = rim[...].astype(F32)
    samples[:, RIM + slab :] = jnp.zeros((channels, samples.shape[1] - RIM - slab), F32)

    def block_sums(s):
        found = []
        for i in range(GROUP):
            begin = pl.multiple_of(RIM + L * s + HOP * i, 128)
            found.append(
                matmul(samples[:, pl.ds(begin, HOP)].astype(BF16), blocks[HOP * i : HOP * i + HOP, :])
            )
        return found

    def keep(found):
        total = found[GROUP - 1]
        later[GROUP - 1] = total
        for q in range(GROUP - 2, -1, -1):
            total = total + found[q]
            later[q] = total

    def one_window(w, q, before):
        offset = offsets[w]
        begin = pl.multiple_of(HOP * w, 128)
        ends = samples[:, pl.ds(begin + L, EDGE)] - samples[:, pl.ds(begin, EDGE)]
        part = matmul(ends.astype(BF16), edge_table(rise, fall, offset))
        total = later[q] if before is None else later[q] + before
        part = (part + turn(total, HOP * q + offset - (TAPS - 1))) * valid[w].astype(F32)
        upright = across(part)
        for c in range(collected.shape[0]):
            collected[c, pl.ds(w, LANES, stride=windows), :] = upright[:, 128 * c : 128 * c + 128]

    fetch(0).wait()
    keep(block_sums(0))

    @pl.loop(0, steps - 1)
    def _(s):
        fetch(s + 1).wait()
        found = block_sums(s + 1)
        before = None
        for q in range(GROUP):
            one_window(GROUP * s + q, q, before)
            before = found[q] if before is None else before + found[q]
        keep(found)

    for q in range(GROUP):
        one_window(GROUP * (steps - 1) + q, q, None)

    width = min(128, channels)
    for c in range(collected.shape[0]):
        block = collected[c].reshape(LANES, windows, 128).astype(BF16)
        for ri in range(2):
            part = block[BINS * ri : BINS * ri + BINS, :, :width]
            out[:, windows * ri : windows * ri + windows, width * c : width * c + width] = part


def own_spectra(record, rim, offsets, valid, transform, rise, fall, order):
    channels, slab = record.shape
    windows = offsets.shape[0]
    smem = pl.BlockSpec(memory_space=pltpu.SMEM)
    vmem = pl.BlockSpec(memory_space=pltpu.VMEM)
    return pl.pallas_call(
        spectra_kernel,
        out_shape=jax.ShapeDtypeStruct((BINS, 2 * windows, channels), BF16),
        in_specs=[smem, smem, pl.BlockSpec(memory_space=pl.ANY), vmem, vmem, vmem, vmem, vmem],
        out_specs=vmem,
        scratch_shapes=[
            pltpu.VMEM((channels, RIM + slab + L - HOP + JITTER), F32),
            pltpu.VMEM((GROUP, channels, LANES), F32),
            pltpu.VMEM((max(channels // 128, 1), LANES * windows, 128), F32),
            pltpu.SemaphoreType.DMA((slab // L,)),
        ],
        compiler_params=pltpu.CompilerParams(vmem_limit_bytes=50 * MIB),
        cost_estimate=pl.CostEstimate(
            flops=2 * channels * LANES * 896 * windows, bytes_accessed=4 * channels * slab, transcendentals=0
        ),
        name="own_spectra",
    )(offsets, valid, record, rim, transform, rise, fall, order)


def with_parts(block, part):
    windows = block.shape[1] // 2
    row = lax.broadcasted_iota(jnp.int32, part.shape, 1)
    moved = jnp.concatenate([part[:, GROUP:], part[:, :GROUP]], axis=1)
    pieces = []
    for ri, extra in enumerate((moved, part)):
        end = windows * ri + windows
        pieces.append(block[:, windows * ri : end - 2 * GROUP])
        pieces.append(block[:, end - 2 * GROUP : end] + jnp.where(row >= GROUP, extra, 0.0))
    return jnp.concatenate(pieces, axis=1)


def join_kernel(skip, own, parts, *chunks):
    *chunks, done = chunks
    done[...] = jnp.zeros_like(done)
    devices = chunks[0].shape[0]
    total = sum(chunk.shape[1] for chunk in chunks)
    for group in range(devices):
        begin = group * BINS // devices + skip
        end = begin + total
        joined = with_parts(own[begin:end].astype(F32), parts[begin:end].astype(F32)).astype(BF16)
        at = 0
        for chunk in chunks:
            chunk[group] = joined[at : at + chunk.shape[1]]
            at += chunk.shape[1]


def first_join_kernel(own, parts, out, staged, sems):
    devices, count = staged.shape[:2]

    def leave(group):
        return pltpu.make_async_copy(staged.at[group], out.at[group], sems.at[group])

    for group in range(devices):
        begin = group * BINS // devices
        end = begin + count
        staged[group] = with_parts(own[begin:end].astype(F32), parts[begin:end].astype(F32)).astype(BF16)
        leave(group).start()
    for group in range(devices):
        leave(group).wait()


def first_chunk(own, parts, devices, count):
    _, rows, channels = own.shape
    vmem = pl.BlockSpec(memory_space=pltpu.VMEM)
    shape = (devices, count, rows, channels)
    return pl.pallas_call(
        first_join_kernel,
        out_shape=jax.ShapeDtypeStruct(shape, BF16),
        in_specs=[vmem, vmem],
        out_specs=pl.BlockSpec(memory_space=pl.ANY),
        scratch_shapes=[pltpu.VMEM(shape, BF16), pltpu.SemaphoreType.DMA((devices,))],
        compiler_params=pltpu.CompilerParams(vmem_limit_bytes=16 * MIB),
        name="first_chunk",
    )(own, parts)


def chunk_sizes(bins):
    count = min(3, bins)
    return [(bins + count - 1 - c) // count for c in range(count)]


def joined_chunks(own, parts, devices, skip, sizes):
    _, rows, channels = own.shape
    vmem = pl.BlockSpec(memory_space=pltpu.VMEM)
    *chunks, done = pl.pallas_call(
        functools.partial(join_kernel, skip),
        out_shape=tuple(jax.ShapeDtypeStruct((devices, count, rows, channels), BF16) for count in sizes)
        + (jax.ShapeDtypeStruct((8, 128), F32),),
        in_specs=[vmem, vmem],
        out_specs=(vmem,) * (len(sizes) + 1),
        compiler_params=pltpu.CompilerParams(vmem_limit_bytes=16 * MIB),
        name="joined_chunks",
    )(own, parts)
    return chunks, done


def left_kernel(own, out):
    sources, _, rows, channels = own.shape
    depth = sources * rows
    half = rows // 2
    straight = own[:, 0].astype(F32)
    turned = jnp.concatenate([straight[:, half:], -straight[:, :half]], axis=1)
    out[0, :channels] = straight.reshape(depth, channels).T.astype(BF16)
    out[0, channels:] = turned.reshape(depth, channels).T.astype(BF16)


def left_sides(own):
    sources, count, rows, channels = own.shape
    shape = (count, 2 * channels, sources * rows)
    return pl.pallas_call(
        left_kernel,
        grid=(count,),
        out_shape=jax.ShapeDtypeStruct(shape, BF16),
        in_specs=[pl.BlockSpec((sources, 1, rows, channels), lambda f: (0, f, 0, 0))],
        out_specs=pl.BlockSpec((1,) + shape[1:], lambda f: (f, 0, 0)),
        compiler_params=pltpu.CompilerParams(vmem_limit_bytes=16 * MIB),
        name="left_sides",
    )(own)


def cross_kernel(scale, stacked, resident, me, left, *rest):
    out, done = rest[-2:]
    done[...] = jnp.zeros_like(done)
    sources, _, rows, channels = rest[0].shape[-4:]
    blocks = out.shape[3] // channels
    f = pl.program_id(0) if resident else 0
    tile = min(256, channels)
    for n in range(blocks):
        if stacked:
            right, at = rest[0][n], channels * n
        else:
            right, at = rest[n][:, pl.ds(f, 1)], pl.multiple_of(channels * ((me[0] ^ n) & (blocks - 1)), 128)
        right = right[:, 0].reshape(sources * rows, channels)
        for j in range(0, channels, tile):
            for r in range(0, 2 * channels, tile):
                both = matmul(left[f, r : r + tile, :], right[:, j : j + tile]) * scale
                out[0, r // channels, r % channels : r % channels + tile, pl.ds(at + j, tile)] = both.astype(BF16)


def cross_products(left, right, result, begin, bins, blocks, first, resident=False):
    sources, count, rows, channels = (right if first is None else right[0]).shape[-4:]
    columns = blocks if first is None else len(right)
    shape = (bins, 2, channels, blocks * channels)
    operands = [lax.axis_index("chan").astype(jnp.int32).reshape(1), left]
    in_specs = [pl.BlockSpec((1,) + left.shape[1:], lambda f, me: (f, 0, 0))]
    if first is None:
        operands.append(right)
        in_specs.append(pl.BlockSpec((blocks, sources, 1, rows, channels), lambda f, me: (0, 0, f, 0, 0)))
    else:
        operands += right
        in_specs += [pl.BlockSpec((sources, 1, rows, channels), lambda f, me: (0, f, 0, 0))] * columns
    if resident:
        in_specs = [pl.BlockSpec(memory_space=pltpu.VMEM)] * len(in_specs)
    if result is None:
        result, aliases = operands[1], {}
    else:
        aliases = {len(operands): 0}
    operands.append(result)
    in_specs.append(pl.BlockSpec(memory_space=pl.ANY))

    def place(f, me):
        return begin + f, 0, 0, 0 if first is None else (me[0] // columns) ^ (first // columns)

    return pl.pallas_call(
        functools.partial(cross_kernel, 2.0 / (sources * rows), first is None, resident),
        grid_spec=pltpu.PrefetchScalarGridSpec(
            num_scalar_prefetch=1,
            grid=(count,),
            in_specs=in_specs,
            out_specs=(
                pl.BlockSpec((1, 2, channels, columns * channels), place),
                pl.BlockSpec((8, 128), lambda f, me: (0, 0)),
            ),
        ),
        out_shape=(jax.ShapeDtypeStruct(shape, BF16), jax.ShapeDtypeStruct((8, 128), F32)),
        input_output_aliases=aliases,
        compiler_params=pltpu.CompilerParams(vmem_limit_bytes=24 * MIB),
        cost_estimate=pl.CostEstimate(
            flops=4 * count * channels * columns * channels * sources * rows,
            bytes_accessed=4 * count * channels * columns * channels,
            transcendentals=0,
        ),
        name="cross_products",
    )(*operands)


def swapped(shard, axis, bit):
    devices = lax.axis_size(axis)
    return lax.ppermute(shard, axis, [(i, i ^ bit) for i in range(devices)])


def fan(shard, axis, bit):
    held = {0: shard}
    while bit:
        held.update({n | bit: swapped(block, axis, bit) for n, block in list(held.items())})
        bit //= 2
    return held


def after_kernel(shard, done, out):
    out[...] = shard[...]


def after(shard, done):
    if done is None:
        return shard
    vmem = pl.BlockSpec(memory_space=pltpu.VMEM)
    return pl.pallas_call(
        after_kernel,
        out_shape=jax.ShapeDtypeStruct(shard.shape, shard.dtype),
        in_specs=[vmem, vmem],
        out_specs=vmem,
        compiler_params=pltpu.CompilerParams(vmem_limit_bytes=8 * MIB),
        name="after",
    )(shard, done)


def per_device(record, whitening, offsets, window_valid):
    devices = lax.axis_size("tm")
    blocks = lax.axis_size("chan")
    stacked = blocks & (blocks - 1) != 0 or record.shape[0] % 128 != 0
    top = blocks // 2
    bins = BINS // devices

    def exchanged(chunk):
        return lax.all_to_all(chunk, "tm", split_axis=0, concat_axis=0, tiled=True)

    def fanned(shard):
        held = fan(shard, "chan", top // 2)
        return [held[n] for n in range(top)]

    inbox, taps = outbox(record, offsets, window_valid, whitening)
    inbox = from_behind(inbox, "tm", 1)
    transform, rise, fall, heads, sums = tables(taps, record)
    parts, done = border_parts(inbox, heads, sums, rise, fall)
    parts = from_behind(parts, "tm", -1)
    own = own_spectra(record, inbox, offsets, window_valid, transform, rise, fall, done)
    sizes = chunk_sizes(bins)
    begins = [sum(sizes[:p]) for p in range(len(sizes))]
    chunks = [first_chunk(own, parts, devices, sizes[0])]
    more, joined = joined_chunks(own, parts, devices, sizes[0], sizes[1:])
    chunks += more
    result, near, far, left, done = None, [], [], [], joined

    def cross(p, right, first, resident=False):
        return cross_products(left[p], right, result, begins[p], bins, blocks, first, resident)

    for p, chunk in enumerate(chunks):
        mine = exchanged(chunk)
        if stacked:
            right = lax.all_gather(mine, "chan", axis=0, tiled=False)
            result, _ = cross_products(left_sides(mine), right, result, begins[p], bins, blocks, None)
            continue
        mine = after(mine, done)
        far.append(swapped(mine, "chan", top))
        near.append(fanned(mine))
        left.append(left_sides(mine))
        ready = done
        result, done = cross(p, near[p], 0)
        if p:
            far[p - 1] = fanned(after(far[p - 1], ready) if p > 1 else far[p - 1])
            result, done = cross(p - 1, far[p - 1], top)
    if not stacked:
        for n, block in enumerate(fanned(after(far[-1], done))):
            result, _ = cross(len(chunks) - 1, [block], top + n, True)
    return result


def solution(mesh):
    in_specs = (P("chan", "tm"), P(), P("tm"), P("tm"))
    out_specs = P("tm", None, "chan", None)
    return jax.shard_map(
        per_device, mesh=mesh, in_specs=in_specs, out_specs=out_specs, check_vma=False
    )
```

```python
import functools
import math

import jax
import jax.numpy as jnp
from jax import lax
from jax.experimental import pallas as pl
from jax.experimental.pallas import tpu as pltpu
from jax.sharding import PartitionSpec as P

L = 2048
HOP = 512
JITTER = 256
TAPS = 65
BINS = 64
K0 = 64
RIM = 128
GROUP = L // HOP
EDGE = RIM + JITTER
LANES = 2 * BINS
MIB = 1 << 20
F32 = jnp.float32
BF16 = jnp.bfloat16


def from_behind(shard, axis, by):
    devices = lax.axis_size(axis)
    pairs = [(i, i + by) for i in range(devices) if 0 <= i + by < devices]
    return lax.ppermute(shard, axis, pairs)


def matmul(a, b):
    return jnp.dot(a, b, preferred_element_type=F32)


def rotation(place):
    lane = lax.broadcasted_iota(jnp.int32, (8, LANES), 1)[:1]
    bins = K0 + (lane & (BINS - 1))
    angles = ((bins * place) & (L - 1)).astype(F32) * (2.0 * math.pi / L)
    sine = jnp.sin(angles)
    return jnp.cos(angles), jnp.where(lane < BINS, -sine, sine)


def turn(values, place):
    cosine, sine = rotation(jnp.full((8, LANES), place + L, jnp.int32))
    return values * cosine[:1] + pltpu.roll(values, BINS, 1) * sine[:1]


def edge_table(rise, fall, offset):
    start = JITTER - offset
    return jnp.concatenate([rise[pl.ds(start, RIM), :], fall[pl.ds(start, JITTER), :]], axis=0).astype(BF16)


def across(values):
    channels = values.shape[0]
    if channels % 128:
        values = jnp.pad(values, ((0, 128 - channels), (0, 0)))
    return values.T


def outbox_kernel(offsets, valid, whitening, record, out, taps):
    taps[...] = jnp.zeros_like(taps)
    for m in range(TAPS):
        taps[m : m + 1, :] = jnp.full((1, LANES), whitening[m], F32)
    top = record[0:8, :]
    row = lax.broadcasted_iota(jnp.int32, top.shape, 0)
    lane = lax.broadcasted_iota(jnp.int32, top.shape, 1)
    first = offsets.shape[0] - GROUP
    for q in range(GROUP):
        top = jnp.where((row == 0) & (lane == q), offsets[first + q].astype(F32), top)
        top = jnp.where((row == 0) & (lane == GROUP + q), valid[first + q].astype(F32), top)
    out[...] = jnp.concatenate([top, record[8:, :]], axis=0).astype(BF16)


def outbox(record, offsets, valid, whitening):
    channels, slab = record.shape
    smem = pl.BlockSpec(memory_space=pltpu.SMEM)
    return pl.pallas_call(
        outbox_kernel,
        grid=(1,),
        out_shape=(jax.ShapeDtypeStruct((channels, RIM), BF16), jax.ShapeDtypeStruct((TAPS + 7, LANES), F32)),
        in_specs=[smem, smem, smem, pl.BlockSpec((channels, RIM), lambda i: (0, slab // RIM - 1))],
        out_specs=(pl.BlockSpec(memory_space=pltpu.VMEM), pl.BlockSpec(memory_space=pltpu.VMEM)),
        compiler_params=pltpu.CompilerParams(vmem_limit_bytes=60 * MIB),
        name="outbox",
    )(offsets, valid, whitening, record)


def tables_kernel(taps, record, blocks, rise, fall, heads, sums, padded, lead, sem):
    fetch = pltpu.make_async_copy(record.at[:, pl.ds(0, lead.shape[1])], lead, sem)
    fetch.start()
    ramp_rows = TAPS - 1
    lane = lax.broadcasted_iota(jnp.int32, (8, LANES), 1)
    row = lax.broadcasted_iota(jnp.int32, (ramp_rows, LANES), 0)

    def phases(cosine, sine):
        half = lax.broadcasted_iota(jnp.int32, cosine.shape, 1) < BINS
        return jnp.where(half, cosine, sine * -1.0) * (1.0 / math.sqrt(L))

    first = phases(*rotation(row))
    padded[0:ramp_rows, :] = jnp.zeros((ramp_rows, LANES), F32)
    padded[ramp_rows : 2 * ramp_rows, :] = first
    padded[2 * ramp_rows :, :] = phases(*rotation(row[:8] + ramp_rows))
    ramp = jnp.zeros((ramp_rows, LANES), F32)
    gain = jnp.zeros((1, LANES), F32)
    for m in range(TAPS):
        tap = taps[m : m + 1, :]
        ramp = ramp + tap * padded[m : m + ramp_rows, :]
        gain = gain + tap * padded[ramp_rows + m : TAPS + m, :]
    gain = jnp.broadcast_to(gain * math.sqrt(L), (8, LANES))
    swapped = pltpu.roll(gain, BINS, 1)
    gain_re = jnp.where(lane < BINS, gain, swapped)[:1]
    gain_im = jnp.where(lane < BINS, -swapped, gain)[:1]
    cosine, sine = rotation(jnp.full((8, LANES), ramp_rows, jnp.int32))
    base = first * cosine[:1] + pltpu.roll(first, BINS, 1) * sine[:1]
    base = base * gain_re + pltpu.roll(base, BINS, 1) * gain_im
    other = pltpu.roll(base, BINS, 1)
    steps = L // ramp_rows
    onward = lax.broadcasted_iota(jnp.int32, (steps, LANES), 0)
    cosines, sines = rotation(L - onward * ramp_rows)
    ahead = JITTER // ramp_rows - 1
    for a in range(steps):
        pure = base * cosines[a : a + 1] + other * sines[a : a + 1]
        blocks[a * ramp_rows : (a + 1) * ramp_rows, :] = pure.astype(BF16)
        if a >= steps - ahead:
            at = (a - steps + ahead) * ramp_rows
            fall[at : at + ramp_rows, :] = pure
        if a == 0:
            fall[ahead * ramp_rows : JITTER, :] = pure - ramp
    fall[JITTER:, :] = jnp.zeros((fall.shape[0] - JITTER, LANES), F32)
    rise[...] = jnp.zeros_like(rise)
    rise[rise.shape[0] - ramp_rows :, :] = -ramp
    fetch.wait()
    heads[...] = lead[...].astype(BF16)
    total = None
    for q in range(GROUP - 1):
        found = matmul(heads[:, HOP * q : HOP * q + HOP], blocks[HOP * q : HOP * q + HOP, :])
        total = found if total is None else total + found
        sums[q] = total


def tables(taps, record):
    channels = record.shape[0]
    lead = L - HOP + JITTER
    vmem = pl.BlockSpec(memory_space=pltpu.VMEM)
    return pl.pallas_call(
        tables_kernel,
        out_shape=(
            jax.ShapeDtypeStruct((L, LANES), BF16),
            jax.ShapeDtypeStruct((EDGE, LANES), F32),
            jax.ShapeDtypeStruct((2 * JITTER, LANES), F32),
            jax.ShapeDtypeStruct((channels, lead), BF16),
            jax.ShapeDtypeStruct((GROUP - 1, channels, LANES), F32),
        ),
        in_specs=[vmem, pl.BlockSpec(memory_space=pl.ANY)],
        out_specs=(vmem,) * 5,
        scratch_shapes=[
            pltpu.VMEM((2 * TAPS + 6, LANES), F32),
            pltpu.VMEM((channels, lead), F32),
            pltpu.SemaphoreType.DMA,
        ],
        compiler_params=pltpu.CompilerParams(vmem_limit_bytes=50 * MIB),
        name="tables",
    )(taps, record)


def border_kernel(inbox, heads, sums, rise, fall, parts, done, collected):
    channels = heads.shape[0]
    done[...] = jnp.zeros_like(done)
    head = inbox[0:16, :].astype(F32)[:1]
    lane = lax.broadcasted_iota(jnp.int32, (1, LANES), 1)

    def told(at):
        return jnp.sum(jnp.where(lane == at, head, 0.0)).astype(jnp.int32)

    for q in range(GROUP):
        offset = told(q)
        edges = edge_table(rise, fall, offset)
        if q == 0:
            part = matmul(heads[:, 0:JITTER], edges[RIM:])
        else:
            part = matmul(heads[:, HOP * q - RIM : HOP * q + JITTER], edges)
            part = part + turn(sums[q - 1], HOP * q + offset - (TAPS - 1))
        upright = across(part * told(GROUP + q).astype(F32))
        for c in range(collected.shape[0]):
            piece = upright[:, 128 * c : 128 * c + 128]
            collected[c, pl.ds(q, BINS, stride=2 * GROUP), :] = piece[:BINS]
            collected[c, pl.ds(GROUP + q, BINS, stride=2 * GROUP), :] = piece[BINS:]
    width = min(128, channels)
    for c in range(collected.shape[0]):
        block = collected[c, : 2 * GROUP * BINS].reshape(BINS, 2 * GROUP, 128).astype(BF16)
        parts[:, :, width * c : width * c + width] = block[:, :, :width]


def border_parts(inbox, heads, sums, rise, fall):
    channels = heads.shape[0]
    vmem = pl.BlockSpec(memory_space=pltpu.VMEM)
    return pl.pallas_call(
        border_kernel,
        out_shape=(jax.ShapeDtypeStruct((BINS, 2 * GROUP, channels), BF16), jax.ShapeDtypeStruct((8, 128), F32)),
        in_specs=[vmem] * 5,
        out_specs=(vmem, vmem),
        scratch_shapes=[pltpu.VMEM((max(channels // 128, 1), 2 * GROUP * BINS + 2 * GROUP, 128), F32)],
        compiler_params=pltpu.CompilerParams(vmem_limit_bytes=50 * MIB),
        cost_estimate=pl.CostEstimate(
            flops=2 * channels * LANES * 1536, bytes_accessed=8 * channels * L, transcendentals=0
        ),
        name="border_parts",
    )(inbox, heads, sums, rise, fall)


def spectra_kernel(offsets, valid, record, rim, blocks, rise, fall, order, out, samples, later, collected, sems):
    channels, slab = record.shape
    steps = slab // L
    windows = GROUP * steps

    def fetch(s):
        return pltpu.make_async_copy(
            record.at[:, pl.ds(L * s, L)], samples.at[:, pl.ds(RIM + L * s, L)], sems.at[s]
        )

    for s in range(steps):
        fetch(s).start()
    samples[:, 0:RIM] = rim[...].astype(F32)
    samples[:, RIM + slab :] = jnp.zeros((channels, samples.shape[1] - RIM - slab), F32)

    def block_sums(s):
        found = []
        for i in range(GROUP):
            begin = pl.multiple_of(RIM + L * s + HOP * i, 128)
            found.append(
                matmul(samples[:, pl.ds(begin, HOP)].astype(BF16), blocks[HOP * i : HOP * i + HOP, :])
            )
        return found

    def keep(found):
        total = found[GROUP - 1]
        later[GROUP - 1] = total
        for q in range(GROUP - 2, -1, -1):
            total = total + found[q]
            later[q] = total

    def one_window(w, q, before):
        offset = offsets[w]
        begin = pl.multiple_of(HOP * w, 128)
        ends = samples[:, pl.ds(begin + L, EDGE)] - samples[:, pl.ds(begin, EDGE)]
        part = matmul(ends.astype(BF16), edge_table(rise, fall, offset))
        total = later[q] if before is None else later[q] + before
        part = (part + turn(total, HOP * q + offset - (TAPS - 1))) * valid[w].astype(F32)
        upright = across(part)
        for c in range(collected.shape[0]):
            collected[c, pl.ds(w, LANES, stride=windows), :] = upright[:, 128 * c : 128 * c + 128]

    fetch(0).wait()
    keep(block_sums(0))

    @pl.loop(0, steps - 1)
    def _(s):
        fetch(s + 1).wait()
        found = block_sums(s + 1)
        before = None
        for q in range(GROUP):
            one_window(GROUP * s + q, q, before)
            before = found[q] if before is None else before + found[q]
        keep(found)

    for q in range(GROUP):
        one_window(GROUP * (steps - 1) + q, q, None)

    width = min(128, channels)
    for c in range(collected.shape[0]):
        block = collected[c, : LANES * windows].reshape(LANES, windows, 128).astype(BF16)
        for ri in range(2):
            part = block[BINS * ri : BINS * ri + BINS, :, :width]
            out[:, windows * ri : windows * ri + windows, width * c : width * c + width] = part


def own_spectra(record, rim, offsets, valid, transform, rise, fall, order):
    channels, slab = record.shape
    windows = offsets.shape[0]
    smem = pl.BlockSpec(memory_space=pltpu.SMEM)
    vmem = pl.BlockSpec(memory_space=pltpu.VMEM)
    return pl.pallas_call(
        spectra_kernel,
        out_shape=jax.ShapeDtypeStruct((BINS, 2 * windows, channels), BF16),
        in_specs=[smem, smem, pl.BlockSpec(memory_space=pl.ANY), vmem, vmem, vmem, vmem, vmem],
        out_specs=vmem,
        scratch_shapes=[
            pltpu.VMEM((channels, RIM + slab + L - HOP + JITTER), F32),
            pltpu.VMEM((GROUP, channels, LANES), F32),
            pltpu.VMEM((max(channels // 128, 1), LANES * windows + windows, 128), F32),
            pltpu.SemaphoreType.DMA((slab // L,)),
        ],
        compiler_params=pltpu.CompilerParams(vmem_limit_bytes=50 * MIB),
        cost_estimate=pl.CostEstimate(
            flops=2 * channels * LANES * 896 * windows, bytes_accessed=4 * channels * slab, transcendentals=0
        ),
        name="own_spectra",
    )(offsets, valid, record, rim, transform, rise, fall, order)


def with_parts(block, part):
    windows = block.shape[1] // 2
    row = lax.broadcasted_iota(jnp.int32, part.shape, 1)
    moved = jnp.concatenate([part[:, GROUP:], part[:, :GROUP]], axis=1)
    pieces = []
    for ri, extra in enumerate((moved, part)):
        end = windows * ri + windows
        pieces.append(block[:, windows * ri : end - 2 * GROUP])
        pieces.append(block[:, end - 2 * GROUP : end] + jnp.where(row >= GROUP, extra, 0.0))
    return jnp.concatenate(pieces, axis=1)


def join_kernel(skip, own, parts, *chunks):
    *chunks, done = chunks
    done[...] = jnp.zeros_like(done)
    devices = chunks[0].shape[0]
    total = sum(chunk.shape[1] for chunk in chunks)
    for group in range(devices):
        begin = group * BINS // devices + skip
        end = begin + total
        joined = with_parts(own[begin:end].astype(F32), parts[begin:end].astype(F32)).astype(BF16)
        at = 0
        for chunk in chunks:
            chunk[group] = joined[at : at + chunk.shape[1]]
            at += chunk.shape[1]


def chunk_sizes(bins):
    count = min(3, bins)
    return [(bins + count - 1 - c) // count for c in range(count)]


def joined_chunks(own, parts, devices, skip, sizes):
    _, rows, channels = own.shape
    vmem = pl.BlockSpec(memory_space=pltpu.VMEM)
    *chunks, done = pl.pallas_call(
        functools.partial(join_kernel, skip),
        out_shape=tuple(jax.ShapeDtypeStruct((devices, count, rows, channels), BF16) for count in sizes)
        + (jax.ShapeDtypeStruct((8, 128), F32),),
        in_specs=[vmem, vmem],
        out_specs=(vmem,) * (len(sizes) + 1),
        compiler_params=pltpu.CompilerParams(vmem_limit_bytes=16 * MIB),
        name="joined_chunks",
    )(own, parts)
    return chunks, done


def left_kernel(own, out):
    sources, _, rows, channels = own.shape
    depth = sources * rows
    half = rows // 2
    straight = own[:, 0].astype(F32)
    turned = jnp.concatenate([straight[:, half:], -straight[:, :half]], axis=1)
    out[0, :channels] = straight.reshape(depth, channels).T.astype(BF16)
    out[0, channels:] = turned.reshape(depth, channels).T.astype(BF16)


def left_sides(own):
    sources, count, rows, channels = own.shape
    shape = (count, 2 * channels, sources * rows)
    return pl.pallas_call(
        left_kernel,
        grid=(count,),
        out_shape=jax.ShapeDtypeStruct(shape, BF16),
        in_specs=[pl.BlockSpec((sources, 1, rows, channels), lambda f: (0, f, 0, 0))],
        out_specs=pl.BlockSpec((1,) + shape[1:], lambda f: (f, 0, 0)),
        compiler_params=pltpu.CompilerParams(vmem_limit_bytes=16 * MIB),
        name="left_sides",
    )(own)


def cross_kernel(scale, stacked, me, left, *rest):
    out, done = rest[-2:]
    done[...] = jnp.zeros_like(done)
    sources, _, rows, channels = rest[0].shape[-4:]
    blocks = out.shape[3] // channels
    tile = min(256, channels)
    for n in range(blocks):
        if stacked:
            right, at = rest[0][n], channels * n
        else:
            right, at = rest[n][...], pl.multiple_of(channels * ((me[0] ^ n) & (blocks - 1)), 128)
        right = right[:, 0].reshape(sources * rows, channels)
        for j in range(0, channels, tile):
            for ri in range(2):
                both = matmul(left[0, channels * ri : channels * ri + channels, :], right[:, j : j + tile]) * scale
                out[0, ri, :, pl.ds(at + j, tile)] = both.astype(BF16)


def cross_products(left, right, result, begin, bins, blocks, first):
    sources, count, rows, channels = (right if first is None else right[0]).shape[-4:]
    columns = blocks if first is None else len(right)
    shape = (bins, 2, channels, blocks * channels)
    operands = [lax.axis_index("chan").astype(jnp.int32).reshape(1), left]
    in_specs = [pl.BlockSpec((1,) + left.shape[1:], lambda f, me: (f, 0, 0))]
    if first is None:
        operands.append(right)
        in_specs.append(pl.BlockSpec((blocks, sources, 1, rows, channels), lambda f, me: (0, 0, f, 0, 0)))
    else:
        operands += right
        in_specs += [pl.BlockSpec((sources, 1, rows, channels), lambda f, me: (0, f, 0, 0))] * columns
    if result is None:
        result, aliases = operands[1], {}
    else:
        aliases = {len(operands): 0}
    operands.append(result)
    in_specs.append(pl.BlockSpec(memory_space=pl.ANY))

    def place(f, me):
        return begin + f, 0, 0, 0 if first is None else (me[0] // columns) ^ (first // columns)

    return pl.pallas_call(
        functools.partial(cross_kernel, 2.0 / (sources * rows), first is None),
        grid_spec=pltpu.PrefetchScalarGridSpec(
            num_scalar_prefetch=1,
            grid=(count,),
            in_specs=in_specs,
            out_specs=(
                pl.BlockSpec((1, 2, channels, columns * channels), place),
                pl.BlockSpec((8, 128), lambda f, me: (0, 0)),
            ),
        ),
        out_shape=(jax.ShapeDtypeStruct(shape, BF16), jax.ShapeDtypeStruct((8, 128), F32)),
        input_output_aliases=aliases,
        compiler_params=pltpu.CompilerParams(vmem_limit_bytes=24 * MIB),
        cost_estimate=pl.CostEstimate(
            flops=4 * count * channels * columns * channels * sources * rows,
            bytes_accessed=4 * count * channels * columns * channels,
            transcendentals=0,
        ),
        name="cross_products",
    )(*operands)


def swapped(shard, axis, bit):
    devices = lax.axis_size(axis)
    return lax.ppermute(shard, axis, [(i, i ^ bit) for i in range(devices)])


def fan(shard, axis, bit):
    held = {0: shard}
    while bit:
        held.update({n | bit: swapped(block, axis, bit) for n, block in list(held.items())})
        bit //= 2
    return held


def after_kernel(shard, done, out):
    out[...] = shard[...]


def after(shard, done):
    if done is None:
        return shard
    vmem = pl.BlockSpec(memory_space=pltpu.VMEM)
    return pl.pallas_call(
        after_kernel,
        out_shape=jax.ShapeDtypeStruct(shard.shape, shard.dtype),
        in_specs=[vmem, vmem],
        out_specs=vmem,
        compiler_params=pltpu.CompilerParams(vmem_limit_bytes=8 * MIB),
        name="after",
    )(shard, done)


def per_device(record, whitening, offsets, window_valid):
    devices = lax.axis_size("tm")
    blocks = lax.axis_size("chan")
    stacked = blocks & (blocks - 1) != 0 or record.shape[0] % 128 != 0
    top = blocks // 2
    bins = BINS // devices

    def exchanged(chunk):
        return lax.all_to_all(chunk, "tm", split_axis=0, concat_axis=0, tiled=True)

    def fanned(shard):
        held = fan(shard, "chan", top // 2)
        return [held[n] for n in range(top)]

    inbox, taps = outbox(record, offsets, window_valid, whitening)
    inbox = from_behind(inbox, "tm", 1)
    transform, rise, fall, heads, sums = tables(taps, record)
    parts, done = border_parts(inbox, heads, sums, rise, fall)
    parts = from_behind(parts, "tm", -1)
    own = own_spectra(record, inbox, offsets, window_valid, transform, rise, fall, done)
    sizes = chunk_sizes(bins)
    begins = [sum(sizes[:p]) for p in range(len(sizes))]
    chunks, _ = joined_chunks(own, parts, devices, 0, sizes[:1])
    more, joined = joined_chunks(own, parts, devices, sizes[0], sizes[1:])
    chunks += more
    result, near, far, left, done = None, [], [], [], joined

    def cross(p, right, first):
        return cross_products(left[p], right, result, begins[p], bins, blocks, first)

    for p, chunk in enumerate(chunks):
        mine = exchanged(chunk)
        if stacked:
            right = lax.all_gather(mine, "chan", axis=0, tiled=False)
            result, _ = cross_products(left_sides(mine), right, result, begins[p], bins, blocks, None)
            continue
        mine = after(mine, done)
        far.append(swapped(mine, "chan", top))
        near.append(fanned(mine))
        left.append(left_sides(mine))
        ready = done
        result, done = cross(p, near[p], 0)
        if p:
            far[p - 1] = fanned(after(far[p - 1], ready) if p > 1 else far[p - 1])
            result, done = cross(p - 1, far[p - 1], top)
    if not stacked:
        for n, block in enumerate(fanned(after(far[-1], done))):
            result, _ = cross(len(chunks) - 1, [block], top + n)
    return result


def solution(mesh):
    in_specs = (P("chan", "tm"), P(), P("tm"), P("tm"))
    out_specs = P("tm", None, "chan", None)
    return jax.shard_map(
        per_device, mesh=mesh, in_specs=in_specs, out_specs=out_specs, check_vma=False
    )
```

```python
import functools
import math

import jax
import jax.numpy as jnp
from jax import lax
from jax.experimental import pallas as pl
from jax.experimental.pallas import tpu as pltpu
from jax.sharding import PartitionSpec as P

L = 2048
HOP = 512
JITTER = 256
TAPS = 65
BINS = 64
K0 = 64
RIM = 128
GROUP = L // HOP
EDGE = RIM + JITTER
LANES = 2 * BINS
MIB = 1 << 20
F32 = jnp.float32
BF16 = jnp.bfloat16


def from_behind(shard, axis, by):
    devices = lax.axis_size(axis)
    pairs = [(i, i + by) for i in range(devices) if 0 <= i + by < devices]
    return lax.ppermute(shard, axis, pairs)


def matmul(a, b):
    return jnp.dot(a, b, preferred_element_type=F32)


def rotation(place):
    lane = lax.broadcasted_iota(jnp.int32, (8, LANES), 1)[:1]
    bins = K0 + (lane & (BINS - 1))
    angles = ((bins * place) & (L - 1)).astype(F32) * (2.0 * math.pi / L)
    sine = jnp.sin(angles)
    return jnp.cos(angles), jnp.where(lane < BINS, -sine, sine)


def turn(values, place):
    cosine, sine = rotation(jnp.full((8, LANES), place + L, jnp.int32))
    return values * cosine[:1] + pltpu.roll(values, BINS, 1) * sine[:1]


def edge_table(rise, fall, offset):
    start = JITTER - offset
    return jnp.concatenate([rise[pl.ds(start, RIM), :], fall[pl.ds(start, JITTER), :]], axis=0).astype(BF16)


def across(values):
    channels = values.shape[0]
    if channels % 128:
        values = jnp.pad(values, ((0, 128 - channels), (0, 0)))
    return values.T


def outbox_kernel(offsets, valid, whitening, record, out, taps):
    taps[...] = jnp.zeros_like(taps)
    for m in range(TAPS):
        taps[m : m + 1, :] = jnp.full((1, LANES), whitening[m], F32)
    top = record[0:8, :]
    row = lax.broadcasted_iota(jnp.int32, top.shape, 0)
    lane = lax.broadcasted_iota(jnp.int32, top.shape, 1)
    first = offsets.shape[0] - GROUP
    for q in range(GROUP):
        top = jnp.where((row == 0) & (lane == q), offsets[first + q].astype(F32), top)
        top = jnp.where((row == 0) & (lane == GROUP + q), valid[first + q].astype(F32), top)
    out[...] = jnp.concatenate([top, record[8:, :]], axis=0).astype(BF16)


def outbox(record, offsets, valid, whitening):
    channels, slab = record.shape
    smem = pl.BlockSpec(memory_space=pltpu.SMEM)
    return pl.pallas_call(
        outbox_kernel,
        grid=(1,),
        out_shape=(jax.ShapeDtypeStruct((channels, RIM), BF16), jax.ShapeDtypeStruct((TAPS + 7, LANES), F32)),
        in_specs=[smem, smem, smem, pl.BlockSpec((channels, RIM), lambda i: (0, slab // RIM - 1))],
        out_specs=(pl.BlockSpec(memory_space=pltpu.VMEM), pl.BlockSpec(memory_space=pltpu.VMEM)),
        compiler_params=pltpu.CompilerParams(vmem_limit_bytes=60 * MIB),
        name="outbox",
    )(offsets, valid, whitening, record)


def tables_kernel(taps, record, blocks, rise, fall, heads, sums, padded, lead, sem):
    fetch = pltpu.make_async_copy(record.at[:, pl.ds(0, lead.shape[1])], lead, sem)
    fetch.start()
    ramp_rows = TAPS - 1
    lane = lax.broadcasted_iota(jnp.int32, (8, LANES), 1)
    row = lax.broadcasted_iota(jnp.int32, (ramp_rows, LANES), 0)

    def phases(cosine, sine):
        half = lax.broadcasted_iota(jnp.int32, cosine.shape, 1) < BINS
        return jnp.where(half, cosine, sine * -1.0) * (1.0 / math.sqrt(L))

    first = phases(*rotation(row))
    padded[0:ramp_rows, :] = jnp.zeros((ramp_rows, LANES), F32)
    padded[ramp_rows : 2 * ramp_rows, :] = first
    padded[2 * ramp_rows :, :] = phases(*rotation(row[:8] + ramp_rows))
    ramp = jnp.zeros((ramp_rows, LANES), F32)
    gain = jnp.zeros((1, LANES), F32)
    for m in range(TAPS):
        tap = taps[m : m + 1, :]
        ramp = ramp + tap * padded[m : m + ramp_rows, :]
        gain = gain + tap * padded[ramp_rows + m : TAPS + m, :]
    gain = jnp.broadcast_to(gain * math.sqrt(L), (8, LANES))
    swapped = pltpu.roll(gain, BINS, 1)
    gain_re = jnp.where(lane < BINS, gain, swapped)[:1]
    gain_im = jnp.where(lane < BINS, -swapped, gain)[:1]
    cosine, sine = rotation(jnp.full((8, LANES), ramp_rows, jnp.int32))
    base = first * cosine[:1] + pltpu.roll(first, BINS, 1) * sine[:1]
    base = base * gain_re + pltpu.roll(base, BINS, 1) * gain_im
    other = pltpu.roll(base, BINS, 1)
    steps = L // ramp_rows
    onward = lax.broadcasted_iota(jnp.int32, (steps, LANES), 0)
    cosines, sines = rotation(L - onward * ramp_rows)
    ahead = JITTER // ramp_rows - 1
    for a in range(steps):
        pure = base * cosines[a : a + 1] + other * sines[a : a + 1]
        blocks[a * ramp_rows : (a + 1) * ramp_rows, :] = pure.astype(BF16)
        if a >= steps - ahead:
            at = (a - steps + ahead) * ramp_rows
            fall[at : at + ramp_rows, :] = pure
        if a == 0:
            fall[ahead * ramp_rows : JITTER, :] = pure - ramp
    fall[JITTER:, :] = jnp.zeros((fall.shape[0] - JITTER, LANES), F32)
    rise[...] = jnp.zeros_like(rise)
    rise[rise.shape[0] - ramp_rows :, :] = -ramp
    fetch.wait()
    heads[...] = lead[...].astype(BF16)
    total = None
    for q in range(GROUP - 1):
        found = matmul(heads[:, HOP * q : HOP * q + HOP], blocks[HOP * q : HOP * q + HOP, :])
        total = found if total is None else total + found
        sums[q] = total


def tables(taps, record):
    channels = record.shape[0]
    lead = L - HOP + JITTER
    vmem = pl.BlockSpec(memory_space=pltpu.VMEM)
    return pl.pallas_call(
        tables_kernel,
        out_shape=(
            jax.ShapeDtypeStruct((L, LANES), BF16),
            jax.ShapeDtypeStruct((EDGE, LANES), F32),
            jax.ShapeDtypeStruct((2 * JITTER, LANES), F32),
            jax.ShapeDtypeStruct((channels, lead), BF16),
            jax.ShapeDtypeStruct((GROUP - 1, channels, LANES), F32),
        ),
        in_specs=[vmem, pl.BlockSpec(memory_space=pl.ANY)],
        out_specs=(vmem,) * 5,
        scratch_shapes=[
            pltpu.VMEM((2 * TAPS + 6, LANES), F32),
            pltpu.VMEM((channels, lead), F32),
            pltpu.SemaphoreType.DMA,
        ],
        compiler_params=pltpu.CompilerParams(vmem_limit_bytes=50 * MIB),
        name="tables",
    )(taps, record)


def border_kernel(inbox, heads, sums, rise, fall, parts, done, collected):
    channels = heads.shape[0]
    done[...] = jnp.zeros_like(done)
    head = inbox[0:16, :].astype(F32)[:1]
    lane = lax.broadcasted_iota(jnp.int32, (1, LANES), 1)

    def told(at):
        return jnp.sum(jnp.where(lane == at, head, 0.0)).astype(jnp.int32)

    for q in range(GROUP):
        offset = told(q)
        edges = edge_table(rise, fall, offset)
        if q == 0:
            part = matmul(heads[:, 0:JITTER], edges[RIM:])
        else:
            part = matmul(heads[:, HOP * q - RIM : HOP * q + JITTER], edges)
            part = part + turn(sums[q - 1], HOP * q + offset - (TAPS - 1))
        upright = across(part * told(GROUP + q).astype(F32))
        for c in range(collected.shape[0]):
            piece = upright[:, 128 * c : 128 * c + 128]
            collected[c, pl.ds(q, BINS, stride=2 * GROUP), :] = piece[:BINS]
            collected[c, pl.ds(GROUP + q, BINS, stride=2 * GROUP), :] = piece[BINS:]
    width = min(128, channels)
    for c in range(collected.shape[0]):
        block = collected[c, : 2 * GROUP * BINS].reshape(BINS, 2 * GROUP, 128).astype(BF16)
        parts[:, :, width * c : width * c + width] = block[:, :, :width]


def border_parts(inbox, heads, sums, rise, fall):
    channels = heads.shape[0]
    vmem = pl.BlockSpec(memory_space=pltpu.VMEM)
    return pl.pallas_call(
        border_kernel,
        out_shape=(jax.ShapeDtypeStruct((BINS, 2 * GROUP, channels), BF16), jax.ShapeDtypeStruct((8, 128), F32)),
        in_specs=[vmem] * 5,
        out_specs=(vmem, vmem),
        scratch_shapes=[pltpu.VMEM((max(channels // 128, 1), 2 * GROUP * BINS + 2 * GROUP, 128), F32)],
        compiler_params=pltpu.CompilerParams(vmem_limit_bytes=50 * MIB),
        cost_estimate=pl.CostEstimate(
            flops=2 * channels * LANES * 1536, bytes_accessed=8 * channels * L, transcendentals=0
        ),
        name="border_parts",
    )(inbox, heads, sums, rise, fall)


def spectra_kernel(offsets, valid, record, rim, blocks, rise, fall, order, out, samples, later, collected, sems):
    channels, slab = record.shape
    steps = slab // L
    windows = GROUP * steps

    def fetch(s):
        return pltpu.make_async_copy(
            record.at[:, pl.ds(L * s, L)], samples.at[:, pl.ds(RIM + L * s, L)], sems.at[s]
        )

    for s in range(steps):
        fetch(s).start()
    samples[:, 0:RIM] = rim[...].astype(F32)
    samples[:, RIM + slab :] = jnp.zeros((channels, samples.shape[1] - RIM - slab), F32)

    def block_sums(s):
        found = []
        for i in range(GROUP):
            begin = pl.multiple_of(RIM + L * s + HOP * i, 128)
            found.append(
                matmul(samples[:, pl.ds(begin, HOP)].astype(BF16), blocks[HOP * i : HOP * i + HOP, :])
            )
        return found

    def keep(found):
        total = found[GROUP - 1]
        later[GROUP - 1] = total
        for q in range(GROUP - 2, -1, -1):
            total = total + found[q]
            later[q] = total

    def one_window(w, q, before):
        offset = offsets[w]
        begin = pl.multiple_of(HOP * w, 128)
        ends = samples[:, pl.ds(begin + L, EDGE)] - samples[:, pl.ds(begin, EDGE)]
        part = matmul(ends.astype(BF16), edge_table(rise, fall, offset))
        total = later[q] if before is None else later[q] + before
        part = (part + turn(total, HOP * q + offset - (TAPS - 1))) * valid[w].astype(F32)
        upright = across(part)
        for c in range(collected.shape[0]):
            collected[c, pl.ds(w, LANES, stride=windows), :] = upright[:, 128 * c : 128 * c + 128]

    fetch(0).wait()
    keep(block_sums(0))

    @pl.loop(0, steps - 1)
    def _(s):
        fetch(s + 1).wait()
        found = block_sums(s + 1)
        before = None
        for q in range(GROUP):
            one_window(GROUP * s + q, q, before)
            before = found[q] if before is None else before + found[q]
        keep(found)

    for q in range(GROUP):
        one_window(GROUP * (steps - 1) + q, q, None)

    width = min(128, channels)
    for c in range(collected.shape[0]):
        block = collected[c, : LANES * windows].reshape(LANES, windows, 128).astype(BF16)
        for ri in range(2):
            part = block[BINS * ri : BINS * ri + BINS, :, :width]
            out[:, windows * ri : windows * ri + windows, width * c : width * c + width] = part


def own_spectra(record, rim, offsets, valid, transform, rise, fall, order):
    channels, slab = record.shape
    windows = offsets.shape[0]
    smem = pl.BlockSpec(memory_space=pltpu.SMEM)
    vmem = pl.BlockSpec(memory_space=pltpu.VMEM)
    return pl.pallas_call(
        spectra_kernel,
        out_shape=jax.ShapeDtypeStruct((BINS, 2 * windows, channels), BF16),
        in_specs=[smem, smem, pl.BlockSpec(memory_space=pl.ANY), vmem, vmem, vmem, vmem, vmem],
        out_specs=vmem,
        scratch_shapes=[
            pltpu.VMEM((channels, RIM + slab + L - HOP + JITTER), F32),
            pltpu.VMEM((GROUP, channels, LANES), F32),
            pltpu.VMEM((max(channels // 128, 1), LANES * windows + windows, 128), F32),
            pltpu.SemaphoreType.DMA((slab // L,)),
        ],
        compiler_params=pltpu.CompilerParams(vmem_limit_bytes=50 * MIB),
        cost_estimate=pl.CostEstimate(
            flops=2 * channels * LANES * 896 * windows, bytes_accessed=4 * channels * slab, transcendentals=0
        ),
        name="own_spectra",
    )(offsets, valid, record, rim, transform, rise, fall, order)


def with_parts(block, part):
    windows = block.shape[1] // 2
    row = lax.broadcasted_iota(jnp.int32, part.shape, 1)
    moved = jnp.concatenate([part[:, GROUP:], part[:, :GROUP]], axis=1)
    pieces = []
    for ri, extra in enumerate((moved, part)):
        end = windows * ri + windows
        pieces.append(block[:, windows * ri : end - 2 * GROUP])
        pieces.append(block[:, end - 2 * GROUP : end] + jnp.where(row >= GROUP, extra, 0.0))
    return jnp.concatenate(pieces, axis=1)


def join_kernel(skip, own, parts, *chunks):
    *chunks, done = chunks
    done[...] = jnp.zeros_like(done)
    devices = chunks[0].shape[0]
    total = sum(chunk.shape[1] for chunk in chunks)
    for group in range(devices):
        begin = group * BINS // devices + skip
        end = begin + total
        joined = with_parts(own[begin:end].astype(F32), parts[begin:end].astype(F32)).astype(BF16)
        at = 0
        for chunk in chunks:
            chunk[group] = joined[at : at + chunk.shape[1]]
            at += chunk.shape[1]


def chunk_sizes(bins):
    count = min(3, bins)
    return [(bins + count - 1 - c) // count for c in range(count)]


def joined_chunks(own, parts, devices, skip, sizes):
    _, rows, channels = own.shape
    vmem = pl.BlockSpec(memory_space=pltpu.VMEM)
    *chunks, done = pl.pallas_call(
        functools.partial(join_kernel, skip),
        out_shape=tuple(jax.ShapeDtypeStruct((devices, count, rows, channels), BF16) for count in sizes)
        + (jax.ShapeDtypeStruct((8, 128), F32),),
        in_specs=[vmem, vmem],
        out_specs=(vmem,) * (len(sizes) + 1),
        compiler_params=pltpu.CompilerParams(vmem_limit_bytes=16 * MIB),
        name="joined_chunks",
    )(own, parts)
    return chunks, done


def left_kernel(own, out):
    sources, _, rows, channels = own.shape
    depth = sources * rows
    half = rows // 2
    straight = own[:, 0].astype(F32)
    turned = jnp.concatenate([straight[:, half:], -straight[:, :half]], axis=1)
    out[0, :channels] = straight.reshape(depth, channels).T.astype(BF16)
    out[0, channels:] = turned.reshape(depth, channels).T.astype(BF16)


def left_sides(own):
    sources, count, rows, channels = own.shape
    shape = (count, 2 * channels, sources * rows)
    return pl.pallas_call(
        left_kernel,
        grid=(count,),
        out_shape=jax.ShapeDtypeStruct(shape, BF16),
        in_specs=[pl.BlockSpec((sources, 1, rows, channels), lambda f: (0, f, 0, 0))],
        out_specs=pl.BlockSpec((1,) + shape[1:], lambda f: (f, 0, 0)),
        compiler_params=pltpu.CompilerParams(vmem_limit_bytes=16 * MIB),
        name="left_sides",
    )(own)


def cross_kernel(scale, stacked, me, left, *rest):
    out, done = rest[-2:]
    done[...] = jnp.zeros_like(done)
    sources, _, rows, channels = rest[0].shape[-4:]
    blocks = out.shape[3] // channels
    tile = min(256, channels)
    for n in range(blocks):
        if stacked:
            right, at = rest[0][n], channels * n
        else:
            right, at = rest[n][...], pl.multiple_of(channels * ((me[0] ^ n) & (blocks - 1)), 128)
        right = right[:, 0].reshape(sources * rows, channels)
        for j in range(0, channels, tile):
            for r in range(0, 2 * channels, tile):
                both = matmul(left[0, r : r + tile, :], right[:, j : j + tile]) * scale
                out[0, r // channels, r % channels : r % channels + tile, pl.ds(at + j, tile)] = both.astype(BF16)


def cross_products(left, right, result, begin, bins, blocks, first):
    sources, count, rows, channels = (right if first is None else right[0]).shape[-4:]
    columns = blocks if first is None else len(right)
    shape = (bins, 2, channels, blocks * channels)
    operands = [lax.axis_index("chan").astype(jnp.int32).reshape(1), left]
    in_specs = [pl.BlockSpec((1,) + left.shape[1:], lambda f, me: (f, 0, 0))]
    if first is None:
        operands.append(right)
        in_specs.append(pl.BlockSpec((blocks, sources, 1, rows, channels), lambda f, me: (0, 0, f, 0, 0)))
    else:
        operands += right
        in_specs += [pl.BlockSpec((sources, 1, rows, channels), lambda f, me: (0, f, 0, 0))] * columns
    if result is None:
        result, aliases = operands[1], {}
    else:
        aliases = {len(operands): 0}
    operands.append(result)
    in_specs.append(pl.BlockSpec(memory_space=pl.ANY))

    def place(f, me):
        return begin + f, 0, 0, 0 if first is None else (me[0] // columns) ^ (first // columns)

    return pl.pallas_call(
        functools.partial(cross_kernel, 2.0 / (sources * rows), first is None),
        grid_spec=pltpu.PrefetchScalarGridSpec(
            num_scalar_prefetch=1,
            grid=(count,),
            in_specs=in_specs,
            out_specs=(
                pl.BlockSpec((1, 2, channels, columns * channels), place),
                pl.BlockSpec((8, 128), lambda f, me: (0, 0)),
            ),
        ),
        out_shape=(jax.ShapeDtypeStruct(shape, BF16), jax.ShapeDtypeStruct((8, 128), F32)),
        input_output_aliases=aliases,
        compiler_params=pltpu.CompilerParams(vmem_limit_bytes=24 * MIB),
        cost_estimate=pl.CostEstimate(
            flops=4 * count * channels * columns * channels * sources * rows,
            bytes_accessed=4 * count * channels * columns * channels,
            transcendentals=0,
        ),
        name="cross_products",
    )(*operands)


def swapped(shard, axis, bit):
    devices = lax.axis_size(axis)
    return lax.ppermute(shard, axis, [(i, i ^ bit) for i in range(devices)])


def fan(shard, axis, bit):
    held = {0: shard}
    while bit:
        held.update({n | bit: swapped(block, axis, bit) for n, block in list(held.items())})
        bit //= 2
    return held


def after_kernel(shard, done, out):
    out[...] = shard[...]


def after(shard, done):
    if done is None:
        return shard
    vmem = pl.BlockSpec(memory_space=pltpu.VMEM)
    return pl.pallas_call(
        after_kernel,
        out_shape=jax.ShapeDtypeStruct(shard.shape, shard.dtype),
        in_specs=[vmem, vmem],
        out_specs=vmem,
        compiler_params=pltpu.CompilerParams(vmem_limit_bytes=8 * MIB),
        name="after",
    )(shard, done)


def per_device(record, whitening, offsets, window_valid):
    devices = lax.axis_size("tm")
    blocks = lax.axis_size("chan")
    stacked = blocks & (blocks - 1) != 0 or record.shape[0] % 128 != 0
    top = blocks // 2
    bins = BINS // devices

    def exchanged(chunk):
        return lax.all_to_all(chunk, "tm", split_axis=0, concat_axis=0, tiled=True)

    def fanned(shard):
        held = fan(shard, "chan", top // 2)
        return [held[n] for n in range(top)]

    inbox, taps = outbox(record, offsets, window_valid, whitening)
    inbox = from_behind(inbox, "tm", 1)
    transform, rise, fall, heads, sums = tables(taps, record)
    parts, done = border_parts(inbox, heads, sums, rise, fall)
    parts = from_behind(parts, "tm", -1)
    own = own_spectra(record, inbox, offsets, window_valid, transform, rise, fall, done)
    sizes = chunk_sizes(bins)
    begins = [sum(sizes[:p]) for p in range(len(sizes))]
    chunks, _ = joined_chunks(own, parts, devices, 0, sizes[:1])
    more, joined = joined_chunks(own, parts, devices, sizes[0], sizes[1:])
    chunks += more
    result, near, far, left, done = None, [], [], [], joined

    def cross(p, right, first):
        return cross_products(left[p], right, result, begins[p], bins, blocks, first)

    for p, chunk in enumerate(chunks):
        mine = exchanged(chunk)
        if stacked:
            right = lax.all_gather(mine, "chan", axis=0, tiled=False)
            result, _ = cross_products(left_sides(mine), right, result, begins[p], bins, blocks, None)
            continue
        mine = after(mine, done)
        far.append(swapped(mine, "chan", top))
        near.append(fanned(mine))
        left.append(left_sides(mine))
        ready = done
        result, done = cross(p, near[p], 0)
        if p:
            far[p - 1] = fanned(after(far[p - 1], ready) if p > 1 else far[p - 1])
            result, done = cross(p - 1, far[p - 1], top)
    if not stacked:
        for n, block in enumerate(fanned(after(far[-1], done))):
            result, _ = cross(len(chunks) - 1, [block], top + n)
    return result


def solution(mesh):
    in_specs = (P("chan", "tm"), P(), P("tm"), P("tm"))
    out_specs = P("tm", None, "chan", None)
    return jax.shard_map(
        per_device, mesh=mesh, in_specs=in_specs, out_specs=out_specs, check_vma=False
    )
```
